512 devices in a mesh: ctx: 16 (over y_lo, x, core), mp: 32 (over z, y_hi).
Axes of the slice: x: 4, y: 4 (y_hi: 2, y_lo: 2; y = y_hi * 2 + y_lo), z: 16, core: 2. Of those that a mesh axis runs over, the one named last changes fastest.
Arguments:
- queries: bfloat16 [16384, 4096], P('ctx', 'mp'), may hold values from -320 to 320
- keys_values: bfloat16 [16384, 2048], P('ctx', 'mp'), may hold values from -40 to 40
- query_taps: float32 [4, 4096], P(None, 'mp'), may hold values from -2.5 to 2.5
- pair_taps: float32 [4, 2048], P(None, 'mp'), may hold values from -2.5 to 2.5
- out_gain: float32 [4096], P('mp'), may hold values from 0.1 to 1.9
Outputs:
- head_outputs: bfloat16 [16384, 4096], P('ctx', 'mp')
The draws below stay inside these ranges and needn't reach their ends.
All inputs are finite; a program needn't handle non-finite values.
Results may differ from the reference program's by a relative error of at most 0.012.
The reference program's roundings to bfloat16 on the way count: a program that leaves them out, or rounds other values in their place, can miss the bound.
Values may be sent and summed in bfloat16 or wider, within the bound.
No kernel may reach another device: no remote copies, remote signals or barrier semaphores. Data moves between devices by JAX's collectives and lax.ppermute only.
A program may use at most 64 MiB of HBM per device.

```python
import math
import jax
import jax.numpy as jnp
import numpy as np
from jax import lax

HEADS = 32
KV_HEADS = 8
HEAD_CHANNELS = 128
TAPS = 4
TRANSFORM_BLOCK = 128
KEEP = 16
FOLDED_SPAN = 512
SEQ = 16384
N_CTX = 16


def draw_queries(key, part):
    base = jnp.clip(jax.random.normal(key, (SEQ, HEADS * HEAD_CHANNELS), jnp.float32), -4.0, 4.0)
    return base.astype(jnp.bfloat16)


def draw_keys_values(key, part):
    columns = 2 * KV_HEADS * HEAD_CHANNELS
    is_value = jnp.arange(columns) // HEAD_CHANNELS % 2 == 1
    channel_draw = jax.random.uniform(jax.random.fold_in(key, 21), (columns,), jnp.float32)
    lower = math.log(0.5)
    upper = jnp.where(is_value, math.log(5.0), math.log(1.5))
    channel_scale = jnp.exp(lower + (upper - lower) * channel_draw)
    row_scale = jnp.exp(jax.random.uniform(jax.random.fold_in(key, 22), (SEQ, 1), jnp.float32, math.log(0.7), math.log(2.0)))
    base = jnp.clip(jax.random.normal(jax.random.fold_in(key, 25), (SEQ, columns), jnp.float32), -4.0, 4.0)
    return (base * channel_scale * row_scale).astype(jnp.bfloat16)


def steps_of(own_key, shape, split, smallest, largest):
    gain = 1.0
    for position, shards_of in split:
        draws = jax.random.uniform(jax.random.fold_in(jax.random.fold_in(own_key, 6), position), (shards_of,), jnp.float32, smallest / len(split), largest / len(split))
        gain = gain * jnp.repeat(jnp.exp(draws), shape[position] // shards_of).reshape((-1,) + (1,) * (len(shape) - 1 - position))
    return gain


def scatter_about(stream_key, shape, spread, most, shards=(), kind=jnp.bfloat16):
    loudness = steps_of(stream_key, shape, shards, -0.22, 0.18) if shards else 1.0
    values = jax.random.normal(stream_key, shape, jnp.float32) * spread * loudness
    return jnp.minimum(jnp.maximum(values, -most), most).astype(kind)


def setup_inputs(seed: int = 0) -> dict:
    key_list = jax.random.split(jax.random.key(seed), 6)
    return {
        "queries": draw_queries(jax.random.fold_in(key_list[5], 71), 0),
        "keys_values": draw_keys_values(jax.random.fold_in(key_list[5], 71), 0),
        "query_taps": scatter_about(key_list[2], (TAPS, HEADS * HEAD_CHANNELS), 0.5, 2.5, ((1, 32),), jnp.float32),
        "pair_taps": scatter_about(key_list[3], (TAPS, 2 * KV_HEADS * HEAD_CHANNELS), 0.5, 2.5, ((1, 32),), jnp.float32),
        "out_gain": jnp.clip(1.0 + 0.18 * jax.random.normal(key_list[4], (HEADS * HEAD_CHANNELS,), jnp.float32), 0.1, 1.9),
    }


def span_sources():
    sources = []
    for stored in range(2 * N_CTX):
        holder = stored // 2
        sources.append(holder if stored % 2 == 0 else 2 * N_CTX - 1 - holder)
    return np.array(sources)

def to_sequence(array):
    spans = array.reshape((2 * N_CTX, FOLDED_SPAN) + array.shape[1:])
    return spans[np.argsort(span_sources())].reshape(array.shape)

def to_storage(array):
    spans = array.reshape((2 * N_CTX, FOLDED_SPAN) + array.shape[1:])
    return spans[span_sources()].reshape(array.shape)

def rounded_values(values):
    return lax.optimization_barrier(values.astype(jnp.bfloat16)).astype(jnp.float32)

def dct_table():
    frequency = jnp.arange(KEEP, dtype=jnp.float32)[:, None]
    offset = jnp.arange(TRANSFORM_BLOCK, dtype=jnp.float32)[None, :]
    table = jnp.cos(math.pi * (offset + 0.5) * frequency / TRANSFORM_BLOCK) * math.sqrt(2.0 / TRANSFORM_BLOCK)
    table = jnp.where(frequency == 0.0, table * math.sqrt(0.5), table)
    return table.astype(jnp.bfloat16)

def causal_conv(values, weights):
    length = values.shape[0]
    lead = TAPS - 1
    padded = jnp.pad(values.astype(jnp.float32), ((lead, 0), (0, 0)))
    total = weights[0] * padded[lead:lead + length]
    for shift in range(1, TAPS):
        total = total + weights[shift] * padded[lead - shift:lead - shift + length]
    return total.astype(jnp.bfloat16)

def compress(values):
    blocks = values.reshape(values.shape[0] // TRANSFORM_BLOCK, TRANSFORM_BLOCK, values.shape[1]).astype(jnp.float32)
    packed = jnp.einsum('jt,btc->bjc', dct_table().astype(jnp.float32), blocks, precision=lax.Precision.HIGHEST)
    return packed.astype(jnp.bfloat16).reshape(-1, values.shape[1])

def reference(queries, keys_values, query_taps, pair_taps, out_gain):
    query_group = HEADS // KV_HEADS
    score_scale = 1.0 / math.sqrt(HEAD_CHANNELS)
    seq_queries = causal_conv(to_sequence(queries), query_taps)
    seq_pairs = causal_conv(to_sequence(keys_values), pair_taps)
    packed = compress(seq_pairs)
    query_heads = seq_queries.reshape(SEQ, KV_HEADS, query_group, HEAD_CHANNELS).transpose(1, 0, 2, 3)
    pair_heads = seq_pairs.reshape(SEQ, KV_HEADS, 2 * HEAD_CHANNELS).transpose(1, 0, 2)
    packed_heads = packed.reshape(-1, KV_HEADS, 2 * HEAD_CHANNELS).transpose(1, 0, 2)

    def head_group(operands):
        query_all, pair_all, packed_all = operands
        outputs = []
        quarter = SEQ // 4
        for portion in range(4):
            limit = (portion + 1) * quarter * KEEP // TRANSFORM_BLOCK
            seen_keys = packed_all[:limit].astype(jnp.float32)
            key_blocks = (jnp.arange(limit) // KEEP).astype(jnp.int32)

            def span_fn(pieces):
                query_span, pair_span, start = pieces
                positions = start + jnp.arange(FOLDED_SPAN).astype(jnp.int32)
                query_blocks = positions // TRANSFORM_BLOCK
                query_single_float = query_span.astype(jnp.float32)
                far = jnp.einsum('qgd,kd->qgk', query_single_float, seen_keys[:, :HEAD_CHANNELS]) * score_scale
                far = jnp.where(key_blocks[None, None, :] < query_blocks[:, None, None], far, -jnp.inf)
                entry_count = FOLDED_SPAN // TRANSFORM_BLOCK
                pair_single_float = pair_span.astype(jnp.float32)
                nearby_scores = jnp.einsum('cehp,cyp->cehy', query_single_float.reshape(entry_count, TRANSFORM_BLOCK, query_group, HEAD_CHANNELS), pair_single_float[:, :HEAD_CHANNELS].reshape(entry_count, TRANSFORM_BLOCK, HEAD_CHANNELS)) * score_scale
                causal = jnp.arange(TRANSFORM_BLOCK)[:, None, None] >= jnp.arange(TRANSFORM_BLOCK)[None, None, :]
                nearby_scores = jnp.where(causal, nearby_scores, -jnp.inf).reshape(FOLDED_SPAN, query_group, TRANSFORM_BLOCK)
                top = jnp.maximum(lax.optimization_barrier(jnp.max(far, -1)), lax.optimization_barrier(jnp.max(nearby_scores, -1)))
                far_weights = jnp.exp(far - top[..., None])
                nearby_weights = jnp.exp(nearby_scores - top[..., None])
                total = lax.optimization_barrier(jnp.sum(far_weights, -1)) + lax.optimization_barrier(jnp.sum(nearby_weights, -1))
                far_out = jnp.einsum('qgk,kd->qgd', rounded_values(far_weights), seen_keys[:, HEAD_CHANNELS:])
                nearby_output = jnp.einsum('oris,osz->oriz', rounded_values(nearby_weights).reshape(entry_count, TRANSFORM_BLOCK, query_group, TRANSFORM_BLOCK), pair_single_float[:, HEAD_CHANNELS:].reshape(entry_count, TRANSFORM_BLOCK, HEAD_CHANNELS)).reshape(FOLDED_SPAN, query_group, HEAD_CHANNELS)
                attended = (far_out + nearby_output) / total[..., None]
                return attended * lax.rsqrt(lax.optimization_barrier(jnp.mean(attended * attended, -1, keepdims=True)) + 1e-06)
            query_part = query_all[portion * quarter:(portion + 1) * quarter].reshape(quarter // FOLDED_SPAN, FOLDED_SPAN, query_group, HEAD_CHANNELS)
            pair_part = pair_all[portion * quarter:(portion + 1) * quarter].reshape(quarter // FOLDED_SPAN, FOLDED_SPAN, 2 * HEAD_CHANNELS)
            starts = (portion * quarter + FOLDED_SPAN * jnp.arange(quarter // FOLDED_SPAN)).astype(jnp.int32)
            outputs.append(lax.map(span_fn, (query_part, pair_part, starts)).reshape(quarter, query_group, HEAD_CHANNELS))
        return jnp.concatenate(outputs, 0)
    attended = lax.map(head_group, (query_heads, pair_heads, packed_heads))
    normed = attended.transpose(1, 0, 2, 3).reshape(SEQ, HEADS * HEAD_CHANNELS)
    return to_storage((normed * out_gain).astype(jnp.bfloat16))
```

```python
import functools
import math

import jax
import jax.numpy as jnp
import numpy as np
from jax import lax
from jax.experimental import pallas as pl
from jax.experimental.pallas import tpu as pltpu
from jax.sharding import Mesh, PartitionSpec as P

HEAD_CHANNELS = 128
TAPS = 4
BLOCK = 128
KEEP = 16
SPAN = 512
ROWS = 2 * SPAN
NEGATIVE = -1e30
EPSILON = 1e-06
EDGE = 16

CTX = ("y_lo", "x", "core")
MP = ("z_hi", "z_lo", "y_hi")
GROUP = ("z_lo", "y_hi")
CHIPS = ("y_lo", "x")

VMEM = pltpu.VMEM
SMEM = pltpu.SMEM
F32 = jnp.float32
BF16 = jnp.bfloat16


def spec(space=VMEM):
    return pl.BlockSpec(memory_space=space)


def dct_tile():
    j = np.arange(KEEP, dtype=np.float32)[:, None]
    u = np.arange(BLOCK, dtype=np.float32)[None, :]
    table = np.cos(np.float32(math.pi) * (u + np.float32(0.5)) * j / np.float32(BLOCK))
    table = table * np.float32(math.sqrt(2.0 / BLOCK))
    table = np.where(j == 0, table * np.float32(math.sqrt(0.5)), table)
    return np.tile(table.T, (1, BLOCK // KEEP)).astype(jnp.bfloat16)


def choose_halos(scalars, own, swap, hop):
    place = scalars[0]
    odd = place % 2 == 1
    lower = jnp.where(odd, swap[0], hop[0])
    lower = jnp.where(place == 0, jnp.zeros_like(lower), lower)
    upper = jnp.where(odd, hop[1], swap[1])
    upper = jnp.where(place == 15, own[0], upper)
    return lower, upper


def pack_kernel(scalars, kv, own, swap, hop, taps, table, conv_out, block_out):
    lower, upper = choose_halos(
        scalars, own[:, EDGE:].astype(F32), swap[:, EDGE:].astype(F32), hop[:, EDGE:].astype(F32)
    )
    lanes = lax.broadcasted_iota(jnp.int32, (64, BLOCK), 1)
    packed = jnp.zeros((64, BLOCK), F32)
    for half, halo in enumerate((lower, upper)):
        values = kv[:, half * SPAN : (half + 1) * SPAN].astype(F32)
        padded = jnp.concatenate([halo, values], 1)
        total = taps[:, 0:1] * values
        for w in range(1, TAPS):
            total = total + taps[:, w : w + 1] * pltpu.roll(padded, w, 1)[:, BLOCK:]
        conv = total.astype(BF16)
        conv_out[:, half * SPAN : (half + 1) * SPAN] = conv
        for b in range(SPAN // BLOCK):
            part = jnp.dot(
                conv[:, b * BLOCK : (b + 1) * BLOCK], table[...], preferred_element_type=F32
            )
            packed = jnp.where(lanes // KEEP == half * 4 + b, part, packed)
    packed = packed.astype(BF16)
    for k in range(block_out.shape[0]):
        block_out[k] = packed


def query_kernel(scalars, q, own, swap, hop, taps, out):
    lower, upper = choose_halos(
        scalars, own[:, :EDGE].astype(F32), swap[:, :EDGE].astype(F32), hop[:, :EDGE].astype(F32)
    )
    for half, halo in enumerate((lower, upper)):
        for b in range(SPAN // BLOCK):
            start = half * SPAN + b * BLOCK
            values = q[start : start + BLOCK].astype(F32)
            if b:
                halo = q[start - EDGE : start].astype(F32)
            padded = jnp.concatenate([halo, values], 0)
            total = taps[0:1] * values
            for w in range(1, TAPS):
                total = total + taps[w : w + 1] * pltpu.roll(padded, w, 0)[EDGE:]
            out[start : start + BLOCK] = total.astype(BF16)


def attend_kernel(
    scalars, q, far_own, far_other, mine, from1, from2, from3, gain, out, pairs, keys, values, scores
):
    place, member = scalars[0], scalars[1]
    core = place % 2
    factor = math.log2(math.e) / math.sqrt(HEAD_CHANNELS)
    for k, ref in enumerate((mine, from1, from2, from3)):
        pairs[member ^ k] = ref[...]
    for i in range(8):
        keys[i, core] = far_own[i, :HEAD_CHANNELS]
        keys[i, 1 - core] = far_other[i, :HEAD_CHANNELS]
        values[i, core] = far_own[i, HEAD_CHANNELS:]
        values[i, 1 - core] = far_other[i, HEAD_CHANNELS:]
    R = 256
    lane = lax.broadcasted_iota(jnp.int32, (BLOCK, BLOCK), 1)
    row = lax.broadcasted_iota(jnp.int32, (BLOCK, BLOCK), 0)
    causal = row >= lane
    lower_half = lane < BLOCK // 2
    key_block = (lane % (BLOCK // 2)) // KEEP
    nt = (((1,), (1,)), ((), ()))
    for half in range(2):
        for r in range(SPAN // R):
            start = half * SPAN + r * R
            query = q[start : start + R]
            tops = []
            for c in range(R // BLOCK):
                s = start + c * BLOCK
                near = jnp.dot(
                    query[c * BLOCK : (c + 1) * BLOCK],
                    jnp.concatenate([pairs[0, :, s : s + BLOCK], pairs[1, :, s : s + BLOCK]], 0),
                    preferred_element_type=F32,
                )
                near = jnp.where(causal, near, NEGATIVE)
                scores[c * BLOCK : (c + 1) * BLOCK, 2048:] = near
                tops.append(near)
            for i in range(8):
                far = jnp.dot(
                    query,
                    jnp.concatenate([keys[i, 0], keys[i, 1]], 1),
                    preferred_element_type=F32,
                )
                for e in range(2):
                    owner = 2 * i + e
                    for c in range(R // BLOCK):
                        block = r * (R // BLOCK) + c
                        if half == 0:
                            limit = jnp.where(owner < place, 4, jnp.where(owner == place, block, 0))
                            seen = lower_half & (key_block < limit)
                        else:
                            limit = jnp.where(owner > place, 4, jnp.where(owner == place, block, 0))
                            seen = lower_half | (key_block < limit)
                        tile = jnp.where(
                            seen,
                            far[c * BLOCK : (c + 1) * BLOCK, e * BLOCK : (e + 1) * BLOCK],
                            NEGATIVE,
                        )
                        scores[c * BLOCK : (c + 1) * BLOCK, owner * BLOCK : (owner + 1) * BLOCK] = tile
                        tops[c] = jnp.maximum(tops[c], tile)
            top = jnp.concatenate([jnp.max(t, 1, keepdims=True) for t in tops], 0) * factor
            total = jnp.zeros((R, BLOCK), F32)
            summed = jnp.zeros((R, HEAD_CHANNELS), F32)
            weights = jnp.exp2(scores[:, 2048:] * factor - top)
            total = total + weights
            weights = weights.astype(BF16)
            nears = []
            for c in range(R // BLOCK):
                s = start + c * BLOCK
                nears.append(
                    lax.dot_general(
                        weights[c * BLOCK : (c + 1) * BLOCK],
                        jnp.concatenate([pairs[2, :, s : s + BLOCK], pairs[3, :, s : s + BLOCK]], 0),
                        nt,
                        preferred_element_type=F32,
                    )
                )
            summed = summed + jnp.concatenate(nears, 0)
            for i in range(8):
                weights = jnp.exp2(scores[:, i * 256 : (i + 1) * 256] * factor - top)
                total = total + weights[:, :BLOCK] + weights[:, BLOCK:]
                summed = summed + lax.dot_general(
                    weights.astype(BF16),
                    jnp.concatenate([values[i, 0], values[i, 1]], 1),
                    nt,
                    preferred_element_type=F32,
                )
            attended = summed / jnp.sum(total, 1, keepdims=True)
            mean = jnp.mean(attended * attended, 1, keepdims=True)
            normed = attended * lax.rsqrt(mean + EPSILON)
            out[start : start + R] = (normed * gain[...]).astype(BF16)


def cost(flops, moved):
    return pl.CostEstimate(flops=flops, bytes_accessed=moved, transcendentals=0)


def per_device(queries, keys_values, query_taps, pair_taps, out_gain):
    place = lax.axis_index(CTX)
    member = lax.axis_index(GROUP)
    scalars = jnp.stack([place, member]).astype(jnp.int32)
    kv = keys_values.T
    tails = jnp.stack(
        [
            jnp.concatenate([queries[e - EDGE : e], kv[:, e - BLOCK : e]], 0)
            for e in (SPAN, ROWS)
        ]
    )
    swap = lax.ppermute(tails, "core", [(0, 1), (1, 0)])
    hop = lax.ppermute(
        tails, CTX, [(i, i + 1) for i in range(1, 15, 2)] + [(i + 1, i) for i in range(1, 15, 2)]
    )
    params = functools.partial(pltpu.CompilerParams, vmem_limit_bytes=24 << 20)
    conv, blocks = pl.pallas_call(
        pack_kernel,
        out_shape=(
            jax.ShapeDtypeStruct((64, ROWS), BF16),
            jax.ShapeDtypeStruct((32, 64, BLOCK), BF16),
        ),
        in_specs=[spec(SMEM)] + [spec()] * 6,
        out_specs=(spec(), spec()),
        compiler_params=params(),
        cost_estimate=cost(1 << 24, 1 << 20),
        name="pack",
    )(scalars, kv, tails, swap, hop, pair_taps.T, jnp.asarray(dct_tile()))
    gathered = lax.all_to_all(blocks, CHIPS + GROUP, 0, 0, tiled=True)
    others = [
        lax.ppermute(conv, GROUP, [(i, i ^ k) for i in range(4)]) for k in (1, 2, 3)
    ]
    query_conv = pl.pallas_call(
        query_kernel,
        out_shape=jax.ShapeDtypeStruct((ROWS, HEAD_CHANNELS), BF16),
        in_specs=[spec(SMEM)] + [spec()] * 5,
        out_specs=spec(),
        compiler_params=params(),
        cost_estimate=cost(1 << 24, 1 << 20),
        name="conv",
    )(scalars, queries, tails, swap, hop, query_taps)
    far_own = gathered.reshape(8, 2 * HEAD_CHANNELS, BLOCK)
    far_other = lax.ppermute(far_own, "core", [(0, 1), (1, 0)])
    return pl.pallas_call(
        attend_kernel,
        out_shape=jax.ShapeDtypeStruct((ROWS, HEAD_CHANNELS), BF16),
        in_specs=[spec(SMEM)] + [spec()] * 8,
        out_specs=spec(),
        scratch_shapes=[
            VMEM((4, 64, ROWS), BF16),
            VMEM((8, 2, HEAD_CHANNELS, BLOCK), BF16),
            VMEM((8, 2, HEAD_CHANNELS, BLOCK), BF16),
            VMEM((256, 2048 + BLOCK), F32),
        ],
        compiler_params=params(),
        cost_estimate=cost(1 << 30, 1 << 21),
        name="attend",
    )(scalars, query_conv, far_own, far_other, conv, *others, out_gain.reshape(1, -1))


def solution(mesh):
    fine = Mesh(mesh.devices.reshape(2, 4, 2, 8, 2, 2), CTX + MP)
    in_specs = (P(CTX, MP), P(CTX, MP), P(None, MP), P(None, MP), P(MP))
    return jax.shard_map(
        per_device, mesh=fine, in_specs=in_specs, out_specs=P(CTX, MP), check_vma=False
    )
```

```python
import functools
import math

import jax
import jax.numpy as jnp
import numpy as np
from jax import lax
from jax.experimental import pallas as pl
from jax.experimental.pallas import tpu as pltpu
from jax.sharding import Mesh, PartitionSpec as P

HEAD_CHANNELS = 128
TAPS = 4
BLOCK = 128
KEEP = 16
SPAN = 512
ROWS = 2 * SPAN
NEGATIVE = -1e30
EPSILON = 1e-06
EDGE = 16
CHUNK = 256
FACTOR = math.log2(math.e) / math.sqrt(HEAD_CHANNELS)

CTX = ("y_lo", "x", "core")
MP = ("z_hi", "z_lo", "y_hi")
GROUP = ("z_lo", "y_hi")
CHIPS = ("y_lo", "x")

VMEM = pltpu.VMEM
SMEM = pltpu.SMEM
F32 = jnp.float32
BF16 = jnp.bfloat16
NT = (((1,), (1,)), ((), ()))


def spec(space=VMEM):
    return pl.BlockSpec(memory_space=space)


def dct_table():
    j = np.arange(KEEP, dtype=np.float32)[:, None]
    u = np.arange(BLOCK, dtype=np.float32)[None, :]
    table = np.cos(np.float32(math.pi) * (u + np.float32(0.5)) * j / np.float32(BLOCK))
    table = table * np.float32(math.sqrt(2.0 / BLOCK))
    table = np.where(j == 0, table * np.float32(math.sqrt(0.5)), table)
    return table.astype(jnp.bfloat16)


def dct_tile():
    return np.tile(dct_table().T, (1, BLOCK // KEEP))


def tails_kernel(q, kv, out, sems):
    copies = []
    for half in range(2):
        end = (half + 1) * SPAN
        copies.append((q.at[end - EDGE : end], out.at[half, :EDGE]))
        copies.append((kv.at[:, end - BLOCK : end], out.at[half, EDGE:]))
    copies = [pltpu.make_async_copy(*c, sems.at[k]) for k, c in enumerate(copies)]
    for copy in copies:
        copy.start()
    for copy in copies:
        copy.wait()


def choose_halos(own, swap, hop):
    place = lax.axis_index(CTX)
    odd = place % 2 == 1
    lower = jnp.where(odd, swap[0], hop[0])
    lower = jnp.where(place == 0, jnp.zeros_like(lower), lower)
    upper = jnp.where(odd, hop[1], swap[1])
    upper = jnp.where(place == 15, own[0], upper)
    return lower, upper


def conv_kernel(kv, own, swap, hop, taps, conv_out):
    turned = jnp.transpose(
        jnp.concatenate(
            [
                jnp.concatenate([taps[...], jnp.zeros((4, 64), F32)], 0),
                jnp.zeros((8, 64), F32),
            ],
            1,
        )
    )[:64]
    halos = choose_halos(*(ref[:, EDGE:].astype(F32) for ref in (own, swap, hop)))
    for half, halo in enumerate(halos):
        values = kv[:, half * SPAN : (half + 1) * SPAN].astype(F32)
        padded = jnp.concatenate([halo, values], 1)
        total = turned[:, 0:1] * values
        for w in range(1, TAPS):
            total = total + turned[:, w : w + 1] * pltpu.roll(padded, w, 1)[:, BLOCK:]
        conv_out[:, half * SPAN : (half + 1) * SPAN] = total.astype(BF16)


def pack_kernel(conv, table, block_out):
    lanes = lax.broadcasted_iota(jnp.int32, (64, BLOCK), 1)
    packed = jnp.zeros((64, BLOCK), F32)
    for b in range(ROWS // BLOCK):
        part = jnp.dot(
            conv[:, b * BLOCK : (b + 1) * BLOCK], table[...], preferred_element_type=F32
        )
        packed = jnp.where(lanes // KEEP == b, part, packed)
    uneven = lax.axis_index(CHIPS) % 2 == 1
    packed = jnp.where(uneven, pltpu.roll(packed, BLOCK // 2, 1), packed).astype(BF16)
    for k in range(block_out.shape[0]):
        block_out[k] = packed


def join_kernel(mine, near, out):
    out[:64] = mine[...]
    out[64:] = near[...]


def query_kernel(q, own, swap, hop, taps, out):
    halos = choose_halos(*(ref[:, :EDGE].astype(F32) for ref in (own, swap, hop)))
    for half, halo in enumerate(halos):
        for b in range(SPAN // BLOCK):
            start = half * SPAN + b * BLOCK
            values = q[start : start + BLOCK].astype(F32)
            if b:
                halo = q[start - EDGE : start].astype(F32)
            padded = jnp.concatenate([halo, values], 0)
            total = taps[0:1] * values
            for w in range(1, TAPS):
                total = total + taps[w : w + 1] * pltpu.roll(padded, w, 0)[EDGE:]
            out[start : start + BLOCK] = total.astype(BF16)


def arrange(far, tiles):
    left = lax.broadcasted_iota(jnp.int32, (64, BLOCK), 1) < BLOCK // 2
    for kind in range(2):
        for j in range(4):
            for m in range(2):
                even, uneven = far[2 * j, 2 * kind + m], far[2 * j + 1, 2 * kind + m]
                rows = slice(64 * m, 64 * (m + 1))
                tiles[kind, 0, j, rows] = jnp.where(left, even, uneven)
                tiles[kind, 1, j, rows] = jnp.where(left, uneven, even)


class FarPass:
    def __init__(self, own, q, tiles, scores, tops, totals, sums):
        place = lax.axis_index(CTX)
        self.own, self.q, self.tiles, self.scores = own, q, tiles, scores
        self.tops, self.totals, self.sums = tops, totals, sums
        self.middle = place // 2
        self.before = self.middle if own else self.middle + place % 2
        self.turn = jnp.minimum(self.before // 2, 3)
        lane = lax.broadcasted_iota(jnp.int32, (1, BLOCK), 1)
        self.key_block = (lane % (BLOCK // 2)) // KEEP
        self.left = lane < BLOCK // 2

    def bias(self, high, j, block):
        def limit(i):
            low = jnp.where(i < self.before, 4, 0)
            top = jnp.where(i >= self.before + (1 if self.own else 0), 4, 0)
            value = jnp.where(high, top, low)
            return jnp.where(i == self.middle, block, value) if self.own else value

        first, second = limit(2 * j), limit(2 * j + 1)
        left, right = jnp.where(high, second, first), jnp.where(high, first, second)
        seen = self.key_block < jnp.where(self.left, left, right)
        return jnp.where(seen, 0.0, NEGATIVE)

    def variable(self):
        for v in range(5):
            high = v > self.turn
            side = high.astype(jnp.int32)
            yield v, high, side, v - side

    def score(self, r):
        rows = slice(r * CHUNK, (r + 1) * CHUNK)
        upper = self.q[SPAN + r * CHUNK : SPAN + (r + 1) * CHUNK]
        for j in range(2):
            far = jnp.dot(
                upper,
                jnp.concatenate([self.tiles[0, 0, 2 * j], self.tiles[0, 0, 2 * j + 1]], 1),
                preferred_element_type=F32,
            )
            one, two = far[:, :BLOCK], far[:, BLOCK:]
            self.scores[r, 5 + 2 * j] = one
            self.scores[r, 6 + 2 * j] = two
            self.tops[1, rows] = jnp.maximum(self.tops[1, rows], jnp.maximum(one, two))
        for v, high, side, j in self.variable():
            start = pl.multiple_of(side * SPAN + r * CHUNK, CHUNK)
            far = jnp.dot(
                self.q[pl.ds(start, CHUNK)], self.tiles[0, side, j], preferred_element_type=F32
            )
            biases = [
                jnp.broadcast_to(self.bias(high, j, r * (CHUNK // BLOCK) + c), (BLOCK, BLOCK))
                for c in range(CHUNK // BLOCK)
            ]
            far = far + jnp.concatenate(biases, 0)
            self.scores[r, v] = far
            self.tops[side, rows] = jnp.maximum(self.tops[side, rows], far)

    def add(self, r):
        rows = slice(r * CHUNK, (r + 1) * CHUNK)
        top = self.tops[1, rows] * FACTOR
        for j in range(2):
            one = jnp.exp2(self.scores[r, 5 + 2 * j] * FACTOR - top)
            two = jnp.exp2(self.scores[r, 6 + 2 * j] * FACTOR - top)
            self.totals[1, rows] = self.totals[1, rows] + one + two
            self.sums[1, rows] = self.sums[1, rows] + lax.dot_general(
                jnp.concatenate([one, two], 1).astype(BF16),
                jnp.concatenate([self.tiles[1, 0, 2 * j], self.tiles[1, 0, 2 * j + 1]], 1),
                NT,
                preferred_element_type=F32,
            )
        for v, high, side, j in self.variable():
            weights = jnp.exp2(self.scores[r, v] * FACTOR - self.tops[side, rows] * FACTOR)
            self.totals[side, rows] = self.totals[side, rows] + weights
            self.sums[side, rows] = self.sums[side, rows] + lax.dot_general(
                weights.astype(BF16), self.tiles[1, side, j], NT, preferred_element_type=F32
            )


def near_kernel(q, far, mine, near, both, tops, totals, sums, pairs, tiles, scores):
    member = lax.axis_index(GROUP)
    pairs[member] = mine[...]
    pairs[member ^ 1] = near[...]
    pairs[member ^ 2] = both[:64]
    pairs[member ^ 3] = both[64:]
    arrange(far, tiles)
    lane = lax.broadcasted_iota(jnp.int32, (BLOCK, BLOCK), 1)
    row = lax.broadcasted_iota(jnp.int32, (BLOCK, BLOCK), 0)

    def near_tile(kind, start):
        return jnp.concatenate(
            [pairs[2 * kind, :, start : start + BLOCK], pairs[2 * kind + 1, :, start : start + BLOCK]], 0
        )

    work = FarPass(True, q, tiles, scores, tops, totals, sums)
    for r in range(SPAN // CHUNK):
        blocks = [
            (half, r * CHUNK + c * BLOCK) for half in range(2) for c in range(CHUNK // BLOCK)
        ]
        for k, (half, start) in enumerate(blocks):
            place = half * SPAN + start
            score = jnp.dot(
                q[place : place + BLOCK], near_tile(0, place), preferred_element_type=F32
            )
            score = jnp.where(row >= lane, score, NEGATIVE)
            scores[r, 9 + half, start % CHUNK : start % CHUNK + BLOCK] = score
            tops[half, start : start + BLOCK] = score
        work.score(r)
        rows = slice(r * CHUNK, (r + 1) * CHUNK)
        for half in range(2):
            tops[half, rows] = jnp.broadcast_to(
                jnp.max(tops[half, rows], 1, keepdims=True), (CHUNK, BLOCK)
            )
        for k, (half, start) in enumerate(blocks):
            place = half * SPAN + start
            weights = jnp.exp2(
                scores[r, 9 + half, start % CHUNK : start % CHUNK + BLOCK] * FACTOR
                - tops[half, start : start + BLOCK] * FACTOR
            )
            totals[half, start : start + BLOCK] = weights
            sums[half, start : start + BLOCK] = lax.dot_general(
                weights.astype(BF16), near_tile(1, place), NT, preferred_element_type=F32
            )
        work.add(r)


def far_kernel(q, far, old_tops, old_totals, old_sums, gain, out, tiles, scores, tops, totals, sums):
    arrange(far, tiles)
    work = FarPass(False, q, tiles, scores, tops, totals, sums)
    for r in range(SPAN // CHUNK):
        rows = slice(r * CHUNK, (r + 1) * CHUNK)
        tops[:, rows] = old_tops[:, rows]
        work.score(r)
        for half in range(2):
            top = jnp.broadcast_to(jnp.max(tops[half, rows], 1, keepdims=True), (CHUNK, BLOCK))
            tops[half, rows] = top
            scale = jnp.exp2((old_tops[half, rows] - top) * FACTOR)
            totals[half, rows] = old_totals[half, rows] * scale
            sums[half, rows] = old_sums[half, rows] * scale
        work.add(r)
        for half in range(2):
            attended = sums[half, rows] / jnp.sum(totals[half, rows], 1, keepdims=True)
            mean = jnp.mean(attended * attended, 1, keepdims=True)
            normed = attended * lax.rsqrt(mean + EPSILON)
            start = half * SPAN + r * CHUNK
            out[start : start + CHUNK] = (normed * gain[...]).astype(BF16)


def cost(flops, moved):
    return pl.CostEstimate(flops=flops, bytes_accessed=moved, transcendentals=0)


def swapped(value, axis):
    return lax.ppermute(value, axis, [(0, 1), (1, 0)])


def per_device(queries, keys_values, query_taps, pair_taps, out_gain):
    def call(kernel, name, out_shape, operands, spaces=None, scratch=(), flops=1 << 24):
        many = isinstance(out_shape, tuple)
        return pl.pallas_call(
            kernel,
            out_shape=out_shape,
            in_specs=[spec(s) for s in spaces] if spaces else [spec()] * len(operands),
            out_specs=(spec(),) * len(out_shape) if many else spec(),
            scratch_shapes=scratch,
            compiler_params=pltpu.CompilerParams(vmem_limit_bytes=24 << 20),
            cost_estimate=cost(flops, 1 << 20),
            name=name,
        )(*operands)

    def shape(*dims, kind=BF16):
        return jax.ShapeDtypeStruct(dims, kind)

    kv = keys_values.T
    tails = call(
        tails_kernel,
        "tails",
        shape(2, EDGE + 64, BLOCK),
        (queries, kv),
        (pltpu.HBM, pltpu.HBM),
        [pltpu.SemaphoreType.DMA((4,))],
    )
    swap = swapped(tails, "core")
    hop = lax.ppermute(
        tails, CTX, [(i, i + 1) for i in range(1, 15, 2)] + [(i + 1, i) for i in range(1, 15, 2)]
    )
    conv = call(conv_kernel, "conv", shape(64, ROWS), (kv, tails, swap, hop, pair_taps))
    blocks = call(
        pack_kernel, "pack", shape(32, 64, BLOCK), (conv, jnp.asarray(dct_tile()))
    )
    gathered = lax.all_to_all(blocks, CHIPS + GROUP, 0, 0, tiled=True)
    near = swapped(conv, "y_hi")
    both = call(join_kernel, "join", shape(128, ROWS), (conv, near), flops=1 << 37)
    both = swapped(both, "z_lo")
    query_conv = call(
        query_kernel,
        "queries",
        shape(ROWS, HEAD_CHANNELS),
        (queries, tails, swap, hop, query_taps),
    )
    gathered, query_conv, both = lax.optimization_barrier((gathered, query_conv, both))
    far_own = gathered.reshape(8, 4, 64, BLOCK)
    far_other = swapped(far_own, "core")
    state = shape(2, SPAN, BLOCK, kind=F32)
    tiles = VMEM((2, 2, 4, HEAD_CHANNELS, BLOCK), BF16)
    tops, totals, sums = call(
        near_kernel,
        "near",
        (state, state, state),
        (query_conv, far_own, conv, near, both),
        scratch=[VMEM((4, 64, ROWS), BF16), tiles, VMEM((2, 11, CHUNK, BLOCK), F32)],
        flops=1 << 30,
    )
    return call(
        far_kernel,
        "far",
        shape(ROWS, HEAD_CHANNELS),
        (query_conv, far_other, tops, totals, sums, out_gain.reshape(1, -1)),
        scratch=[tiles, VMEM((2, 9, CHUNK, BLOCK), F32)] + [VMEM((2, SPAN, BLOCK), F32)] * 3,
        flops=1 << 30,
    )


def solution(mesh):
    fine = Mesh(mesh.devices.reshape(2, 4, 2, 8, 2, 2), CTX + MP)
    in_specs = (P(CTX, MP), P(CTX, MP), P(None, MP), P(None, MP), P(MP))
    return jax.shard_map(
        per_device, mesh=fine, in_specs=in_specs, out_specs=P(CTX, MP), check_vma=False
    )
```

```python
import functools
import math

import jax
import jax.numpy as jnp
import numpy as np
from jax import lax
from jax.experimental import pallas as pl
from jax.experimental.pallas import tpu as pltpu
from jax.sharding import Mesh, PartitionSpec as P

HEAD_CHANNELS = 128
TAPS = 4
BLOCK = 128
KEEP = 16
SPAN = 512
ROWS = 2 * SPAN
NEGATIVE = -1e30
EPSILON = 1e-06
EDGE = 16
SENT = 64 + 2 * EDGE
CHUNK = 256

CTX = ("y_lo", "x", "core")
MP = ("z_hi", "z_lo", "y_hi")
GROUP = ("z_lo", "y_hi")
CHIPS = ("y_lo", "x")

VMEM = pltpu.VMEM
SMEM = pltpu.SMEM
F32 = jnp.float32
BF16 = jnp.bfloat16
NT = (((1,), (1,)), ((), ()))
TN = (((0,), (0,)), ((), ()))


def spec(space=VMEM):
    return pl.BlockSpec(memory_space=space)


def dct_table():
    j = np.arange(KEEP, dtype=np.float32)[:, None]
    u = np.arange(BLOCK, dtype=np.float32)[None, :]
    table = np.cos(np.float32(math.pi) * (u + np.float32(0.5)) * j / np.float32(BLOCK))
    table = table * np.float32(math.sqrt(2.0 / BLOCK))
    table = np.where(j == 0, table * np.float32(math.sqrt(0.5)), table)
    return table.astype(jnp.bfloat16)


def dct_tile():
    return np.tile(dct_table().T, (1, BLOCK // KEEP))


def head_tables():
    table = dct_table()
    whole = np.zeros((16, 8, 2, 8, BLOCK), table.dtype)
    half = BLOCK // 2
    for owner in range(16):
        for t in range(TAPS - 1):
            low, high = (0, half) if owner % 2 == 0 else (half, 0)
            whole[owner, t, 0, owner // 2, low : low + KEEP] = table[:, t]
            whole[owner, 3 + t, 1, owner // 2, high : high + KEEP] = table[:, t]
    return whole.reshape(128, 16 * BLOCK)


def conv_kernel(
    kv_in, taps_in, table_in, conv_result, block_result, kv, taps, table, conv_out, block_out, sems
):
    moves = [(kv_in, kv), (taps_in, taps), (table_in, table)]
    moves += [(conv_out, conv_result), (block_out, block_result)]
    moves = [pltpu.make_async_copy(*move, sems.at[k]) for k, move in enumerate(moves)]
    for move in moves[:3]:
        move.start()
    for move in moves[:3]:
        move.wait()
    lanes = lax.broadcasted_iota(jnp.int32, (64, BLOCK), 1)
    turned = jnp.transpose(
        jnp.concatenate(
            [
                jnp.concatenate([taps[...], jnp.zeros((4, 64), F32)], 0),
                jnp.zeros((8, 64), F32),
            ],
            1,
        )
    )[:64]
    heads, tails = [], []
    for half in range(2):
        values = kv[:, half * SPAN : (half + 1) * SPAN].astype(F32)
        padded = jnp.concatenate([values, jnp.zeros((64, BLOCK), F32)], 1)
        total = turned[:, 0:1] * padded
        for w in range(1, TAPS):
            total = total + turned[:, w : w + 1] * pltpu.roll(padded, w, 1)
        conv_out[:, half * SPAN : (half + 1) * SPAN] = total[:, :SPAN].astype(BF16)
        if half:
            moves[3].start()
        heads.append(total[:, :BLOCK])
        tails.append(total[:, SPAN:])

    def join(pair):
        upper = pltpu.roll(pair[1], 3, 1)
        return jnp.where(lanes < 3, pair[0], jnp.where(lanes < 6, upper, 0.0))

    heads, tails = join(heads), join(tails)
    uneven = lax.axis_index("y_hi") == 1
    edges = jnp.concatenate([jnp.where(uneven, tails, heads), jnp.where(uneven, heads, tails)], 0)
    edges = jnp.transpose(edges)[:8]
    high = edges.astype(BF16)
    low = edges - high.astype(F32)
    edges = jnp.concatenate([high.astype(F32), low], 0).astype(BF16)
    packed = jnp.zeros((64, BLOCK), F32)
    for b in range(ROWS // BLOCK):
        part = conv_out[:, b * BLOCK : (b + 1) * BLOCK]
        if b * BLOCK % SPAN == 0:
            part = jnp.where(lanes < TAPS - 1, 0.0, part.astype(F32)).astype(BF16)
        part = jnp.dot(part, table[...], preferred_element_type=F32)
        packed = jnp.where(lanes // KEEP == b, part, packed)
    packed = jnp.where(lax.axis_index("core") == 1, pltpu.roll(packed, BLOCK // 2, 1), packed)
    high = packed.astype(BF16)
    low = jnp.where(lanes % (BLOCK // 2) < KEEP, packed - high.astype(F32), 0.0)
    rest = low[:EDGE]
    for g in range(1, 4):
        rest = rest + pltpu.roll(low[g * EDGE : (g + 1) * EDGE], g * KEEP, 1)
    rest = rest.astype(BF16)
    for k in range(block_out.shape[0]):
        block_out[k, :64] = high
        block_out[k, 64 : 64 + EDGE] = edges
        block_out[k, 64 + EDGE :] = rest
    moves[4].start()
    moves[3].wait()
    moves[4].wait()


def join_kernel(mine, near, out):
    out[:64] = mine[...]
    out[64:] = near[...]


def query_kernel(q, own, swap, hop, taps, out):
    place = lax.axis_index(CTX)
    odd = place % 2 == 1
    own, swap, hop = own[...].astype(F32), swap[...].astype(F32), hop[...].astype(F32)
    lower = jnp.where(odd, swap[0], hop[0])
    lower = jnp.where(place == 0, jnp.zeros_like(lower), lower)
    upper = jnp.where(odd, hop[1], swap[1])
    upper = jnp.where(place == 15, own[0], upper)
    for half, halo in enumerate((lower, upper)):
        for b in range(SPAN // BLOCK):
            start = half * SPAN + b * BLOCK
            values = q[start : start + BLOCK].astype(F32)
            if b:
                halo = q[start - EDGE : start].astype(F32)
            padded = jnp.concatenate([halo, values], 0)
            total = taps[0:1] * values
            for w in range(1, TAPS):
                total = total + taps[w : w + 1] * pltpu.roll(padded, w, 0)[EDGE:]
            out[start : start + BLOCK] = total.astype(BF16)


def pairs_kernel(mine, near, far, pairs):
    member = lax.axis_index(GROUP)
    pairs[member] = mine[...]
    pairs[member ^ 1] = near[...]
    pairs[member ^ 2] = far[:64]
    pairs[member ^ 3] = far[64:]


def attend_kernel(q, pairs, far_own, far_other, table, gain, out, packed, scores, ends):
    place = lax.axis_index(CTX)
    middle = place // 2
    odd = place % 2 == 1
    factor = math.log2(math.e) / math.sqrt(HEAD_CHANNELS)
    lane = lax.broadcasted_iota(jnp.int32, (BLOCK, BLOCK), 1)
    row = lax.broadcasted_iota(jnp.int32, (BLOCK, BLOCK), 0)
    edge_lane = lax.broadcasted_iota(jnp.int32, (8, BLOCK), 1) < BLOCK // 2
    edge_row = lax.broadcasted_iota(jnp.int32, (8, BLOCK), 0)
    tile_lane = lax.broadcasted_iota(jnp.int32, (64, BLOCK), 1)
    own_lane = jnp.where(tile_lane < BLOCK // 2, 1, 0) != jnp.where(odd, 1, 0)
    first_lane = lax.broadcasted_iota(jnp.int32, (EDGE, BLOCK), 1) % (BLOCK // 2) < KEEP

    def turned(value):
        return pltpu.roll(value, BLOCK // 2, 1)

    def edges_of(owner, m):
        mine = far_own[owner // 2, m, 64 : 64 + EDGE]
        other = far_other[owner // 2, m, 64 : 64 + EDGE]
        tile = jnp.where(odd, other, mine) if owner % 2 == 0 else jnp.where(odd, mine, other)
        tile = tile.astype(F32)
        return tile[:8] + tile[8:]

    def whole_tile(ref, i, m):
        rest = ref[i, m, 64 + EDGE :].astype(F32)
        parts = [rest] + [pltpu.roll(rest, BLOCK - g * KEEP, 1) for g in range(1, 4)]
        parts = [jnp.where(first_lane, part, 0.0) for part in parts]
        return ref[i, m, :64].astype(F32) + jnp.concatenate(parts, 0)

    first_rows = []
    for kind in range(2):
        heads, tails = [], []
        for owner in range(16):
            left, right = edges_of(owner, 2 * kind), edges_of(owner, 2 * kind + 1)
            heads.append(jnp.where(edge_lane, left, right))
            tails.append(turned(jnp.where(edge_lane, right, left)))
        for owner in range(16):
            below = tails[owner - 1] if owner else jnp.zeros((8, BLOCK), F32)
            above = tails[owner + 1] if owner < 15 else pltpu.roll(tails[15], 3, 0)
            ends[kind, owner] = heads[owner] + jnp.where(edge_row < 3, below, above)
        both = jnp.transpose(ends[kind].reshape(128, HEAD_CHANNELS)).astype(BF16)
        fix = jnp.dot(both, table[...], preferred_element_type=F32)
        for i in range(8):
            for m in range(2):
                rows = slice(64 * m, 64 * (m + 1))
                mine = whole_tile(far_own, i, 2 * kind + m)
                other = whole_tile(far_other, i, 2 * kind + m)
                low = jnp.where(own_lane, mine, other) + fix[rows, i * BLOCK : (i + 1) * BLOCK]
                high = jnp.where(own_lane, other, mine)
                high = high + fix[rows, (8 + i) * BLOCK : (9 + i) * BLOCK]
                packed[kind, 0, i, rows] = low.astype(BF16)
                packed[kind, 1, i, rows] = high.astype(BF16)
        pick = (
            (edge_row < 3)
            & (lax.broadcasted_iota(jnp.int32, (8, BLOCK), 1) == edge_row)
        ) | (
            (edge_row >= 3)
            & (edge_row < 6)
            & (lax.broadcasted_iota(jnp.int32, (8, BLOCK), 1) == edge_row - 3 + BLOCK // 2)
        )
        first_rows.append(
            lax.dot_general(
                ends[kind, place].astype(BF16),
                jnp.where(pick, 1.0, 0.0).astype(BF16),
                TN,
                preferred_element_type=F32,
            )
        )

    def near_tile(kind, start):
        tile = jnp.concatenate(
            [pairs[2 * kind, :, start : start + BLOCK], pairs[2 * kind + 1, :, start : start + BLOCK]], 0
        )
        if start % SPAN == 0:
            first = first_rows[kind] if start == 0 else turned(first_rows[kind])
            tile = jnp.where(lane < TAPS - 1, first, tile.astype(F32)).astype(BF16)
        return tile

    key_block = (lax.broadcasted_iota(jnp.int32, (1, BLOCK), 1) % (BLOCK // 2)) // KEEP
    left_lanes = lax.broadcasted_iota(jnp.int32, (1, BLOCK), 1) < BLOCK // 2
    per_chunk = CHUNK // BLOCK
    for r in range(SPAN // CHUNK):
        tops = [jnp.full((CHUNK, BLOCK), NEGATIVE, F32) for _ in range(2)]
        for half in range(2):
            tiles = []
            for c in range(per_chunk):
                start = half * SPAN + r * CHUNK + c * BLOCK
                near = jnp.dot(
                    q[start : start + BLOCK], near_tile(0, start), preferred_element_type=F32
                )
                tiles.append(jnp.where(row >= lane, near, NEGATIVE))
            tops[half] = jnp.concatenate(tiles, 0)
            scores[17 + half] = tops[half]
        upper = q[SPAN + r * CHUNK : SPAN + (r + 1) * CHUNK]
        for i in range(4):
            far = jnp.dot(
                upper,
                jnp.concatenate([packed[0, 0, 2 * i], packed[0, 0, 2 * i + 1]], 1),
                preferred_element_type=F32,
            )
            scores[9 + 2 * i] = far[:, :BLOCK]
            scores[10 + 2 * i] = far[:, BLOCK:]
            tops[1] = jnp.maximum(tops[1], jnp.maximum(far[:, :BLOCK], far[:, BLOCK:]))
        for j in range(9):
            high = j > middle
            side = high.astype(jnp.int32)
            partial = (j == middle) | (j == middle + 1)
            start = pl.multiple_of(side * SPAN + r * CHUNK, CHUNK)
            far = jnp.dot(
                q[pl.ds(start, CHUNK)], packed[0, side, j - side], preferred_element_type=F32
            )
            biases = []
            for c in range(per_chunk):
                block = r * per_chunk + c
                left = jnp.where(high, jnp.where(odd, block, 4), jnp.where(odd, 4, block))
                right = jnp.where(high, jnp.where(odd, 0, block), jnp.where(odd, block, 0))
                left, right = jnp.where(partial, left, 4), jnp.where(partial, right, 4)
                seen = key_block < jnp.where(left_lanes, left, right)
                biases.append(
                    jnp.broadcast_to(jnp.where(seen, 0.0, NEGATIVE), (BLOCK, BLOCK))
                )
            far = far + jnp.concatenate(biases, 0)
            scores[j] = far
            tops[0] = jnp.maximum(tops[0], jnp.where(high, NEGATIVE, far))
            tops[1] = jnp.maximum(tops[1], jnp.where(high, far, NEGATIVE))
        tops = [
            jnp.broadcast_to(jnp.max(t, 1, keepdims=True) * factor, (CHUNK, BLOCK)) for t in tops
        ]
        totals, sums = [], []
        for half in range(2):
            weights = jnp.exp2(scores[17 + half] * factor - tops[half])
            totals.append(weights)
            weights = weights.astype(BF16)
            sums.append(
                jnp.concatenate(
                    [
                        lax.dot_general(
                            weights[c * BLOCK : (c + 1) * BLOCK],
                            near_tile(1, half * SPAN + r * CHUNK + c * BLOCK),
                            NT,
                            preferred_element_type=F32,
                        )
                        for c in range(per_chunk)
                    ],
                    0,
                )
            )
        for i in range(4):
            first = jnp.exp2(scores[9 + 2 * i] * factor - tops[1])
            second = jnp.exp2(scores[10 + 2 * i] * factor - tops[1])
            totals[1] = totals[1] + first + second
            sums[1] = sums[1] + lax.dot_general(
                jnp.concatenate([first, second], 1).astype(BF16),
                jnp.concatenate([packed[1, 0, 2 * i], packed[1, 0, 2 * i + 1]], 1),
                NT,
                preferred_element_type=F32,
            )
        for j in range(9):
            high = j > middle
            side = high.astype(jnp.int32)
            weights = jnp.exp2(scores[j] * factor - jnp.where(high, tops[1], tops[0]))
            totals[0] = totals[0] + jnp.where(high, 0.0, weights)
            totals[1] = totals[1] + jnp.where(high, weights, 0.0)
            part = lax.dot_general(
                weights.astype(BF16), packed[1, side, j - side], NT, preferred_element_type=F32
            )
            sums[0] = sums[0] + jnp.where(high, 0.0, part)
            sums[1] = sums[1] + jnp.where(high, part, 0.0)
        for half in range(2):
            attended = sums[half] / jnp.sum(totals[half], 1, keepdims=True)
            mean = jnp.mean(attended * attended, 1, keepdims=True)
            normed = attended * lax.rsqrt(mean + EPSILON)
            start = half * SPAN + r * CHUNK
            out[start : start + CHUNK] = (normed * gain[...]).astype(BF16)


def cost(flops, moved):
    return pl.CostEstimate(flops=flops, bytes_accessed=moved, transcendentals=0)


def swapped(value, axis):
    return lax.ppermute(value, axis, [(0, 1), (1, 0)])


def per_device(queries, keys_values, query_taps, pair_taps, out_gain):
    def call(kernel, name, out_shape, operands, spaces=None, scratch=(), flops=1 << 24):
        many = isinstance(out_shape, tuple)
        return pl.pallas_call(
            kernel,
            out_shape=out_shape,
            in_specs=[spec(s) for s in spaces] if spaces else [spec()] * len(operands),
            out_specs=(spec(),) * len(out_shape) if many else spec(),
            scratch_shapes=scratch,
            compiler_params=pltpu.CompilerParams(vmem_limit_bytes=24 << 20),
            cost_estimate=cost(flops, 1 << 20),
            name=name,
        )(*operands)

    def shape(*dims):
        return jax.ShapeDtypeStruct(dims, BF16)

    conv, blocks = pl.pallas_call(
        conv_kernel,
        out_shape=(shape(64, ROWS), shape(32, SENT, BLOCK)),
        in_specs=[spec(pl.ANY)] * 3,
        out_specs=(spec(pl.ANY), spec(pl.ANY)),
        scratch_shapes=[
            VMEM((64, ROWS), BF16),
            VMEM((TAPS, 64), F32),
            VMEM((BLOCK, BLOCK), BF16),
            VMEM((64, ROWS), BF16),
            VMEM((32, SENT, BLOCK), BF16),
            pltpu.SemaphoreType.DMA((5,)),
        ],
        compiler_params=pltpu.CompilerParams(vmem_limit_bytes=56 << 20),
        cost_estimate=cost(1 << 24, 1 << 20),
        name="conv",
    )(keys_values.T, pair_taps, jnp.asarray(dct_tile()))
    gathered = lax.all_to_all(blocks, CHIPS + GROUP, 0, 0, tiled=True)
    near = swapped(conv, "y_hi")
    far = call(join_kernel, "join", shape(128, ROWS), (conv, near), flops=1 << 37)
    far = swapped(far, "z_lo")
    tails = jnp.stack([queries[e - EDGE : e] for e in (SPAN, ROWS)])
    swap = swapped(tails, "core")
    hop = lax.ppermute(
        tails, CTX, [(i, i + 1) for i in range(1, 15, 2)] + [(i + 1, i) for i in range(1, 15, 2)]
    )
    query_conv = call(
        query_kernel,
        "queries",
        shape(ROWS, HEAD_CHANNELS),
        (queries, tails, swap, hop, query_taps),
    )
    gathered, query_conv, far = lax.optimization_barrier((gathered, query_conv, far))
    far_own = gathered.reshape(8, 4, SENT, BLOCK)
    far_other = swapped(far_own, "core")
    pairs = call(pairs_kernel, "pairs", shape(4, 64, ROWS), (conv, near, far))
    return call(
        attend_kernel,
        "attend",
        shape(ROWS, HEAD_CHANNELS),
        (query_conv, pairs, far_own, far_other, jnp.asarray(head_tables()), out_gain.reshape(1, -1)),
        scratch=[
            VMEM((2, 2, 8, HEAD_CHANNELS, BLOCK), BF16),
            VMEM((19, CHUNK, BLOCK), F32),
            VMEM((2, 16, 8, HEAD_CHANNELS), F32),
        ],
        flops=1 << 30,
    )


def solution(mesh):
    fine = Mesh(mesh.devices.reshape(2, 4, 2, 8, 2, 2), CTX + MP)
    in_specs = (P(CTX, MP), P(CTX, MP), P(None, MP), P(None, MP), P(MP))
    return jax.shard_map(
        per_device, mesh=fine, in_specs=in_specs, out_specs=P(CTX, MP), check_vma=False
    )
```

```python
import functools
import math

import jax
import jax.numpy as jnp
import numpy as np
from jax import lax
from jax.experimental import pallas as pl
from jax.experimental.pallas import tpu as pltpu
from jax.sharding import Mesh, PartitionSpec as P

HEAD_CHANNELS = 128
TAPS = 4
BLOCK = 128
KEEP = 16
SPAN = 512
ROWS = 2 * SPAN
NEGATIVE = -1e30
EPSILON = 1e-06
EDGE = 16
SENT = 64 + 2 * EDGE
CHUNK = 256

CTX = ("y_lo", "x", "core")
MP = ("z_hi", "z_lo", "y_hi")
GROUP = ("z_lo", "y_hi")
CHIPS = ("y_lo", "x")

VMEM = pltpu.VMEM
SMEM = pltpu.SMEM
F32 = jnp.float32
BF16 = jnp.bfloat16
NT = (((1,), (1,)), ((), ()))
TN = (((0,), (0,)), ((), ()))


def spec(space=VMEM):
    return pl.BlockSpec(memory_space=space)


def dct_table():
    j = np.arange(KEEP, dtype=np.float32)[:, None]
    u = np.arange(BLOCK, dtype=np.float32)[None, :]
    table = np.cos(np.float32(math.pi) * (u + np.float32(0.5)) * j / np.float32(BLOCK))
    table = table * np.float32(math.sqrt(2.0 / BLOCK))
    table = np.where(j == 0, table * np.float32(math.sqrt(0.5)), table)
    return table.astype(jnp.bfloat16)


def dct_tile():
    return np.tile(dct_table().T, (1, BLOCK // KEEP))


def head_tables():
    table = dct_table()
    whole = np.zeros((16, 8, 2, 8, BLOCK), table.dtype)
    half = BLOCK // 2
    for owner in range(16):
        for t in range(TAPS - 1):
            low, high = (0, half) if owner % 2 == 0 else (half, 0)
            whole[owner, t, 0, owner // 2, low : low + KEEP] = table[:, t]
            whole[owner, 3 + t, 1, owner // 2, high : high + KEEP] = table[:, t]
    return whole.reshape(128, 16 * BLOCK)


def conv_kernel(
    kv_in, taps_in, table_in, conv_result, block_result, kv, taps, table, conv_out, block_out, sems
):
    moves = [(kv_in, kv), (taps_in, taps), (table_in, table)]
    moves += [(conv_out, conv_result), (block_out, block_result)]
    moves = [pltpu.make_async_copy(*move, sems.at[k]) for k, move in enumerate(moves)]
    for move in moves[:3]:
        move.start()
    for move in moves[:3]:
        move.wait()
    lanes = lax.broadcasted_iota(jnp.int32, (64, BLOCK), 1)
    turned = jnp.transpose(
        jnp.concatenate(
            [
                jnp.concatenate([taps[...], jnp.zeros((4, 64), F32)], 0),
                jnp.zeros((8, 64), F32),
            ],
            1,
        )
    )[:64]
    heads, tails = [], []
    for half in range(2):
        values = kv[:, half * SPAN : (half + 1) * SPAN].astype(F32)
        padded = jnp.concatenate([values, jnp.zeros((64, BLOCK), F32)], 1)
        total = turned[:, 0:1] * padded
        for w in range(1, TAPS):
            total = total + turned[:, w : w + 1] * pltpu.roll(padded, w, 1)
        conv_out[:, half * SPAN : (half + 1) * SPAN] = total[:, :SPAN].astype(BF16)
        if half:
            moves[3].start()
        heads.append(total[:, :BLOCK])
        tails.append(total[:, SPAN:])

    def join(pair):
        upper = pltpu.roll(pair[1], 3, 1)
        return jnp.where(lanes < 3, pair[0], jnp.where(lanes < 6, upper, 0.0))

    heads, tails = join(heads), join(tails)
    uneven = lax.axis_index("y_hi") == 1
    edges = jnp.concatenate([jnp.where(uneven, tails, heads), jnp.where(uneven, heads, tails)], 0)
    edges = jnp.transpose(edges)[:8]
    high = edges.astype(BF16)
    low = edges - high.astype(F32)
    edges = jnp.concatenate([high.astype(F32), low], 0).astype(BF16)
    packed = jnp.zeros((64, BLOCK), F32)
    for b in range(ROWS // BLOCK):
        part = conv_out[:, b * BLOCK : (b + 1) * BLOCK]
        if b * BLOCK % SPAN == 0:
            part = jnp.where(lanes < TAPS - 1, 0.0, part.astype(F32)).astype(BF16)
        part = jnp.dot(part, table[...], preferred_element_type=F32)
        packed = jnp.where(lanes // KEEP == b, part, packed)
    packed = jnp.where(lax.axis_index("core") == 1, pltpu.roll(packed, BLOCK // 2, 1), packed)
    high = packed.astype(BF16)
    low = jnp.where(lanes % (BLOCK // 2) < KEEP, packed - high.astype(F32), 0.0)
    rest = low[:EDGE]
    for g in range(1, 4):
        rest = rest + pltpu.roll(low[g * EDGE : (g + 1) * EDGE], g * KEEP, 1)
    rest = rest.astype(BF16)
    for k in range(block_out.shape[0]):
        block_out[k, :64] = high
        block_out[k, 64 : 64 + EDGE] = edges
        block_out[k, 64 + EDGE :] = rest
    moves[4].start()
    moves[3].wait()
    moves[4].wait()


def join_kernel(mine, near, out):
    out[:64] = mine[...]
    out[64:] = near[...]


def query_kernel(q, own, swap, hop, taps, out):
    place = lax.axis_index(CTX)
    odd = place % 2 == 1
    own, swap, hop = own[...].astype(F32), swap[...].astype(F32), hop[...].astype(F32)
    lower = jnp.where(odd, swap[0], hop[0])
    lower = jnp.where(place == 0, jnp.zeros_like(lower), lower)
    upper = jnp.where(odd, hop[1], swap[1])
    upper = jnp.where(place == 15, own[0], upper)
    for half, halo in enumerate((lower, upper)):
        for b in range(SPAN // BLOCK):
            start = half * SPAN + b * BLOCK
            values = q[start : start + BLOCK].astype(F32)
            if b:
                halo = q[start - EDGE : start].astype(F32)
            padded = jnp.concatenate([halo, values], 0)
            total = taps[0:1] * values
            for w in range(1, TAPS):
                total = total + taps[w : w + 1] * pltpu.roll(padded, w, 0)[EDGE:]
            out[start : start + BLOCK] = total.astype(BF16)


def pairs_kernel(mine, near, far, pairs):
    member = lax.axis_index(GROUP)
    pairs[member] = mine[...]
    pairs[member ^ 1] = near[...]
    pairs[member ^ 2] = far[:64]
    pairs[member ^ 3] = far[64:]


def attend_kernel(q, pairs, far_own, far_other, table, gain, out, packed, scores, ends):
    place = lax.axis_index(CTX)
    middle = place // 2
    odd = place % 2 == 1
    factor = math.log2(math.e) / math.sqrt(HEAD_CHANNELS)
    lane = lax.broadcasted_iota(jnp.int32, (BLOCK, BLOCK), 1)
    row = lax.broadcasted_iota(jnp.int32, (BLOCK, BLOCK), 0)
    edge_lane = lax.broadcasted_iota(jnp.int32, (8, BLOCK), 1) < BLOCK // 2
    edge_row = lax.broadcasted_iota(jnp.int32, (8, BLOCK), 0)
    tile_lane = lax.broadcasted_iota(jnp.int32, (64, BLOCK), 1)
    own_lane = jnp.where(tile_lane < BLOCK // 2, 1, 0) != jnp.where(odd, 1, 0)
    first_lane = lax.broadcasted_iota(jnp.int32, (EDGE, BLOCK), 1) % (BLOCK // 2) < KEEP

    def turned(value):
        return pltpu.roll(value, BLOCK // 2, 1)

    def edges_of(owner, m):
        mine = far_own[owner // 2, m, 64 : 64 + EDGE]
        other = far_other[owner // 2, m, 64 : 64 + EDGE]
        tile = jnp.where(odd, other, mine) if owner % 2 == 0 else jnp.where(odd, mine, other)
        tile = tile.astype(F32)
        return tile[:8] + tile[8:]

    def whole_tile(ref, i, m):
        rest = ref[i, m, 64 + EDGE :].astype(F32)
        parts = [rest] + [pltpu.roll(rest, BLOCK - g * KEEP, 1) for g in range(1, 4)]
        parts = [jnp.where(first_lane, part, 0.0) for part in parts]
        return ref[i, m, :64].astype(F32) + jnp.concatenate(parts, 0)

    first_rows = []
    for kind in range(2):
        heads, tails = [], []
        for owner in range(16):
            left, right = edges_of(owner, 2 * kind), edges_of(owner, 2 * kind + 1)
            heads.append(jnp.where(edge_lane, left, right))
            tails.append(turned(jnp.where(edge_lane, right, left)))
        for owner in range(16):
            below = tails[owner - 1] if owner else jnp.zeros((8, BLOCK), F32)
            above = tails[owner + 1] if owner < 15 else pltpu.roll(tails[15], 3, 0)
            ends[kind, owner] = heads[owner] + jnp.where(edge_row < 3, below, above)
        both = jnp.transpose(ends[kind].reshape(128, HEAD_CHANNELS)).astype(BF16)
        fix = jnp.dot(both, table[...], preferred_element_type=F32)
        for i in range(8):
            for m in range(2):
                rows = slice(64 * m, 64 * (m + 1))
                mine = whole_tile(far_own, i, 2 * kind + m)
                other = whole_tile(far_other, i, 2 * kind + m)
                low = jnp.where(own_lane, mine, other) + fix[rows, i * BLOCK : (i + 1) * BLOCK]
                high = jnp.where(own_lane, other, mine)
                high = high + fix[rows, (8 + i) * BLOCK : (9 + i) * BLOCK]
                packed[kind, 0, i, rows] = low.astype(BF16)
                packed[kind, 1, i, rows] = high.astype(BF16)
        pick = (
            (edge_row < 3)
            & (lax.broadcasted_iota(jnp.int32, (8, BLOCK), 1) == edge_row)
        ) | (
            (edge_row >= 3)
            & (edge_row < 6)
            & (lax.broadcasted_iota(jnp.int32, (8, BLOCK), 1) == edge_row - 3 + BLOCK // 2)
        )
        first_rows.append(
            lax.dot_general(
                ends[kind, place].astype(BF16),
                jnp.where(pick, 1.0, 0.0).astype(BF16),
                TN,
                preferred_element_type=F32,
            )
        )

    def near_tile(kind, start):
        tile = jnp.concatenate(
            [pairs[2 * kind, :, start : start + BLOCK], pairs[2 * kind + 1, :, start : start + BLOCK]], 0
        )
        if start % SPAN == 0:
            first = first_rows[kind] if start == 0 else turned(first_rows[kind])
            tile = jnp.where(lane < TAPS - 1, first, tile.astype(F32)).astype(BF16)
        return tile

    key_block = (lax.broadcasted_iota(jnp.int32, (1, BLOCK), 1) % (BLOCK // 2)) // KEEP
    left_lanes = lax.broadcasted_iota(jnp.int32, (1, BLOCK), 1) < BLOCK // 2
    per_chunk = CHUNK // BLOCK
    for r in range(SPAN // CHUNK):
        tops = [jnp.full((CHUNK, BLOCK), NEGATIVE, F32) for _ in range(2)]
        for half in range(2):
            tiles = []
            for c in range(per_chunk):
                start = half * SPAN + r * CHUNK + c * BLOCK
                near = jnp.dot(
                    q[start : start + BLOCK], near_tile(0, start), preferred_element_type=F32
                )
                tiles.append(jnp.where(row >= lane, near, NEGATIVE))
            tops[half] = jnp.concatenate(tiles, 0)
            scores[17 + half] = tops[half]
        upper = q[SPAN + r * CHUNK : SPAN + (r + 1) * CHUNK]
        for i in range(4):
            far = jnp.dot(
                upper,
                jnp.concatenate([packed[0, 0, 2 * i], packed[0, 0, 2 * i + 1]], 1),
                preferred_element_type=F32,
            )
            scores[9 + 2 * i] = far[:, :BLOCK]
            scores[10 + 2 * i] = far[:, BLOCK:]
            tops[1] = jnp.maximum(tops[1], jnp.maximum(far[:, :BLOCK], far[:, BLOCK:]))
        for j in range(9):
            high = j > middle
            side = high.astype(jnp.int32)
            partial = (j == middle) | (j == middle + 1)
            start = pl.multiple_of(side * SPAN + r * CHUNK, CHUNK)
            far = jnp.dot(
                q[pl.ds(start, CHUNK)], packed[0, side, j - side], preferred_element_type=F32
            )
            biases = []
            for c in range(per_chunk):
                block = r * per_chunk + c
                left = jnp.where(high, jnp.where(odd, block, 4), jnp.where(odd, 4, block))
                right = jnp.where(high, jnp.where(odd, 0, block), jnp.where(odd, block, 0))
                left, right = jnp.where(partial, left, 4), jnp.where(partial, right, 4)
                seen = key_block < jnp.where(left_lanes, left, right)
                biases.append(
                    jnp.broadcast_to(jnp.where(seen, 0.0, NEGATIVE), (BLOCK, BLOCK))
                )
            far = far + jnp.concatenate(biases, 0)
            scores[j] = far
            tops[0] = jnp.maximum(tops[0], jnp.where(high, NEGATIVE, far))
            tops[1] = jnp.maximum(tops[1], jnp.where(high, far, NEGATIVE))
        tops = [
            jnp.broadcast_to(jnp.max(t, 1, keepdims=True) * factor, (CHUNK, BLOCK)) for t in tops
        ]
        totals, sums = [], []
        for half in range(2):
            weights = jnp.exp2(scores[17 + half] * factor - tops[half])
            totals.append(weights)
            weights = weights.astype(BF16)
            sums.append(
                jnp.concatenate(
                    [
                        lax.dot_general(
                            weights[c * BLOCK : (c + 1) * BLOCK],
                            near_tile(1, half * SPAN + r * CHUNK + c * BLOCK),
                            NT,
                            preferred_element_type=F32,
                        )
                        for c in range(per_chunk)
                    ],
                    0,
                )
            )
        for i in range(4):
            first = jnp.exp2(scores[9 + 2 * i] * factor - tops[1])
            second = jnp.exp2(scores[10 + 2 * i] * factor - tops[1])
            totals[1] = totals[1] + first + second
            sums[1] = sums[1] + lax.dot_general(
                jnp.concatenate([first, second], 1).astype(BF16),
                jnp.concatenate([packed[1, 0, 2 * i], packed[1, 0, 2 * i + 1]], 1),
                NT,
                preferred_element_type=F32,
            )
        for j in range(9):
            high = j > middle
            side = high.astype(jnp.int32)
            weights = jnp.exp2(scores[j] * factor - jnp.where(high, tops[1], tops[0]))
            totals[0] = totals[0] + jnp.where(high, 0.0, weights)
            totals[1] = totals[1] + jnp.where(high, weights, 0.0)
            part = lax.dot_general(
                weights.astype(BF16), packed[1, side, j - side], NT, preferred_element_type=F32
            )
            sums[0] = sums[0] + jnp.where(high, 0.0, part)
            sums[1] = sums[1] + jnp.where(high, part, 0.0)
        for half in range(2):
            attended = sums[half] / jnp.sum(totals[half], 1, keepdims=True)
            mean = jnp.mean(attended * attended, 1, keepdims=True)
            normed = attended * lax.rsqrt(mean + EPSILON)
            start = half * SPAN + r * CHUNK
            out[start : start + CHUNK] = (normed * gain[...]).astype(BF16)


def cost(flops, moved):
    return pl.CostEstimate(flops=flops, bytes_accessed=moved, transcendentals=0)


def swapped(value, axis):
    return lax.ppermute(value, axis, [(0, 1), (1, 0)])


def per_device(queries, keys_values, query_taps, pair_taps, out_gain):
    def call(kernel, name, out_shape, operands, spaces=None, scratch=(), flops=1 << 24):
        many = isinstance(out_shape, tuple)
        return pl.pallas_call(
            kernel,
            out_shape=out_shape,
            in_specs=[spec(s) for s in spaces] if spaces else [spec()] * len(operands),
            out_specs=(spec(),) * len(out_shape) if many else spec(),
            scratch_shapes=scratch,
            compiler_params=pltpu.CompilerParams(vmem_limit_bytes=24 << 20),
            cost_estimate=cost(flops, 1 << 20),
            name=name,
        )(*operands)

    def shape(*dims):
        return jax.ShapeDtypeStruct(dims, BF16)

    conv, blocks = pl.pallas_call(
        conv_kernel,
        out_shape=(shape(64, ROWS), shape(32, SENT, BLOCK)),
        in_specs=[spec(pl.ANY)] * 3,
        out_specs=(spec(pl.ANY), spec(pl.ANY)),
        scratch_shapes=[
            VMEM((64, ROWS), BF16),
            VMEM((TAPS, 64), F32),
            VMEM((BLOCK, BLOCK), BF16),
            VMEM((64, ROWS), BF16),
            VMEM((32, SENT, BLOCK), BF16),
            pltpu.SemaphoreType.DMA((5,)),
        ],
        compiler_params=pltpu.CompilerParams(vmem_limit_bytes=56 << 20),
        cost_estimate=cost(1 << 24, 1 << 20),
        name="conv",
    )(keys_values.T, pair_taps, jnp.asarray(dct_tile()))
    gathered = lax.all_to_all(blocks, CHIPS + GROUP, 0, 0, tiled=True)
    near = swapped(conv, "y_hi")
    far = call(join_kernel, "join", shape(128, ROWS), (conv, near), flops=1 << 37)
    far = swapped(far, "z_lo")
    tails = jnp.stack([queries[e - EDGE : e] for e in (SPAN, ROWS)])
    swap = swapped(tails, "core")
    hop = lax.ppermute(
        tails, CTX, [(i, i + 1) for i in range(1, 15, 2)] + [(i + 1, i) for i in range(1, 15, 2)]
    )
    query_conv = call(
        query_kernel,
        "queries",
        shape(ROWS, HEAD_CHANNELS),
        (queries, tails, swap, hop, query_taps),
    )
    gathered, query_conv = lax.optimization_barrier((gathered, query_conv))
    far_own = gathered.reshape(8, 4, SENT, BLOCK)
    far_other = swapped(far_own, "core")
    pairs = call(pairs_kernel, "pairs", shape(4, 64, ROWS), (conv, near, far), flops=1 << 37)
    return call(
        attend_kernel,
        "attend",
        shape(ROWS, HEAD_CHANNELS),
        (query_conv, pairs, far_own, far_other, jnp.asarray(head_tables()), out_gain.reshape(1, -1)),
        scratch=[
            VMEM((2, 2, 8, HEAD_CHANNELS, BLOCK), BF16),
            VMEM((19, CHUNK, BLOCK), F32),
            VMEM((2, 16, 8, HEAD_CHANNELS), F32),
        ],
        flops=1 << 30,
    )


def solution(mesh):
    fine = Mesh(mesh.devices.reshape(2, 4, 2, 8, 2, 2), CTX + MP)
    in_specs = (P(CTX, MP), P(CTX, MP), P(None, MP), P(None, MP), P(MP))
    return jax.shard_map(
        per_device, mesh=fine, in_specs=in_specs, out_specs=P(CTX, MP), check_vma=False
    )
```

```python
import functools
import math

import jax
import jax.numpy as jnp
import numpy as np
from jax import lax
from jax.experimental import pallas as pl
from jax.experimental.pallas import tpu as pltpu
from jax.sharding import Mesh, PartitionSpec as P

HEAD_CHANNELS = 128
TAPS = 4
BLOCK = 128
KEEP = 16
SPAN = 512
ROWS = 2 * SPAN
NEGATIVE = -1e30
EPSILON = 1e-06
EDGE = 16
SENT = 64 + 2 * EDGE
CHUNK = 256

CTX = ("y_lo", "x", "core")
MP = ("z_hi", "z_lo", "y_hi")
GROUP = ("z_lo", "y_hi")
CHIPS = ("y_lo", "x")

VMEM = pltpu.VMEM
SMEM = pltpu.SMEM
F32 = jnp.float32
BF16 = jnp.bfloat16
NT = (((1,), (1,)), ((), ()))
TN = (((0,), (0,)), ((), ()))


def spec(space=VMEM):
    return pl.BlockSpec(memory_space=space)


def dct_table():
    j = np.arange(KEEP, dtype=np.float32)[:, None]
    u = np.arange(BLOCK, dtype=np.float32)[None, :]
    table = np.cos(np.float32(math.pi) * (u + np.float32(0.5)) * j / np.float32(BLOCK))
    table = table * np.float32(math.sqrt(2.0 / BLOCK))
    table = np.where(j == 0, table * np.float32(math.sqrt(0.5)), table)
    return table.astype(jnp.bfloat16)


def dct_tile():
    return np.tile(dct_table().T, (1, BLOCK // KEEP))


def head_tables():
    table = dct_table()
    whole = np.zeros((16, 8, 2, 8, BLOCK), table.dtype)
    half = BLOCK // 2
    for owner in range(16):
        for t in range(TAPS - 1):
            low, high = (0, half) if owner % 2 == 0 else (half, 0)
            whole[owner, t, 0, owner // 2, low : low + KEEP] = table[:, t]
            whole[owner, 3 + t, 1, owner // 2, high : high + KEEP] = table[:, t]
    return whole.reshape(128, 16 * BLOCK)


def conv_kernel(
    kv_in, taps_in, table_in, conv_result, block_result, kv, taps, table, conv_out, block_out, sems
):
    moves = [(kv_in, kv), (taps_in, taps), (table_in, table)]
    moves += [(conv_out, conv_result), (block_out, block_result)]
    moves = [pltpu.make_async_copy(*move, sems.at[k]) for k, move in enumerate(moves)]
    for move in moves[:3]:
        move.start()
    for move in moves[:3]:
        move.wait()
    lanes = lax.broadcasted_iota(jnp.int32, (64, BLOCK), 1)
    turned = jnp.transpose(
        jnp.concatenate(
            [
                jnp.concatenate([taps[...], jnp.zeros((4, 64), F32)], 0),
                jnp.zeros((8, 64), F32),
            ],
            1,
        )
    )[:64]
    heads, tails = [], []
    for half in range(2):
        values = kv[:, half * SPAN : (half + 1) * SPAN].astype(F32)
        padded = jnp.concatenate([values, jnp.zeros((64, BLOCK), F32)], 1)
        total = turned[:, 0:1] * padded
        for w in range(1, TAPS):
            total = total + turned[:, w : w + 1] * pltpu.roll(padded, w, 1)
        conv_out[:, half * SPAN : (half + 1) * SPAN] = total[:, :SPAN].astype(BF16)
        if half:
            moves[3].start()
        heads.append(total[:, :BLOCK])
        tails.append(total[:, SPAN:])

    def join(pair):
        upper = pltpu.roll(pair[1], 3, 1)
        return jnp.where(lanes < 3, pair[0], jnp.where(lanes < 6, upper, 0.0))

    heads, tails = join(heads), join(tails)
    uneven = lax.axis_index("y_hi") == 1
    edges = jnp.concatenate([jnp.where(uneven, tails, heads), jnp.where(uneven, heads, tails)], 0)
    edges = jnp.transpose(edges)[:8]
    high = edges.astype(BF16)
    low = edges - high.astype(F32)
    edges = jnp.concatenate([high.astype(F32), low], 0).astype(BF16)
    packed = jnp.zeros((64, BLOCK), F32)
    for b in range(ROWS // BLOCK):
        part = conv_out[:, b * BLOCK : (b + 1) * BLOCK]
        if b * BLOCK % SPAN == 0:
            part = jnp.where(lanes < TAPS - 1, 0.0, part.astype(F32)).astype(BF16)
        part = jnp.dot(part, table[...], preferred_element_type=F32)
        packed = jnp.where(lanes // KEEP == b, part, packed)
    packed = jnp.where(lax.axis_index("core") == 1, pltpu.roll(packed, BLOCK // 2, 1), packed)
    high = packed.astype(BF16)
    low = jnp.where(lanes % (BLOCK // 2) < KEEP, packed - high.astype(F32), 0.0)
    rest = low[:EDGE]
    for g in range(1, 4):
        rest = rest + pltpu.roll(low[g * EDGE : (g + 1) * EDGE], g * KEEP, 1)
    rest = rest.astype(BF16)
    block_out[:64] = high
    block_out[64 : 64 + EDGE] = edges
    block_out[64 + EDGE :] = rest
    moves[4].start()
    moves[3].wait()
    moves[4].wait()


def spread_kernel(mine, other, out):
    first = lax.axis_index("z_lo") == 0
    lower = jnp.where(first, mine[...], other[...])
    upper = jnp.where(first, other[...], mine[...])
    for k in range(out.shape[0]):
        out[k, 0] = lower
        out[k, 1] = upper


def join_kernel(mine, near, out):
    out[:64] = mine[...]
    out[64:] = near[...]


def query_kernel(q, own, swap, hop, taps, out):
    place = lax.axis_index(CTX)
    odd = place % 2 == 1
    own, swap, hop = own[...].astype(F32), swap[...].astype(F32), hop[...].astype(F32)
    lower = jnp.where(odd, swap[0], hop[0])
    lower = jnp.where(place == 0, jnp.zeros_like(lower), lower)
    upper = jnp.where(odd, hop[1], swap[1])
    upper = jnp.where(place == 15, own[0], upper)
    for half, halo in enumerate((lower, upper)):
        for b in range(SPAN // BLOCK):
            start = half * SPAN + b * BLOCK
            values = q[start : start + BLOCK].astype(F32)
            if b:
                halo = q[start - EDGE : start].astype(F32)
            padded = jnp.concatenate([halo, values], 0)
            total = taps[0:1] * values
            for w in range(1, TAPS):
                total = total + taps[w : w + 1] * pltpu.roll(padded, w, 0)[EDGE:]
            out[start : start + BLOCK] = total.astype(BF16)


def pairs_kernel(mine, near, far, pairs):
    member = lax.axis_index(GROUP)
    pairs[member] = mine[...]
    pairs[member ^ 1] = near[...]
    pairs[member ^ 2] = far[:64]
    pairs[member ^ 3] = far[64:]


def slot(m):
    return m % 2 * 2 + m // 2


def attend_kernel(q, pairs, far_own, far_other, table, gain, out, packed, scores, ends):
    place = lax.axis_index(CTX)
    middle = place // 2
    odd = place % 2 == 1
    factor = math.log2(math.e) / math.sqrt(HEAD_CHANNELS)
    lane = lax.broadcasted_iota(jnp.int32, (BLOCK, BLOCK), 1)
    row = lax.broadcasted_iota(jnp.int32, (BLOCK, BLOCK), 0)
    edge_lane = lax.broadcasted_iota(jnp.int32, (8, BLOCK), 1) < BLOCK // 2
    edge_row = lax.broadcasted_iota(jnp.int32, (8, BLOCK), 0)
    tile_lane = lax.broadcasted_iota(jnp.int32, (64, BLOCK), 1)
    own_lane = jnp.where(tile_lane < BLOCK // 2, 1, 0) != jnp.where(odd, 1, 0)
    first_lane = lax.broadcasted_iota(jnp.int32, (EDGE, BLOCK), 1) % (BLOCK // 2) < KEEP

    def turned(value):
        return pltpu.roll(value, BLOCK // 2, 1)

    def edges_of(owner, m):
        mine = far_own[owner // 2, slot(m), 64 : 64 + EDGE]
        other = far_other[owner // 2, slot(m), 64 : 64 + EDGE]
        tile = jnp.where(odd, other, mine) if owner % 2 == 0 else jnp.where(odd, mine, other)
        tile = tile.astype(F32)
        return tile[:8] + tile[8:]

    def whole_tile(ref, i, m):
        rest = ref[i, m, 64 + EDGE :].astype(F32)
        parts = [rest] + [pltpu.roll(rest, BLOCK - g * KEEP, 1) for g in range(1, 4)]
        parts = [jnp.where(first_lane, part, 0.0) for part in parts]
        return ref[i, m, :64].astype(F32) + jnp.concatenate(parts, 0)

    first_rows = []
    for kind in range(2):
        heads, tails = [], []
        for owner in range(16):
            left, right = edges_of(owner, 2 * kind), edges_of(owner, 2 * kind + 1)
            heads.append(jnp.where(edge_lane, left, right))
            tails.append(turned(jnp.where(edge_lane, right, left)))
        for owner in range(16):
            below = tails[owner - 1] if owner else jnp.zeros((8, BLOCK), F32)
            above = tails[owner + 1] if owner < 15 else pltpu.roll(tails[15], 3, 0)
            ends[kind, owner] = heads[owner] + jnp.where(edge_row < 3, below, above)
        both = jnp.transpose(ends[kind].reshape(128, HEAD_CHANNELS)).astype(BF16)
        fix = jnp.dot(both, table[...], preferred_element_type=F32)
        for i in range(8):
            for m in range(2):
                rows = slice(64 * m, 64 * (m + 1))
                mine = whole_tile(far_own, i, slot(2 * kind + m))
                other = whole_tile(far_other, i, slot(2 * kind + m))
                low = jnp.where(own_lane, mine, other) + fix[rows, i * BLOCK : (i + 1) * BLOCK]
                high = jnp.where(own_lane, other, mine)
                high = high + fix[rows, (8 + i) * BLOCK : (9 + i) * BLOCK]
                packed[kind, 0, i, rows] = low.astype(BF16)
                packed[kind, 1, i, rows] = high.astype(BF16)
        pick = (
            (edge_row < 3)
            & (lax.broadcasted_iota(jnp.int32, (8, BLOCK), 1) == edge_row)
        ) | (
            (edge_row >= 3)
            & (edge_row < 6)
            & (lax.broadcasted_iota(jnp.int32, (8, BLOCK), 1) == edge_row - 3 + BLOCK // 2)
        )
        first_rows.append(
            lax.dot_general(
                ends[kind, place].astype(BF16),
                jnp.where(pick, 1.0, 0.0).astype(BF16),
                TN,
                preferred_element_type=F32,
            )
        )

    def near_tile(kind, start):
        tile = jnp.concatenate(
            [pairs[2 * kind, :, start : start + BLOCK], pairs[2 * kind + 1, :, start : start + BLOCK]], 0
        )
        if start % SPAN == 0:
            first = first_rows[kind] if start == 0 else turned(first_rows[kind])
            tile = jnp.where(lane < TAPS - 1, first, tile.astype(F32)).astype(BF16)
        return tile

    key_block = (lax.broadcasted_iota(jnp.int32, (1, BLOCK), 1) % (BLOCK // 2)) // KEEP
    left_lanes = lax.broadcasted_iota(jnp.int32, (1, BLOCK), 1) < BLOCK // 2
    per_chunk = CHUNK // BLOCK
    for r in range(SPAN // CHUNK):
        tops = [jnp.full((CHUNK, BLOCK), NEGATIVE, F32) for _ in range(2)]
        for half in range(2):
            tiles = []
            for c in range(per_chunk):
                start = half * SPAN + r * CHUNK + c * BLOCK
                near = jnp.dot(
                    q[start : start + BLOCK], near_tile(0, start), preferred_element_type=F32
                )
                tiles.append(jnp.where(row >= lane, near, NEGATIVE))
            tops[half] = jnp.concatenate(tiles, 0)
            scores[17 + half] = tops[half]
        upper = q[SPAN + r * CHUNK : SPAN + (r + 1) * CHUNK]
        for i in range(4):
            far = jnp.dot(
                upper,
                jnp.concatenate([packed[0, 0, 2 * i], packed[0, 0, 2 * i + 1]], 1),
                preferred_element_type=F32,
            )
            scores[9 + 2 * i] = far[:, :BLOCK]
            scores[10 + 2 * i] = far[:, BLOCK:]
            tops[1] = jnp.maximum(tops[1], jnp.maximum(far[:, :BLOCK], far[:, BLOCK:]))
        for j in range(9):
            high = j > middle
            side = high.astype(jnp.int32)
            partial = (j == middle) | (j == middle + 1)
            start = pl.multiple_of(side * SPAN + r * CHUNK, CHUNK)
            far = jnp.dot(
                q[pl.ds(start, CHUNK)], packed[0, side, j - side], preferred_element_type=F32
            )
            biases = []
            for c in range(per_chunk):
                block = r * per_chunk + c
                left = jnp.where(high, jnp.where(odd, block, 4), jnp.where(odd, 4, block))
                right = jnp.where(high, jnp.where(odd, 0, block), jnp.where(odd, block, 0))
                left, right = jnp.where(partial, left, 4), jnp.where(partial, right, 4)
                seen = key_block < jnp.where(left_lanes, left, right)
                biases.append(
                    jnp.broadcast_to(jnp.where(seen, 0.0, NEGATIVE), (BLOCK, BLOCK))
                )
            far = far + jnp.concatenate(biases, 0)
            scores[j] = far
            tops[0] = jnp.maximum(tops[0], jnp.where(high, NEGATIVE, far))
            tops[1] = jnp.maximum(tops[1], jnp.where(high, far, NEGATIVE))
        tops = [
            jnp.broadcast_to(jnp.max(t, 1, keepdims=True) * factor, (CHUNK, BLOCK)) for t in tops
        ]
        totals, sums = [], []
        for half in range(2):
            weights = jnp.exp2(scores[17 + half] * factor - tops[half])
            totals.append(weights)
            weights = weights.astype(BF16)
            sums.append(
                jnp.concatenate(
                    [
                        lax.dot_general(
                            weights[c * BLOCK : (c + 1) * BLOCK],
                            near_tile(1, half * SPAN + r * CHUNK + c * BLOCK),
                            NT,
                            preferred_element_type=F32,
                        )
                        for c in range(per_chunk)
                    ],
                    0,
                )
            )
        for i in range(4):
            first = jnp.exp2(scores[9 + 2 * i] * factor - tops[1])
            second = jnp.exp2(scores[10 + 2 * i] * factor - tops[1])
            totals[1] = totals[1] + first + second
            sums[1] = sums[1] + lax.dot_general(
                jnp.concatenate([first, second], 1).astype(BF16),
                jnp.concatenate([packed[1, 0, 2 * i], packed[1, 0, 2 * i + 1]], 1),
                NT,
                preferred_element_type=F32,
            )
        for j in range(9):
            high = j > middle
            side = high.astype(jnp.int32)
            weights = jnp.exp2(scores[j] * factor - jnp.where(high, tops[1], tops[0]))
            totals[0] = totals[0] + jnp.where(high, 0.0, weights)
            totals[1] = totals[1] + jnp.where(high, weights, 0.0)
            part = lax.dot_general(
                weights.astype(BF16), packed[1, side, j - side], NT, preferred_element_type=F32
            )
            sums[0] = sums[0] + jnp.where(high, 0.0, part)
            sums[1] = sums[1] + jnp.where(high, part, 0.0)
        for half in range(2):
            attended = sums[half] / jnp.sum(totals[half], 1, keepdims=True)
            mean = jnp.mean(attended * attended, 1, keepdims=True)
            normed = attended * lax.rsqrt(mean + EPSILON)
            start = half * SPAN + r * CHUNK
            out[start : start + CHUNK] = (normed * gain[...]).astype(BF16)


def cost(flops, moved):
    return pl.CostEstimate(flops=flops, bytes_accessed=moved, transcendentals=0)


def swapped(value, axis):
    return lax.ppermute(value, axis, [(0, 1), (1, 0)])


def per_device(queries, keys_values, query_taps, pair_taps, out_gain):
    def call(kernel, name, out_shape, operands, spaces=None, scratch=(), flops=1 << 24):
        many = isinstance(out_shape, tuple)
        return pl.pallas_call(
            kernel,
            out_shape=out_shape,
            in_specs=[spec(s) for s in spaces] if spaces else [spec()] * len(operands),
            out_specs=(spec(),) * len(out_shape) if many else spec(),
            scratch_shapes=scratch,
            compiler_params=pltpu.CompilerParams(vmem_limit_bytes=24 << 20),
            cost_estimate=cost(flops, 1 << 20),
            name=name,
        )(*operands)

    def shape(*dims):
        return jax.ShapeDtypeStruct(dims, BF16)

    conv, block = pl.pallas_call(
        conv_kernel,
        out_shape=(shape(64, ROWS), shape(SENT, BLOCK)),
        in_specs=[spec(pl.ANY)] * 3,
        out_specs=(spec(pl.ANY), spec(pl.ANY)),
        scratch_shapes=[
            VMEM((64, ROWS), BF16),
            VMEM((TAPS, 64), F32),
            VMEM((BLOCK, BLOCK), BF16),
            VMEM((64, ROWS), BF16),
            VMEM((SENT, BLOCK), BF16),
            pltpu.SemaphoreType.DMA((5,)),
        ],
        compiler_params=pltpu.CompilerParams(vmem_limit_bytes=56 << 20),
        cost_estimate=cost(1 << 24, 1 << 20),
        name="conv",
    )(keys_values.T, pair_taps, jnp.asarray(dct_tile()))
    blocks = call(
        spread_kernel, "spread", shape(16, 2, SENT, BLOCK), (block, swapped(block, "z_lo"))
    )
    gathered = lax.all_to_all(blocks, CHIPS + ("y_hi",), 0, 0, tiled=True)
    near = swapped(conv, "y_hi")
    far = call(join_kernel, "join", shape(128, ROWS), (conv, near), flops=1 << 37)
    far = swapped(far, "z_lo")
    tails = jnp.stack([queries[e - EDGE : e] for e in (SPAN, ROWS)])
    swap = swapped(tails, "core")
    hop = lax.ppermute(
        tails, CTX, [(i, i + 1) for i in range(1, 15, 2)] + [(i + 1, i) for i in range(1, 15, 2)]
    )
    query_conv = call(
        query_kernel,
        "queries",
        shape(ROWS, HEAD_CHANNELS),
        (queries, tails, swap, hop, query_taps),
    )
    gathered, query_conv = lax.optimization_barrier((gathered, query_conv))
    far_own = gathered.reshape(8, 4, SENT, BLOCK)
    far_other = swapped(far_own, "core")
    pairs = call(pairs_kernel, "pairs", shape(4, 64, ROWS), (conv, near, far), flops=1 << 37)
    return call(
        attend_kernel,
        "attend",
        shape(ROWS, HEAD_CHANNELS),
        (query_conv, pairs, far_own, far_other, jnp.asarray(head_tables()), out_gain.reshape(1, -1)),
        scratch=[
            VMEM((2, 2, 8, HEAD_CHANNELS, BLOCK), BF16),
            VMEM((19, CHUNK, BLOCK), F32),
            VMEM((2, 16, 8, HEAD_CHANNELS), F32),
        ],
        flops=1 << 30,
    )


def solution(mesh):
    fine = Mesh(mesh.devices.reshape(2, 4, 2, 8, 2, 2), CTX + MP)
    in_specs = (P(CTX, MP), P(CTX, MP), P(None, MP), P(None, MP), P(MP))
    return jax.shard_map(
        per_device, mesh=fine, in_specs=in_specs, out_specs=P(CTX, MP), check_vma=False
    )
```

```python
import functools
import math

import jax
import jax.numpy as jnp
import numpy as np
from jax import lax
from jax.experimental import pallas as pl
from jax.experimental.pallas import tpu as pltpu
from jax.sharding import Mesh, PartitionSpec as P

HEAD_CHANNELS = 128
TAPS = 4
BLOCK = 128
KEEP = 16
SPAN = 512
ROWS = 2 * SPAN
NEGATIVE = -1e30
EPSILON = 1e-06
EDGE = 16
SENT = 64 + 2 * EDGE
CHUNK = 256

CTX = ("y_lo", "x", "core")
MP = ("z_hi", "z_lo", "y_hi")
GROUP = ("z_lo", "y_hi")
CHIPS = ("y_lo", "x")

VMEM = pltpu.VMEM
SMEM = pltpu.SMEM
F32 = jnp.float32
BF16 = jnp.bfloat16
NT = (((1,), (1,)), ((), ()))
TN = (((0,), (0,)), ((), ()))


def spec(space=VMEM):
    return pl.BlockSpec(memory_space=space)


def dct_table():
    j = np.arange(KEEP, dtype=np.float32)[:, None]
    u = np.arange(BLOCK, dtype=np.float32)[None, :]
    table = np.cos(np.float32(math.pi) * (u + np.float32(0.5)) * j / np.float32(BLOCK))
    table = table * np.float32(math.sqrt(2.0 / BLOCK))
    table = np.where(j == 0, table * np.float32(math.sqrt(0.5)), table)
    return table.astype(jnp.bfloat16)


def dct_tile():
    return np.tile(dct_table().T, (1, BLOCK // KEEP))


def head_tables():
    table = dct_table()
    whole = np.zeros((16, 8, 2, 8, BLOCK), table.dtype)
    half = BLOCK // 2
    for owner in range(16):
        for t in range(TAPS - 1):
            low, high = (0, half) if owner % 2 == 0 else (half, 0)
            whole[owner, t, 0, owner // 2, low : low + KEEP] = table[:, t]
            whole[owner, 3 + t, 1, owner // 2, high : high + KEEP] = table[:, t]
    return whole.reshape(128, 16 * BLOCK)


def conv_kernel(
    kv_in, taps_in, table_in, conv_result, block_result, kv, taps, table, conv_out, block_out, sems
):
    moves = [(kv_in, kv), (taps_in, taps), (table_in, table)]
    moves += [(conv_out, conv_result), (block_out, block_result)]
    moves = [pltpu.make_async_copy(*move, sems.at[k]) for k, move in enumerate(moves)]
    for move in moves[:3]:
        move.start()
    for move in moves[:3]:
        move.wait()
    lanes = lax.broadcasted_iota(jnp.int32, (64, BLOCK), 1)
    turned = jnp.transpose(
        jnp.concatenate(
            [
                jnp.concatenate([taps[...], jnp.zeros((4, 64), F32)], 0),
                jnp.zeros((8, 64), F32),
            ],
            1,
        )
    )[:64]
    heads, tails = [], []
    for half in range(2):
        values = kv[:, half * SPAN : (half + 1) * SPAN].astype(F32)
        padded = jnp.concatenate([values, jnp.zeros((64, BLOCK), F32)], 1)
        total = turned[:, 0:1] * padded
        for w in range(1, TAPS):
            total = total + turned[:, w : w + 1] * pltpu.roll(padded, w, 1)
        conv_out[:, half * SPAN : (half + 1) * SPAN] = total[:, :SPAN].astype(BF16)
        if half:
            moves[3].start()
        heads.append(total[:, :BLOCK])
        tails.append(total[:, SPAN:])

    def join(pair):
        upper = pltpu.roll(pair[1], 3, 1)
        return jnp.where(lanes < 3, pair[0], jnp.where(lanes < 6, upper, 0.0))

    heads, tails = join(heads), join(tails)
    uneven = lax.axis_index("y_hi") == 1
    edges = jnp.concatenate([jnp.where(uneven, tails, heads), jnp.where(uneven, heads, tails)], 0)
    edges = jnp.transpose(edges)[:8]
    high = edges.astype(BF16)
    low = edges - high.astype(F32)
    edges = jnp.concatenate([high.astype(F32), low], 0).astype(BF16)
    packed = jnp.zeros((64, BLOCK), F32)
    for b in range(ROWS // BLOCK):
        part = conv_out[:, b * BLOCK : (b + 1) * BLOCK]
        if b * BLOCK % SPAN == 0:
            part = jnp.where(lanes < TAPS - 1, 0.0, part.astype(F32)).astype(BF16)
        part = jnp.dot(part, table[...], preferred_element_type=F32)
        packed = jnp.where(lanes // KEEP == b, part, packed)
    packed = jnp.where(lax.axis_index("core") == 1, pltpu.roll(packed, BLOCK // 2, 1), packed)
    high = packed.astype(BF16)
    low = jnp.where(lanes % (BLOCK // 2) < KEEP, packed - high.astype(F32), 0.0)
    rest = low[:EDGE]
    for g in range(1, 4):
        rest = rest + pltpu.roll(low[g * EDGE : (g + 1) * EDGE], g * KEEP, 1)
    rest = rest.astype(BF16)
    block_out[:64] = high
    block_out[64 : 64 + EDGE] = edges
    block_out[64 + EDGE :] = rest
    moves[4].start()
    moves[3].wait()
    moves[4].wait()


def spread_kernel(mine, other, out, sems):
    place = lax.axis_index("z_lo")
    copies = []
    for k in range(out.shape[0]):
        copies.append(pltpu.make_async_copy(mine, out.at[k, place], sems.at[k, 0]))
        copies.append(pltpu.make_async_copy(other, out.at[k, 1 - place], sems.at[k, 1]))
    for copy in copies:
        copy.start()
    for copy in copies:
        copy.wait()


def join_kernel(mine, near, out):
    out[:64] = mine[...]
    out[64:] = near[...]


def query_kernel(q, own, swap, hop, taps, out):
    place = lax.axis_index(CTX)
    odd = place % 2 == 1
    own, swap, hop = own[...].astype(F32), swap[...].astype(F32), hop[...].astype(F32)
    lower = jnp.where(odd, swap[0], hop[0])
    lower = jnp.where(place == 0, jnp.zeros_like(lower), lower)
    upper = jnp.where(odd, hop[1], swap[1])
    upper = jnp.where(place == 15, own[0], upper)
    for half, halo in enumerate((lower, upper)):
        for b in range(SPAN // BLOCK):
            start = half * SPAN + b * BLOCK
            values = q[start : start + BLOCK].astype(F32)
            if b:
                halo = q[start - EDGE : start].astype(F32)
            padded = jnp.concatenate([halo, values], 0)
            total = taps[0:1] * values
            for w in range(1, TAPS):
                total = total + taps[w : w + 1] * pltpu.roll(padded, w, 0)[EDGE:]
            out[start : start + BLOCK] = total.astype(BF16)


def pairs_kernel(mine, near, far, pairs):
    member = lax.axis_index(GROUP)
    pairs[member] = mine[...]
    pairs[member ^ 1] = near[...]
    pairs[member ^ 2] = far[:64]
    pairs[member ^ 3] = far[64:]


def slot(m):
    return m % 2 * 2 + m // 2


def attend_kernel(q, pairs, far_own, far_other, table, gain, out, packed, scores, ends):
    place = lax.axis_index(CTX)
    middle = place // 2
    odd = place % 2 == 1
    factor = math.log2(math.e) / math.sqrt(HEAD_CHANNELS)
    lane = lax.broadcasted_iota(jnp.int32, (BLOCK, BLOCK), 1)
    row = lax.broadcasted_iota(jnp.int32, (BLOCK, BLOCK), 0)
    edge_lane = lax.broadcasted_iota(jnp.int32, (8, BLOCK), 1) < BLOCK // 2
    edge_row = lax.broadcasted_iota(jnp.int32, (8, BLOCK), 0)
    tile_lane = lax.broadcasted_iota(jnp.int32, (64, BLOCK), 1)
    own_lane = jnp.where(tile_lane < BLOCK // 2, 1, 0) != jnp.where(odd, 1, 0)
    first_lane = lax.broadcasted_iota(jnp.int32, (EDGE, BLOCK), 1) % (BLOCK // 2) < KEEP

    def turned(value):
        return pltpu.roll(value, BLOCK // 2, 1)

    def edges_of(owner, m):
        mine = far_own[owner // 2, slot(m), 64 : 64 + EDGE]
        other = far_other[owner // 2, slot(m), 64 : 64 + EDGE]
        tile = jnp.where(odd, other, mine) if owner % 2 == 0 else jnp.where(odd, mine, other)
        tile = tile.astype(F32)
        return tile[:8] + tile[8:]

    def whole_tile(ref, i, m):
        rest = ref[i, m, 64 + EDGE :].astype(F32)
        parts = [rest] + [pltpu.roll(rest, BLOCK - g * KEEP, 1) for g in range(1, 4)]
        parts = [jnp.where(first_lane, part, 0.0) for part in parts]
        return ref[i, m, :64].astype(F32) + jnp.concatenate(parts, 0)

    first_rows = []
    for kind in range(2):
        heads, tails = [], []
        for owner in range(16):
            left, right = edges_of(owner, 2 * kind), edges_of(owner, 2 * kind + 1)
            heads.append(jnp.where(edge_lane, left, right))
            tails.append(turned(jnp.where(edge_lane, right, left)))
        for owner in range(16):
            below = tails[owner - 1] if owner else jnp.zeros((8, BLOCK), F32)
            above = tails[owner + 1] if owner < 15 else pltpu.roll(tails[15], 3, 0)
            ends[kind, owner] = heads[owner] + jnp.where(edge_row < 3, below, above)
        both = jnp.transpose(ends[kind].reshape(128, HEAD_CHANNELS)).astype(BF16)
        fix = jnp.dot(both, table[...], preferred_element_type=F32)
        for i in range(8):
            for m in range(2):
                rows = slice(64 * m, 64 * (m + 1))
                mine = whole_tile(far_own, i, slot(2 * kind + m))
                other = whole_tile(far_other, i, slot(2 * kind + m))
                low = jnp.where(own_lane, mine, other) + fix[rows, i * BLOCK : (i + 1) * BLOCK]
                high = jnp.where(own_lane, other, mine)
                high = high + fix[rows, (8 + i) * BLOCK : (9 + i) * BLOCK]
                packed[kind, 0, i, rows] = low.astype(BF16)
                packed[kind, 1, i, rows] = high.astype(BF16)
        pick = (
            (edge_row < 3)
            & (lax.broadcasted_iota(jnp.int32, (8, BLOCK), 1) == edge_row)
        ) | (
            (edge_row >= 3)
            & (edge_row < 6)
            & (lax.broadcasted_iota(jnp.int32, (8, BLOCK), 1) == edge_row - 3 + BLOCK // 2)
        )
        first_rows.append(
            lax.dot_general(
                ends[kind, place].astype(BF16),
                jnp.where(pick, 1.0, 0.0).astype(BF16),
                TN,
                preferred_element_type=F32,
            )
        )

    def near_tile(kind, start):
        tile = jnp.concatenate(
            [pairs[2 * kind, :, start : start + BLOCK], pairs[2 * kind + 1, :, start : start + BLOCK]], 0
        )
        if start % SPAN == 0:
            first = first_rows[kind] if start == 0 else turned(first_rows[kind])
            tile = jnp.where(lane < TAPS - 1, first, tile.astype(F32)).astype(BF16)
        return tile

    key_block = (lax.broadcasted_iota(jnp.int32, (1, BLOCK), 1) % (BLOCK // 2)) // KEEP
    left_lanes = lax.broadcasted_iota(jnp.int32, (1, BLOCK), 1) < BLOCK // 2
    per_chunk = CHUNK // BLOCK
    for r in range(SPAN // CHUNK):
        tops = [jnp.full((CHUNK, BLOCK), NEGATIVE, F32) for _ in range(2)]
        for half in range(2):
            tiles = []
            for c in range(per_chunk):
                start = half * SPAN + r * CHUNK + c * BLOCK
                near = jnp.dot(
                    q[start : start + BLOCK], near_tile(0, start), preferred_element_type=F32
                )
                tiles.append(jnp.where(row >= lane, near, NEGATIVE))
            tops[half] = jnp.concatenate(tiles, 0)
            scores[17 + half] = tops[half]
        upper = q[SPAN + r * CHUNK : SPAN + (r + 1) * CHUNK]
        for i in range(4):
            far = jnp.dot(
                upper,
                jnp.concatenate([packed[0, 0, 2 * i], packed[0, 0, 2 * i + 1]], 1),
                preferred_element_type=F32,
            )
            scores[9 + 2 * i] = far[:, :BLOCK]
            scores[10 + 2 * i] = far[:, BLOCK:]
            tops[1] = jnp.maximum(tops[1], jnp.maximum(far[:, :BLOCK], far[:, BLOCK:]))
        for j in range(9):
            high = j > middle
            side = high.astype(jnp.int32)
            partial = (j == middle) | (j == middle + 1)
            start = pl.multiple_of(side * SPAN + r * CHUNK, CHUNK)
            far = jnp.dot(
                q[pl.ds(start, CHUNK)], packed[0, side, j - side], preferred_element_type=F32
            )
            biases = []
            for c in range(per_chunk):
                block = r * per_chunk + c
                left = jnp.where(high, jnp.where(odd, block, 4), jnp.where(odd, 4, block))
                right = jnp.where(high, jnp.where(odd, 0, block), jnp.where(odd, block, 0))
                left, right = jnp.where(partial, left, 4), jnp.where(partial, right, 4)
                seen = key_block < jnp.where(left_lanes, left, right)
                biases.append(
                    jnp.broadcast_to(jnp.where(seen, 0.0, NEGATIVE), (BLOCK, BLOCK))
                )
            far = far + jnp.concatenate(biases, 0)
            scores[j] = far
            tops[0] = jnp.maximum(tops[0], jnp.where(high, NEGATIVE, far))
            tops[1] = jnp.maximum(tops[1], jnp.where(high, far, NEGATIVE))
        tops = [
            jnp.broadcast_to(jnp.max(t, 1, keepdims=True) * factor, (CHUNK, BLOCK)) for t in tops
        ]
        totals, sums = [], []
        for half in range(2):
            weights = jnp.exp2(scores[17 + half] * factor - tops[half])
            totals.append(weights)
            weights = weights.astype(BF16)
            sums.append(
                jnp.concatenate(
                    [
                        lax.dot_general(
                            weights[c * BLOCK : (c + 1) * BLOCK],
                            near_tile(1, half * SPAN + r * CHUNK + c * BLOCK),
                            NT,
                            preferred_element_type=F32,
                        )
                        for c in range(per_chunk)
                    ],
                    0,
                )
            )
        for i in range(4):
            first = jnp.exp2(scores[9 + 2 * i] * factor - tops[1])
            second = jnp.exp2(scores[10 + 2 * i] * factor - tops[1])
            totals[1] = totals[1] + first + second
            sums[1] = sums[1] + lax.dot_general(
                jnp.concatenate([first, second], 1).astype(BF16),
                jnp.concatenate([packed[1, 0, 2 * i], packed[1, 0, 2 * i + 1]], 1),
                NT,
                preferred_element_type=F32,
            )
        for j in range(9):
            high = j > middle
            side = high.astype(jnp.int32)
            weights = jnp.exp2(scores[j] * factor - jnp.where(high, tops[1], tops[0]))
            totals[0] = totals[0] + jnp.where(high, 0.0, weights)
            totals[1] = totals[1] + jnp.where(high, weights, 0.0)
            part = lax.dot_general(
                weights.astype(BF16), packed[1, side, j - side], NT, preferred_element_type=F32
            )
            sums[0] = sums[0] + jnp.where(high, 0.0, part)
            sums[1] = sums[1] + jnp.where(high, part, 0.0)
        for half in range(2):
            attended = sums[half] / jnp.sum(totals[half], 1, keepdims=True)
            mean = jnp.mean(attended * attended, 1, keepdims=True)
            normed = attended * lax.rsqrt(mean + EPSILON)
            start = half * SPAN + r * CHUNK
            out[start : start + CHUNK] = (normed * gain[...]).astype(BF16)


def cost(flops, moved):
    return pl.CostEstimate(flops=flops, bytes_accessed=moved, transcendentals=0)


def swapped(value, axis):
    return lax.ppermute(value, axis, [(0, 1), (1, 0)])


def per_device(queries, keys_values, query_taps, pair_taps, out_gain):
    def call(kernel, name, out_shape, operands, spaces=None, scratch=(), flops=1 << 24):
        many = isinstance(out_shape, tuple)
        return pl.pallas_call(
            kernel,
            out_shape=out_shape,
            in_specs=[spec(s) for s in spaces] if spaces else [spec()] * len(operands),
            out_specs=(spec(),) * len(out_shape) if many else spec(),
            scratch_shapes=scratch,
            compiler_params=pltpu.CompilerParams(vmem_limit_bytes=24 << 20),
            cost_estimate=cost(flops, 1 << 20),
            name=name,
        )(*operands)

    def shape(*dims):
        return jax.ShapeDtypeStruct(dims, BF16)

    conv, block = pl.pallas_call(
        conv_kernel,
        out_shape=(shape(64, ROWS), shape(SENT, BLOCK)),
        in_specs=[spec(pl.ANY)] * 3,
        out_specs=(spec(pl.ANY), spec(pl.ANY)),
        scratch_shapes=[
            VMEM((64, ROWS), BF16),
            VMEM((TAPS, 64), F32),
            VMEM((BLOCK, BLOCK), BF16),
            VMEM((64, ROWS), BF16),
            VMEM((SENT, BLOCK), BF16),
            pltpu.SemaphoreType.DMA((5,)),
        ],
        compiler_params=pltpu.CompilerParams(vmem_limit_bytes=56 << 20),
        cost_estimate=cost(1 << 24, 1 << 20),
        name="conv",
    )(keys_values.T, pair_taps, jnp.asarray(dct_tile()))
    blocks = pl.pallas_call(
        spread_kernel,
        out_shape=shape(16, 2, SENT, BLOCK),
        in_specs=[spec(pl.ANY)] * 2,
        out_specs=spec(pl.ANY),
        scratch_shapes=[pltpu.SemaphoreType.DMA((16, 2))],
        compiler_params=pltpu.CompilerParams(vmem_limit_bytes=56 << 20),
        cost_estimate=cost(1 << 37, 1 << 20),
        name="spread",
    )(block, swapped(block, "z_lo"))
    gathered = lax.all_to_all(blocks, CHIPS + ("y_hi",), 0, 0, tiled=True)
    near = swapped(conv, "y_hi")
    far = call(join_kernel, "join", shape(128, ROWS), (conv, near), flops=1 << 37)
    far = swapped(far, "z_lo")
    tails = jnp.stack([queries[e - EDGE : e] for e in (SPAN, ROWS)])
    swap = swapped(tails, "core")
    hop = lax.ppermute(
        tails, CTX, [(i, i + 1) for i in range(1, 15, 2)] + [(i + 1, i) for i in range(1, 15, 2)]
    )
    query_conv = call(
        query_kernel,
        "queries",
        shape(ROWS, HEAD_CHANNELS),
        (queries, tails, swap, hop, query_taps),
    )
    gathered, query_conv = lax.optimization_barrier((gathered, query_conv))
    far_own = gathered.reshape(8, 4, SENT, BLOCK)
    far_other = swapped(far_own, "core")
    pairs = call(pairs_kernel, "pairs", shape(4, 64, ROWS), (conv, near, far), flops=1 << 37)
    return call(
        attend_kernel,
        "attend",
        shape(ROWS, HEAD_CHANNELS),
        (query_conv, pairs, far_own, far_other, jnp.asarray(head_tables()), out_gain.reshape(1, -1)),
        scratch=[
            VMEM((2, 2, 8, HEAD_CHANNELS, BLOCK), BF16),
            VMEM((19, CHUNK, BLOCK), F32),
            VMEM((2, 16, 8, HEAD_CHANNELS), F32),
        ],
        flops=1 << 30,
    )


def solution(mesh):
    fine = Mesh(mesh.devices.reshape(2, 4, 2, 8, 2, 2), CTX + MP)
    in_specs = (P(CTX, MP), P(CTX, MP), P(None, MP), P(None, MP), P(MP))
    return jax.shard_map(
        per_device, mesh=fine, in_specs=in_specs, out_specs=P(CTX, MP), check_vma=False
    )
```

```python
import functools
import math

import jax
import jax.numpy as jnp
import numpy as np
from jax import lax
from jax.experimental import pallas as pl
from jax.experimental.pallas import tpu as pltpu
from jax.sharding import Mesh, PartitionSpec as P

HEAD_CHANNELS = 128
TAPS = 4
BLOCK = 128
KEEP = 16
SPAN = 512
ROWS = 2 * SPAN
NEGATIVE = -1e30
EPSILON = 1e-06
EDGE = 16
SENT = 64 + 2 * EDGE
CHUNK = 256

CTX = ("y_lo", "x", "core")
MP = ("z_hi", "z_lo", "y_hi")
GROUP = ("z_lo", "y_hi")
CHIPS = ("y_lo", "x")

VMEM = pltpu.VMEM
SMEM = pltpu.SMEM
F32 = jnp.float32
BF16 = jnp.bfloat16
NT = (((1,), (1,)), ((), ()))
TN = (((0,), (0,)), ((), ()))


def spec(space=VMEM):
    return pl.BlockSpec(memory_space=space)


def dct_table():
    j = np.arange(KEEP, dtype=np.float32)[:, None]
    u = np.arange(BLOCK, dtype=np.float32)[None, :]
    table = np.cos(np.float32(math.pi) * (u + np.float32(0.5)) * j / np.float32(BLOCK))
    table = table * np.float32(math.sqrt(2.0 / BLOCK))
    table = np.where(j == 0, table * np.float32(math.sqrt(0.5)), table)
    return table.astype(jnp.bfloat16)


def dct_tile():
    return np.tile(dct_table().T, (1, BLOCK // KEEP))


def head_tables():
    table = dct_table()
    whole = np.zeros((16, 8, 2, 8, BLOCK), table.dtype)
    half = BLOCK // 2
    for owner in range(16):
        for t in range(TAPS - 1):
            low, high = (0, half) if owner % 2 == 0 else (half, 0)
            whole[owner, t, 0, owner // 2, low : low + KEEP] = table[:, t]
            whole[owner, 3 + t, 1, owner // 2, high : high + KEEP] = table[:, t]
    return whole.reshape(128, 16 * BLOCK)


def conv_kernel(
    kv_in, taps_in, table_in, conv_result, block_result, kv, taps, table, conv_out, block_out, sems
):
    moves = [(kv_in, kv), (taps_in, taps), (table_in, table)]
    moves += [(conv_out, conv_result), (block_out, block_result)]
    moves = [pltpu.make_async_copy(*move, sems.at[k]) for k, move in enumerate(moves)]
    for move in moves[:3]:
        move.start()
    for move in moves[:3]:
        move.wait()
    lanes = lax.broadcasted_iota(jnp.int32, (64, BLOCK), 1)
    turned = jnp.transpose(
        jnp.concatenate(
            [
                jnp.concatenate([taps[...], jnp.zeros((4, 64), F32)], 0),
                jnp.zeros((8, 64), F32),
            ],
            1,
        )
    )[:64]
    heads, tails = [], []
    for half in range(2):
        values = kv[:, half * SPAN : (half + 1) * SPAN].astype(F32)
        padded = jnp.concatenate([values, jnp.zeros((64, BLOCK), F32)], 1)
        total = turned[:, 0:1] * padded
        for w in range(1, TAPS):
            total = total + turned[:, w : w + 1] * pltpu.roll(padded, w, 1)
        conv_out[:, half * SPAN : (half + 1) * SPAN] = total[:, :SPAN].astype(BF16)
        if half:
            moves[3].start()
        heads.append(total[:, :BLOCK])
        tails.append(total[:, SPAN:])

    def join(pair):
        upper = pltpu.roll(pair[1], 3, 1)
        return jnp.where(lanes < 3, pair[0], jnp.where(lanes < 6, upper, 0.0))

    heads, tails = join(heads), join(tails)
    uneven = lax.axis_index("y_hi") == 1
    edges = jnp.concatenate([jnp.where(uneven, tails, heads), jnp.where(uneven, heads, tails)], 0)
    edges = jnp.transpose(edges)[:8]
    high = edges.astype(BF16)
    low = edges - high.astype(F32)
    edges = jnp.concatenate([high.astype(F32), low], 0).astype(BF16)
    packed = jnp.zeros((64, BLOCK), F32)
    for b in range(ROWS // BLOCK):
        part = conv_out[:, b * BLOCK : (b + 1) * BLOCK]
        if b * BLOCK % SPAN == 0:
            part = jnp.where(lanes < TAPS - 1, 0.0, part.astype(F32)).astype(BF16)
        part = jnp.dot(part, table[...], preferred_element_type=F32)
        packed = jnp.where(lanes // KEEP == b, part, packed)
    packed = jnp.where(lax.axis_index("core") == 1, pltpu.roll(packed, BLOCK // 2, 1), packed)
    high = packed.astype(BF16)
    low = jnp.where(lanes % (BLOCK // 2) < KEEP, packed - high.astype(F32), 0.0)
    rest = low[:EDGE]
    for g in range(1, 4):
        rest = rest + pltpu.roll(low[g * EDGE : (g + 1) * EDGE], g * KEEP, 1)
    rest = rest.astype(BF16)
    for k in range(block_out.shape[0]):
        block_out[k, :64] = high
        block_out[k, 64 : 64 + EDGE] = edges
        block_out[k, 64 + EDGE :] = rest
    moves[4].start()
    moves[3].wait()
    moves[4].wait()


def tails_kernel(q, near, out):
    for half in range(2):
        out[half] = q[(half + 1) * SPAN - EDGE : (half + 1) * SPAN]


def join_kernel(mine, near, query_conv, out):
    out[:64] = mine[...]
    out[64:] = near[...]


def query_kernel(q, own, swap, hop, taps, out):
    place = lax.axis_index(CTX)
    odd = place % 2 == 1
    own, swap, hop = own[...].astype(F32), swap[...].astype(F32), hop[...].astype(F32)
    lower = jnp.where(odd, swap[0], hop[0])
    lower = jnp.where(place == 0, jnp.zeros_like(lower), lower)
    upper = jnp.where(odd, hop[1], swap[1])
    upper = jnp.where(place == 15, own[0], upper)
    for half, halo in enumerate((lower, upper)):
        for b in range(SPAN // BLOCK):
            start = half * SPAN + b * BLOCK
            values = q[start : start + BLOCK].astype(F32)
            if b:
                halo = q[start - EDGE : start].astype(F32)
            padded = jnp.concatenate([halo, values], 0)
            total = taps[0:1] * values
            for w in range(1, TAPS):
                total = total + taps[w : w + 1] * pltpu.roll(padded, w, 0)[EDGE:]
            out[start : start + BLOCK] = total.astype(BF16)


def pairs_kernel(mine, near, far, pairs):
    member = lax.axis_index(GROUP)
    pairs[member] = mine[...]
    pairs[member ^ 1] = near[...]
    pairs[member ^ 2] = far[:64]
    pairs[member ^ 3] = far[64:]


def attend_kernel(q, pairs, far_own, far_other, table, gain, out, packed, scores, ends):
    place = lax.axis_index(CTX)
    middle = place // 2
    odd = place % 2 == 1
    factor = math.log2(math.e) / math.sqrt(HEAD_CHANNELS)
    lane = lax.broadcasted_iota(jnp.int32, (BLOCK, BLOCK), 1)
    row = lax.broadcasted_iota(jnp.int32, (BLOCK, BLOCK), 0)
    edge_lane = lax.broadcasted_iota(jnp.int32, (8, BLOCK), 1) < BLOCK // 2
    edge_row = lax.broadcasted_iota(jnp.int32, (8, BLOCK), 0)
    tile_lane = lax.broadcasted_iota(jnp.int32, (64, BLOCK), 1)
    own_lane = jnp.where(tile_lane < BLOCK // 2, 1, 0) != jnp.where(odd, 1, 0)
    first_lane = lax.broadcasted_iota(jnp.int32, (EDGE, BLOCK), 1) % (BLOCK // 2) < KEEP

    def turned(value):
        return pltpu.roll(value, BLOCK // 2, 1)

    def edges_of(owner, m):
        mine = far_own[owner // 2, m, 64 : 64 + EDGE]
        other = far_other[owner // 2, m, 64 : 64 + EDGE]
        tile = jnp.where(odd, other, mine) if owner % 2 == 0 else jnp.where(odd, mine, other)
        tile = tile.astype(F32)
        return tile[:8] + tile[8:]

    def whole_tile(ref, i, m):
        rest = ref[i, m, 64 + EDGE :].astype(F32)
        parts = [rest] + [pltpu.roll(rest, BLOCK - g * KEEP, 1) for g in range(1, 4)]
        parts = [jnp.where(first_lane, part, 0.0) for part in parts]
        return ref[i, m, :64].astype(F32) + jnp.concatenate(parts, 0)

    first_rows = []
    for kind in range(2):
        heads, tails = [], []
        for owner in range(16):
            left, right = edges_of(owner, 2 * kind), edges_of(owner, 2 * kind + 1)
            heads.append(jnp.where(edge_lane, left, right))
            tails.append(turned(jnp.where(edge_lane, right, left)))
        for owner in range(16):
            below = tails[owner - 1] if owner else jnp.zeros((8, BLOCK), F32)
            above = tails[owner + 1] if owner < 15 else pltpu.roll(tails[15], 3, 0)
            ends[kind, owner] = heads[owner] + jnp.where(edge_row < 3, below, above)
        both = jnp.transpose(ends[kind].reshape(128, HEAD_CHANNELS)).astype(BF16)
        fix = jnp.dot(both, table[...], preferred_element_type=F32)
        for i in range(8):
            for m in range(2):
                rows = slice(64 * m, 64 * (m + 1))
                mine = whole_tile(far_own, i, 2 * kind + m)
                other = whole_tile(far_other, i, 2 * kind + m)
                low = jnp.where(own_lane, mine, other) + fix[rows, i * BLOCK : (i + 1) * BLOCK]
                high = jnp.where(own_lane, other, mine)
                high = high + fix[rows, (8 + i) * BLOCK : (9 + i) * BLOCK]
                packed[kind, 0, i, rows] = low.astype(BF16)
                packed[kind, 1, i, rows] = high.astype(BF16)
        pick = (
            (edge_row < 3)
            & (lax.broadcasted_iota(jnp.int32, (8, BLOCK), 1) == edge_row)
        ) | (
            (edge_row >= 3)
            & (edge_row < 6)
            & (lax.broadcasted_iota(jnp.int32, (8, BLOCK), 1) == edge_row - 3 + BLOCK // 2)
        )
        first_rows.append(
            lax.dot_general(
                ends[kind, place].astype(BF16),
                jnp.where(pick, 1.0, 0.0).astype(BF16),
                TN,
                preferred_element_type=F32,
            )
        )

    def near_tile(kind, start):
        tile = jnp.concatenate(
            [pairs[2 * kind, :, start : start + BLOCK], pairs[2 * kind + 1, :, start : start + BLOCK]], 0
        )
        if start % SPAN == 0:
            first = first_rows[kind] if start == 0 else turned(first_rows[kind])
            tile = jnp.where(lane < TAPS - 1, first, tile.astype(F32)).astype(BF16)
        return tile

    key_block = (lax.broadcasted_iota(jnp.int32, (1, BLOCK), 1) % (BLOCK // 2)) // KEEP
    left_lanes = lax.broadcasted_iota(jnp.int32, (1, BLOCK), 1) < BLOCK // 2
    per_chunk = CHUNK // BLOCK
    for r in range(SPAN // CHUNK):
        tops = [jnp.full((CHUNK, BLOCK), NEGATIVE, F32) for _ in range(2)]
        for half in range(2):
            tiles = []
            for c in range(per_chunk):
                start = half * SPAN + r * CHUNK + c * BLOCK
                near = jnp.dot(
                    q[start : start + BLOCK], near_tile(0, start), preferred_element_type=F32
                )
                tiles.append(jnp.where(row >= lane, near, NEGATIVE))
            tops[half] = jnp.concatenate(tiles, 0)
            scores[17 + half] = tops[half]
        upper = q[SPAN + r * CHUNK : SPAN + (r + 1) * CHUNK]
        for i in range(4):
            far = jnp.dot(
                upper,
                jnp.concatenate([packed[0, 0, 2 * i], packed[0, 0, 2 * i + 1]], 1),
                preferred_element_type=F32,
            )
            scores[9 + 2 * i] = far[:, :BLOCK]
            scores[10 + 2 * i] = far[:, BLOCK:]
            tops[1] = jnp.maximum(tops[1], jnp.maximum(far[:, :BLOCK], far[:, BLOCK:]))
        for j in range(9):
            high = j > middle
            side = high.astype(jnp.int32)
            partial = (j == middle) | (j == middle + 1)
            start = pl.multiple_of(side * SPAN + r * CHUNK, CHUNK)
            far = jnp.dot(
                q[pl.ds(start, CHUNK)], packed[0, side, j - side], preferred_element_type=F32
            )
            biases = []
            for c in range(per_chunk):
                block = r * per_chunk + c
                left = jnp.where(high, jnp.where(odd, block, 4), jnp.where(odd, 4, block))
                right = jnp.where(high, jnp.where(odd, 0, block), jnp.where(odd, block, 0))
                left, right = jnp.where(partial, left, 4), jnp.where(partial, right, 4)
                seen = key_block < jnp.where(left_lanes, left, right)
                biases.append(
                    jnp.broadcast_to(jnp.where(seen, 0.0, NEGATIVE), (BLOCK, BLOCK))
                )
            far = far + jnp.concatenate(biases, 0)
            scores[j] = far
            tops[0] = jnp.maximum(tops[0], jnp.where(high, NEGATIVE, far))
            tops[1] = jnp.maximum(tops[1], jnp.where(high, far, NEGATIVE))
        tops = [
            jnp.broadcast_to(jnp.max(t, 1, keepdims=True) * factor, (CHUNK, BLOCK)) for t in tops
        ]
        totals, sums = [], []
        for half in range(2):
            weights = jnp.exp2(scores[17 + half] * factor - tops[half])
            totals.append(weights)
            weights = weights.astype(BF16)
            sums.append(
                jnp.concatenate(
                    [
                        lax.dot_general(
                            weights[c * BLOCK : (c + 1) * BLOCK],
                            near_tile(1, half * SPAN + r * CHUNK + c * BLOCK),
                            NT,
                            preferred_element_type=F32,
                        )
                        for c in range(per_chunk)
                    ],
                    0,
                )
            )
        for i in range(4):
            first = jnp.exp2(scores[9 + 2 * i] * factor - tops[1])
            second = jnp.exp2(scores[10 + 2 * i] * factor - tops[1])
            totals[1] = totals[1] + first + second
            sums[1] = sums[1] + lax.dot_general(
                jnp.concatenate([first, second], 1).astype(BF16),
                jnp.concatenate([packed[1, 0, 2 * i], packed[1, 0, 2 * i + 1]], 1),
                NT,
                preferred_element_type=F32,
            )
        for j in range(9):
            high = j > middle
            side = high.astype(jnp.int32)
            weights = jnp.exp2(scores[j] * factor - jnp.where(high, tops[1], tops[0]))
            totals[0] = totals[0] + jnp.where(high, 0.0, weights)
            totals[1] = totals[1] + jnp.where(high, weights, 0.0)
            part = lax.dot_general(
                weights.astype(BF16), packed[1, side, j - side], NT, preferred_element_type=F32
            )
            sums[0] = sums[0] + jnp.where(high, 0.0, part)
            sums[1] = sums[1] + jnp.where(high, part, 0.0)
        for half in range(2):
            attended = sums[half] / jnp.sum(totals[half], 1, keepdims=True)
            mean = jnp.mean(attended * attended, 1, keepdims=True)
            normed = attended * lax.rsqrt(mean + EPSILON)
            start = half * SPAN + r * CHUNK
            out[start : start + CHUNK] = (normed * gain[...]).astype(BF16)


def cost(flops, moved):
    return pl.CostEstimate(flops=flops, bytes_accessed=moved, transcendentals=0)


def swapped(value, axis):
    return lax.ppermute(value, axis, [(0, 1), (1, 0)])


def per_device(queries, keys_values, query_taps, pair_taps, out_gain):
    def call(kernel, name, out_shape, operands, spaces=None, scratch=(), flops=1 << 24):
        many = isinstance(out_shape, tuple)
        return pl.pallas_call(
            kernel,
            out_shape=out_shape,
            in_specs=[spec(s) for s in spaces] if spaces else [spec()] * len(operands),
            out_specs=(spec(),) * len(out_shape) if many else spec(),
            scratch_shapes=scratch,
            compiler_params=pltpu.CompilerParams(vmem_limit_bytes=24 << 20),
            cost_estimate=cost(flops, 1 << 20),
            name=name,
        )(*operands)

    def shape(*dims):
        return jax.ShapeDtypeStruct(dims, BF16)

    conv, blocks = pl.pallas_call(
        conv_kernel,
        out_shape=(shape(64, ROWS), shape(32, SENT, BLOCK)),
        in_specs=[spec(pl.ANY)] * 3,
        out_specs=(spec(pl.ANY), spec(pl.ANY)),
        scratch_shapes=[
            VMEM((64, ROWS), BF16),
            VMEM((TAPS, 64), F32),
            VMEM((BLOCK, BLOCK), BF16),
            VMEM((64, ROWS), BF16),
            VMEM((32, SENT, BLOCK), BF16),
            pltpu.SemaphoreType.DMA((5,)),
        ],
        compiler_params=pltpu.CompilerParams(vmem_limit_bytes=56 << 20),
        cost_estimate=cost(1 << 24, 1 << 20),
        name="conv",
    )(keys_values.T, pair_taps, jnp.asarray(dct_tile()))
    gathered = lax.all_to_all(blocks, CHIPS + GROUP, 0, 0, tiled=True)
    near = swapped(conv, "y_hi")
    tails = call(
        tails_kernel,
        "tails",
        shape(2, EDGE, BLOCK),
        (queries, near),
        (VMEM, pl.ANY),
        flops=1 << 37,
    )
    swap = swapped(tails, "core")
    hop = lax.ppermute(
        tails, CTX, [(i, i + 1) for i in range(1, 15, 2)] + [(i + 1, i) for i in range(1, 15, 2)]
    )
    query_conv = call(
        query_kernel,
        "queries",
        shape(ROWS, HEAD_CHANNELS),
        (queries, tails, swap, hop, query_taps),
    )
    joined = call(
        join_kernel, "join", shape(128, ROWS), (conv, near, query_conv), (VMEM, VMEM, pl.ANY)
    )
    far = swapped(joined, "z_lo")
    gathered, query_conv = lax.optimization_barrier((gathered, query_conv))
    far_own = gathered.reshape(8, 4, SENT, BLOCK)
    far_other = swapped(far_own, "core")
    pairs = call(pairs_kernel, "pairs", shape(4, 64, ROWS), (conv, near, far), flops=1 << 37)
    return call(
        attend_kernel,
        "attend",
        shape(ROWS, HEAD_CHANNELS),
        (query_conv, pairs, far_own, far_other, jnp.asarray(head_tables()), out_gain.reshape(1, -1)),
        scratch=[
            VMEM((2, 2, 8, HEAD_CHANNELS, BLOCK), BF16),
            VMEM((19, CHUNK, BLOCK), F32),
            VMEM((2, 16, 8, HEAD_CHANNELS), F32),
        ],
        flops=1 << 30,
    )


def solution(mesh):
    fine = Mesh(mesh.devices.reshape(2, 4, 2, 8, 2, 2), CTX + MP)
    in_specs = (P(CTX, MP), P(CTX, MP), P(None, MP), P(None, MP), P(MP))
    return jax.shard_map(
        per_device, mesh=fine, in_specs=in_specs, out_specs=P(CTX, MP), check_vma=False
    )
```

```python
import functools
import math

import jax
import jax.numpy as jnp
import numpy as np
from jax import lax
from jax.experimental import pallas as pl
from jax.experimental.pallas import tpu as pltpu
from jax.sharding import Mesh, PartitionSpec as P

HEAD_CHANNELS = 128
TAPS = 4
BLOCK = 128
KEEP = 16
SPAN = 512
ROWS = 2 * SPAN
NEGATIVE = -1e30
EPSILON = 1e-06
EDGE = 16
SENT = 64 + 2 * EDGE
CHUNK = 256

CTX = ("y_lo", "x", "core")
MP = ("z_hi", "z_lo", "y_hi")
GROUP = ("z_lo", "y_hi")
CHIPS = ("y_lo", "x")

VMEM = pltpu.VMEM
SMEM = pltpu.SMEM
F32 = jnp.float32
BF16 = jnp.bfloat16
NT = (((1,), (1,)), ((), ()))
TN = (((0,), (0,)), ((), ()))


def spec(space=VMEM):
    return pl.BlockSpec(memory_space=space)


def dct_table():
    j = np.arange(KEEP, dtype=np.float32)[:, None]
    u = np.arange(BLOCK, dtype=np.float32)[None, :]
    table = np.cos(np.float32(math.pi) * (u + np.float32(0.5)) * j / np.float32(BLOCK))
    table = table * np.float32(math.sqrt(2.0 / BLOCK))
    table = np.where(j == 0, table * np.float32(math.sqrt(0.5)), table)
    return table.astype(jnp.bfloat16)


def dct_tile():
    return np.tile(dct_table().T, (1, BLOCK // KEEP))


def head_tables():
    table = dct_table()
    whole = np.zeros((16, 8, 2, 8, BLOCK), table.dtype)
    half = BLOCK // 2
    for owner in range(16):
        for t in range(TAPS - 1):
            low, high = (0, half) if owner % 2 == 0 else (half, 0)
            whole[owner, t, 0, owner // 2, low : low + KEEP] = table[:, t]
            whole[owner, 3 + t, 1, owner // 2, high : high + KEEP] = table[:, t]
    return whole.reshape(128, 16 * BLOCK)


def conv_kernel(
    kv_in, taps_in, table_in, conv_result, block_result, kv, taps, table, conv_out, block_out, sems
):
    moves = [(kv_in, kv), (taps_in, taps), (table_in, table)]
    moves += [(conv_out, conv_result), (block_out, block_result)]
    moves = [pltpu.make_async_copy(*move, sems.at[k]) for k, move in enumerate(moves)]
    for move in moves[:3]:
        move.start()
    for move in moves[:3]:
        move.wait()
    lanes = lax.broadcasted_iota(jnp.int32, (64, BLOCK), 1)
    turned = jnp.transpose(
        jnp.concatenate(
            [
                jnp.concatenate([taps[...], jnp.zeros((4, 64), F32)], 0),
                jnp.zeros((8, 64), F32),
            ],
            1,
        )
    )[:64]
    heads, tails = [], []
    for half in range(2):
        values = kv[:, half * SPAN : (half + 1) * SPAN].astype(F32)
        padded = jnp.concatenate([values, jnp.zeros((64, BLOCK), F32)], 1)
        total = turned[:, 0:1] * padded
        for w in range(1, TAPS):
            total = total + turned[:, w : w + 1] * pltpu.roll(padded, w, 1)
        conv_out[:, half * SPAN : (half + 1) * SPAN] = total[:, :SPAN].astype(BF16)
        if half:
            moves[3].start()
        heads.append(total[:, :BLOCK])
        tails.append(total[:, SPAN:])

    def join(pair):
        upper = pltpu.roll(pair[1], 3, 1)
        return jnp.where(lanes < 3, pair[0], jnp.where(lanes < 6, upper, 0.0))

    heads, tails = join(heads), join(tails)
    uneven = lax.axis_index("y_hi") == 1
    edges = jnp.concatenate([jnp.where(uneven, tails, heads), jnp.where(uneven, heads, tails)], 0)
    edges = jnp.transpose(edges)[:8]
    high = edges.astype(BF16)
    low = edges - high.astype(F32)
    edges = jnp.concatenate([high.astype(F32), low], 0).astype(BF16)
    packed = jnp.zeros((64, BLOCK), F32)
    for b in range(ROWS // BLOCK):
        part = conv_out[:, b * BLOCK : (b + 1) * BLOCK]
        if b * BLOCK % SPAN == 0:
            part = jnp.where(lanes < TAPS - 1, 0.0, part.astype(F32)).astype(BF16)
        part = jnp.dot(part, table[...], preferred_element_type=F32)
        packed = jnp.where(lanes // KEEP == b, part, packed)
    packed = jnp.where(lax.axis_index("core") == 1, pltpu.roll(packed, BLOCK // 2, 1), packed)
    high = packed.astype(BF16)
    low = jnp.where(lanes % (BLOCK // 2) < KEEP, packed - high.astype(F32), 0.0)
    rest = low[:EDGE]
    for g in range(1, 4):
        rest = rest + pltpu.roll(low[g * EDGE : (g + 1) * EDGE], g * KEEP, 1)
    rest = rest.astype(BF16)
    for k in range(block_out.shape[0]):
        block_out[k, :64] = high
        block_out[k, 64 : 64 + EDGE] = edges
        block_out[k, 64 + EDGE :] = rest
    moves[4].start()
    moves[3].wait()
    moves[4].wait()


def tails_kernel(q, near, out):
    for half in range(2):
        out[half] = q[(half + 1) * SPAN - EDGE : (half + 1) * SPAN]


def join_kernel(mine, near, query_conv, out):
    out[:64] = mine[...]
    out[64:] = near[...]


def query_kernel(q, own, swap, hop, taps, gain, out, gain_out):
    gain_out[...] = gain[...]
    place = lax.axis_index(CTX)
    odd = place % 2 == 1
    own, swap, hop = own[...].astype(F32), swap[...].astype(F32), hop[...].astype(F32)
    lower = jnp.where(odd, swap[0], hop[0])
    lower = jnp.where(place == 0, jnp.zeros_like(lower), lower)
    upper = jnp.where(odd, hop[1], swap[1])
    upper = jnp.where(place == 15, own[0], upper)
    for half, halo in enumerate((lower, upper)):
        for b in range(SPAN // BLOCK):
            start = half * SPAN + b * BLOCK
            values = q[start : start + BLOCK].astype(F32)
            if b:
                halo = q[start - EDGE : start].astype(F32)
            padded = jnp.concatenate([halo, values], 0)
            total = taps[0:1] * values
            for w in range(1, TAPS):
                total = total + taps[w : w + 1] * pltpu.roll(padded, w, 0)[EDGE:]
            out[start : start + BLOCK] = total.astype(BF16)


def pairs_kernel(mine, near, far, pairs):
    member = lax.axis_index(GROUP)
    pairs[member] = mine[...]
    pairs[member ^ 1] = near[...]
    pairs[member ^ 2] = far[:64]
    pairs[member ^ 3] = far[64:]


def attend_kernel(q, pairs, far_own, far_other, table, gain, out, packed, scores, ends):
    place = lax.axis_index(CTX)
    middle = place // 2
    odd = place % 2 == 1
    factor = math.log2(math.e) / math.sqrt(HEAD_CHANNELS)
    lane = lax.broadcasted_iota(jnp.int32, (BLOCK, BLOCK), 1)
    row = lax.broadcasted_iota(jnp.int32, (BLOCK, BLOCK), 0)
    edge_lane = lax.broadcasted_iota(jnp.int32, (8, BLOCK), 1) < BLOCK // 2
    edge_row = lax.broadcasted_iota(jnp.int32, (8, BLOCK), 0)
    tile_lane = lax.broadcasted_iota(jnp.int32, (64, BLOCK), 1)
    own_lane = jnp.where(tile_lane < BLOCK // 2, 1, 0) != jnp.where(odd, 1, 0)
    first_lane = lax.broadcasted_iota(jnp.int32, (EDGE, BLOCK), 1) % (BLOCK // 2) < KEEP

    def turned(value):
        return pltpu.roll(value, BLOCK // 2, 1)

    def edges_of(owner, m):
        mine = far_own[owner // 2, m, 64 : 64 + EDGE]
        other = far_other[owner // 2, m, 64 : 64 + EDGE]
        tile = jnp.where(odd, other, mine) if owner % 2 == 0 else jnp.where(odd, mine, other)
        tile = tile.astype(F32)
        return tile[:8] + tile[8:]

    def whole_tile(ref, i, m):
        rest = ref[i, m, 64 + EDGE :].astype(F32)
        parts = [rest] + [pltpu.roll(rest, BLOCK - g * KEEP, 1) for g in range(1, 4)]
        parts = [jnp.where(first_lane, part, 0.0) for part in parts]
        return ref[i, m, :64].astype(F32) + jnp.concatenate(parts, 0)

    first_rows = []
    for kind in range(2):
        heads, tails = [], []
        for owner in range(16):
            left, right = edges_of(owner, 2 * kind), edges_of(owner, 2 * kind + 1)
            heads.append(jnp.where(edge_lane, left, right))
            tails.append(turned(jnp.where(edge_lane, right, left)))
        for owner in range(16):
            below = tails[owner - 1] if owner else jnp.zeros((8, BLOCK), F32)
            above = tails[owner + 1] if owner < 15 else pltpu.roll(tails[15], 3, 0)
            ends[kind, owner] = heads[owner] + jnp.where(edge_row < 3, below, above)
        both = jnp.transpose(ends[kind].reshape(128, HEAD_CHANNELS)).astype(BF16)
        fix = jnp.dot(both, table[...], preferred_element_type=F32)
        for i in range(8):
            for m in range(2):
                rows = slice(64 * m, 64 * (m + 1))
                mine = whole_tile(far_own, i, 2 * kind + m)
                other = whole_tile(far_other, i, 2 * kind + m)
                low = jnp.where(own_lane, mine, other) + fix[rows, i * BLOCK : (i + 1) * BLOCK]
                high = jnp.where(own_lane, other, mine)
                high = high + fix[rows, (8 + i) * BLOCK : (9 + i) * BLOCK]
                packed[kind, 0, i, rows] = low.astype(BF16)
                packed[kind, 1, i, rows] = high.astype(BF16)
        pick = (
            (edge_row < 3)
            & (lax.broadcasted_iota(jnp.int32, (8, BLOCK), 1) == edge_row)
        ) | (
            (edge_row >= 3)
            & (edge_row < 6)
            & (lax.broadcasted_iota(jnp.int32, (8, BLOCK), 1) == edge_row - 3 + BLOCK // 2)
        )
        first_rows.append(
            lax.dot_general(
                ends[kind, place].astype(BF16),
                jnp.where(pick, 1.0, 0.0).astype(BF16),
                TN,
                preferred_element_type=F32,
            )
        )

    def near_tile(kind, start):
        tile = jnp.concatenate(
            [pairs[2 * kind, :, start : start + BLOCK], pairs[2 * kind + 1, :, start : start + BLOCK]], 0
        )
        if start % SPAN == 0:
            first = first_rows[kind] if start == 0 else turned(first_rows[kind])
            tile = jnp.where(lane < TAPS - 1, first, tile.astype(F32)).astype(BF16)
        return tile

    key_block = (lax.broadcasted_iota(jnp.int32, (1, BLOCK), 1) % (BLOCK // 2)) // KEEP
    left_lanes = lax.broadcasted_iota(jnp.int32, (1, BLOCK), 1) < BLOCK // 2
    per_chunk = CHUNK // BLOCK
    for r in range(SPAN // CHUNK):
        tops = [jnp.full((CHUNK, BLOCK), NEGATIVE, F32) for _ in range(2)]
        for half in range(2):
            tiles = []
            for c in range(per_chunk):
                start = half * SPAN + r * CHUNK + c * BLOCK
                near = jnp.dot(
                    q[start : start + BLOCK], near_tile(0, start), preferred_element_type=F32
                )
                tiles.append(jnp.where(row >= lane, near, NEGATIVE))
            tops[half] = jnp.concatenate(tiles, 0)
            scores[17 + half] = tops[half]
        upper = q[SPAN + r * CHUNK : SPAN + (r + 1) * CHUNK]
        for i in range(4):
            far = jnp.dot(
                upper,
                jnp.concatenate([packed[0, 0, 2 * i], packed[0, 0, 2 * i + 1]], 1),
                preferred_element_type=F32,
            )
            scores[9 + 2 * i] = far[:, :BLOCK]
            scores[10 + 2 * i] = far[:, BLOCK:]
            tops[1] = jnp.maximum(tops[1], jnp.maximum(far[:, :BLOCK], far[:, BLOCK:]))
        for j in range(9):
            high = j > middle
            side = high.astype(jnp.int32)
            partial = (j == middle) | (j == middle + 1)
            start = pl.multiple_of(side * SPAN + r * CHUNK, CHUNK)
            far = jnp.dot(
                q[pl.ds(start, CHUNK)], packed[0, side, j - side], preferred_element_type=F32
            )
            biases = []
            for c in range(per_chunk):
                block = r * per_chunk + c
                left = jnp.where(high, jnp.where(odd, block, 4), jnp.where(odd, 4, block))
                right = jnp.where(high, jnp.where(odd, 0, block), jnp.where(odd, block, 0))
                left, right = jnp.where(partial, left, 4), jnp.where(partial, right, 4)
                seen = key_block < jnp.where(left_lanes, left, right)
                biases.append(
                    jnp.broadcast_to(jnp.where(seen, 0.0, NEGATIVE), (BLOCK, BLOCK))
                )
            far = far + jnp.concatenate(biases, 0)
            scores[j] = far
            tops[0] = jnp.maximum(tops[0], jnp.where(high, NEGATIVE, far))
            tops[1] = jnp.maximum(tops[1], jnp.where(high, far, NEGATIVE))
        tops = [
            jnp.broadcast_to(jnp.max(t, 1, keepdims=True) * factor, (CHUNK, BLOCK)) for t in tops
        ]
        totals, sums = [], []
        for half in range(2):
            weights = jnp.exp2(scores[17 + half] * factor - tops[half])
            totals.append(weights)
            weights = weights.astype(BF16)
            sums.append(
                jnp.concatenate(
                    [
                        lax.dot_general(
                            weights[c * BLOCK : (c + 1) * BLOCK],
                            near_tile(1, half * SPAN + r * CHUNK + c * BLOCK),
                            NT,
                            preferred_element_type=F32,
                        )
                        for c in range(per_chunk)
                    ],
                    0,
                )
            )
        for i in range(4):
            first = jnp.exp2(scores[9 + 2 * i] * factor - tops[1])
            second = jnp.exp2(scores[10 + 2 * i] * factor - tops[1])
            totals[1] = totals[1] + first + second
            sums[1] = sums[1] + lax.dot_general(
                jnp.concatenate([first, second], 1).astype(BF16),
                jnp.concatenate([packed[1, 0, 2 * i], packed[1, 0, 2 * i + 1]], 1),
                NT,
                preferred_element_type=F32,
            )
        for j in range(9):
            high = j > middle
            side = high.astype(jnp.int32)
            weights = jnp.exp2(scores[j] * factor - jnp.where(high, tops[1], tops[0]))
            totals[0] = totals[0] + jnp.where(high, 0.0, weights)
            totals[1] = totals[1] + jnp.where(high, weights, 0.0)
            part = lax.dot_general(
                weights.astype(BF16), packed[1, side, j - side], NT, preferred_element_type=F32
            )
            sums[0] = sums[0] + jnp.where(high, 0.0, part)
            sums[1] = sums[1] + jnp.where(high, part, 0.0)
        for half in range(2):
            attended = sums[half] / jnp.sum(totals[half], 1, keepdims=True)
            mean = jnp.mean(attended * attended, 1, keepdims=True)
            normed = attended * lax.rsqrt(mean + EPSILON)
            start = half * SPAN + r * CHUNK
            out[start : start + CHUNK] = (normed * gain[...]).astype(BF16)


def cost(flops, moved):
    return pl.CostEstimate(flops=flops, bytes_accessed=moved, transcendentals=0)


def swapped(value, axis):
    return lax.ppermute(value, axis, [(0, 1), (1, 0)])


def per_device(queries, keys_values, query_taps, pair_taps, out_gain):
    def call(kernel, name, out_shape, operands, spaces=None, scratch=(), flops=1 << 24):
        many = isinstance(out_shape, tuple)
        return pl.pallas_call(
            kernel,
            out_shape=out_shape,
            in_specs=[spec(s) for s in spaces] if spaces else [spec()] * len(operands),
            out_specs=(spec(),) * len(out_shape) if many else spec(),
            scratch_shapes=scratch,
            compiler_params=pltpu.CompilerParams(vmem_limit_bytes=24 << 20),
            cost_estimate=cost(flops, 1 << 20),
            name=name,
        )(*operands)

    def shape(*dims):
        return jax.ShapeDtypeStruct(dims, BF16)

    conv, blocks = pl.pallas_call(
        conv_kernel,
        out_shape=(shape(64, ROWS), shape(32, SENT, BLOCK)),
        in_specs=[spec(pl.ANY)] * 3,
        out_specs=(spec(pl.ANY), spec(pl.ANY)),
        scratch_shapes=[
            VMEM((64, ROWS), BF16),
            VMEM((TAPS, 64), F32),
            VMEM((BLOCK, BLOCK), BF16),
            VMEM((64, ROWS), BF16),
            VMEM((32, SENT, BLOCK), BF16),
            pltpu.SemaphoreType.DMA((5,)),
        ],
        compiler_params=pltpu.CompilerParams(vmem_limit_bytes=56 << 20),
        cost_estimate=cost(1 << 24, 1 << 20),
        name="conv",
    )(keys_values.T, pair_taps, jnp.asarray(dct_tile()))
    gathered = lax.all_to_all(blocks, CHIPS + GROUP, 0, 0, tiled=True)
    near = swapped(conv, "y_hi")
    tails = call(
        tails_kernel,
        "tails",
        shape(2, EDGE, BLOCK),
        (queries, near),
        (VMEM, pl.ANY),
        flops=1 << 37,
    )
    swap = swapped(tails, "core")
    hop = lax.ppermute(
        tails, CTX, [(i, i + 1) for i in range(1, 15, 2)] + [(i + 1, i) for i in range(1, 15, 2)]
    )
    query_conv, gain = call(
        query_kernel,
        "queries",
        (shape(ROWS, HEAD_CHANNELS), jax.ShapeDtypeStruct((1, HEAD_CHANNELS), F32)),
        (queries, tails, swap, hop, query_taps, out_gain.reshape(1, -1)),
    )
    joined = call(
        join_kernel, "join", shape(128, ROWS), (conv, near, query_conv), (VMEM, VMEM, pl.ANY)
    )
    far = swapped(joined, "z_lo")
    gathered, query_conv = lax.optimization_barrier((gathered, query_conv))
    far_own = gathered.reshape(8, 4, SENT, BLOCK)
    far_other = swapped(far_own, "core")
    pairs = call(pairs_kernel, "pairs", shape(4, 64, ROWS), (conv, near, far), flops=1 << 37)
    return call(
        attend_kernel,
        "attend",
        shape(ROWS, HEAD_CHANNELS),
        (query_conv, pairs, far_own, far_other, jnp.asarray(head_tables()), gain),
        scratch=[
            VMEM((2, 2, 8, HEAD_CHANNELS, BLOCK), BF16),
            VMEM((19, CHUNK, BLOCK), F32),
            VMEM((2, 16, 8, HEAD_CHANNELS), F32),
        ],
        flops=1 << 30,
    )


def solution(mesh):
    fine = Mesh(mesh.devices.reshape(2, 4, 2, 8, 2, 2), CTX + MP)
    in_specs = (P(CTX, MP), P(CTX, MP), P(None, MP), P(None, MP), P(MP))
    return jax.shard_map(
        per_device, mesh=fine, in_specs=in_specs, out_specs=P(CTX, MP), check_vma=False
    )
```

```python
import functools
import math

import jax
import jax.numpy as jnp
import numpy as np
from jax import lax
from jax.experimental import pallas as pl
from jax.experimental.pallas import tpu as pltpu
from jax.sharding import Mesh, PartitionSpec as P

HEAD_CHANNELS = 128
TAPS = 4
BLOCK = 128
KEEP = 16
SPAN = 512
ROWS = 2 * SPAN
NEGATIVE = -1e30
EPSILON = 1e-06
EDGE = 16
SENT = 64 + 2 * EDGE
CHUNK = 256

CTX = ("y_lo", "x", "core")
MP = ("z_hi", "z_lo", "y_hi")
GROUP = ("z_lo", "y_hi")
CHIPS = ("y_lo", "x")

VMEM = pltpu.VMEM
SMEM = pltpu.SMEM
F32 = jnp.float32
BF16 = jnp.bfloat16
NT = (((1,), (1,)), ((), ()))
TN = (((0,), (0,)), ((), ()))


def spec(space=VMEM):
    return pl.BlockSpec(memory_space=space)


def dct_table():
    j = np.arange(KEEP, dtype=np.float32)[:, None]
    u = np.arange(BLOCK, dtype=np.float32)[None, :]
    table = np.cos(np.float32(math.pi) * (u + np.float32(0.5)) * j / np.float32(BLOCK))
    table = table * np.float32(math.sqrt(2.0 / BLOCK))
    table = np.where(j == 0, table * np.float32(math.sqrt(0.5)), table)
    return table.astype(jnp.bfloat16)


def dct_tile():
    return np.tile(dct_table().T, (1, BLOCK // KEEP))


def head_tables():
    table = dct_table()
    whole = np.zeros((16, 8, 2, 8, BLOCK), table.dtype)
    half = BLOCK // 2
    for owner in range(16):
        for t in range(TAPS - 1):
            low, high = (0, half) if owner % 2 == 0 else (half, 0)
            whole[owner, t, 0, owner // 2, low : low + KEEP] = table[:, t]
            whole[owner, 3 + t, 1, owner // 2, high : high + KEEP] = table[:, t]
    return whole.reshape(128, 16 * BLOCK)


def conv_kernel(
    kv_in, taps_in, table_in, conv_result, block_result, kv, taps, table, conv_out, block_out, sems
):
    moves = [(kv_in, kv), (taps_in, taps), (table_in, table)]
    moves += [(conv_out, conv_result), (block_out, block_result)]
    moves = [pltpu.make_async_copy(*move, sems.at[k]) for k, move in enumerate(moves)]
    for move in moves[:3]:
        move.start()
    for move in moves[:3]:
        move.wait()
    lanes = lax.broadcasted_iota(jnp.int32, (64, BLOCK), 1)
    turned = jnp.transpose(
        jnp.concatenate(
            [
                jnp.concatenate([taps[...], jnp.zeros((4, 64), F32)], 0),
                jnp.zeros((8, 64), F32),
            ],
            1,
        )
    )[:64]
    heads, tails = [], []
    for half in range(2):
        values = kv[:, half * SPAN : (half + 1) * SPAN].astype(F32)
        padded = jnp.concatenate([values, jnp.zeros((64, BLOCK), F32)], 1)
        total = turned[:, 0:1] * padded
        for w in range(1, TAPS):
            total = total + turned[:, w : w + 1] * pltpu.roll(padded, w, 1)
        conv_out[:, half * SPAN : (half + 1) * SPAN] = total[:, :SPAN].astype(BF16)
        if half:
            moves[3].start()
        heads.append(total[:, :BLOCK])
        tails.append(total[:, SPAN:])

    def join(pair):
        upper = pltpu.roll(pair[1], 3, 1)
        return jnp.where(lanes < 3, pair[0], jnp.where(lanes < 6, upper, 0.0))

    heads, tails = join(heads), join(tails)
    uneven = lax.axis_index("y_hi") == 1
    edges = jnp.concatenate([jnp.where(uneven, tails, heads), jnp.where(uneven, heads, tails)], 0)
    edges = jnp.transpose(edges)[:8]
    high = edges.astype(BF16)
    low = edges - high.astype(F32)
    edges = jnp.concatenate([high.astype(F32), low], 0).astype(BF16)
    packed = jnp.zeros((64, BLOCK), F32)
    for b in range(ROWS // BLOCK):
        part = conv_out[:, b * BLOCK : (b + 1) * BLOCK]
        if b * BLOCK % SPAN == 0:
            part = jnp.where(lanes < TAPS - 1, 0.0, part.astype(F32)).astype(BF16)
        part = jnp.dot(part, table[...], preferred_element_type=F32)
        packed = jnp.where(lanes // KEEP == b, part, packed)
    packed = jnp.where(lax.axis_index("core") == 1, pltpu.roll(packed, BLOCK // 2, 1), packed)
    high = packed.astype(BF16)
    low = jnp.where(lanes % (BLOCK // 2) < KEEP, packed - high.astype(F32), 0.0)
    rest = low[:EDGE]
    for g in range(1, 4):
        rest = rest + pltpu.roll(low[g * EDGE : (g + 1) * EDGE], g * KEEP, 1)
    rest = rest.astype(BF16)
    for k in range(block_out.shape[0]):
        block_out[k, :64] = high
        block_out[k, 64 : 64 + EDGE] = edges
        block_out[k, 64 + EDGE :] = rest
    moves[4].start()
    moves[3].wait()
    moves[4].wait()


def tails_kernel(q, near, conv, out):
    for half in range(2):
        out[half] = q[(half + 1) * SPAN - EDGE : (half + 1) * SPAN]


def join_kernel(mine, near, query_conv, out):
    out[:64] = mine[...]
    out[64:] = near[...]


def query_kernel(q, own, swap, hop, taps, gain, out, gain_out):
    gain_out[...] = gain[...]
    place = lax.axis_index(CTX)
    odd = place % 2 == 1
    own, swap, hop = own[...].astype(F32), swap[...].astype(F32), hop[...].astype(F32)
    lower = jnp.where(odd, swap[0], hop[0])
    lower = jnp.where(place == 0, jnp.zeros_like(lower), lower)
    upper = jnp.where(odd, hop[1], swap[1])
    upper = jnp.where(place == 15, own[0], upper)
    for half, halo in enumerate((lower, upper)):
        for b in range(SPAN // BLOCK):
            start = half * SPAN + b * BLOCK
            values = q[start : start + BLOCK].astype(F32)
            if b:
                halo = q[start - EDGE : start].astype(F32)
            padded = jnp.concatenate([halo, values], 0)
            total = taps[0:1] * values
            for w in range(1, TAPS):
                total = total + taps[w : w + 1] * pltpu.roll(padded, w, 0)[EDGE:]
            out[start : start + BLOCK] = total.astype(BF16)


def pairs_kernel(mine, near, far, pairs):
    member = lax.axis_index(GROUP)
    pairs[member] = mine[...]
    pairs[member ^ 1] = near[...]
    pairs[member ^ 2] = far[:64]
    pairs[member ^ 3] = far[64:]


def attend_kernel(q, pairs, far_own, far_other, table, gain, out, packed, scores, ends):
    place = lax.axis_index(CTX)
    middle = place // 2
    odd = place % 2 == 1
    factor = math.log2(math.e) / math.sqrt(HEAD_CHANNELS)
    lane = lax.broadcasted_iota(jnp.int32, (BLOCK, BLOCK), 1)
    row = lax.broadcasted_iota(jnp.int32, (BLOCK, BLOCK), 0)
    edge_lane = lax.broadcasted_iota(jnp.int32, (8, BLOCK), 1) < BLOCK // 2
    edge_row = lax.broadcasted_iota(jnp.int32, (8, BLOCK), 0)
    tile_lane = lax.broadcasted_iota(jnp.int32, (64, BLOCK), 1)
    own_lane = jnp.where(tile_lane < BLOCK // 2, 1, 0) != jnp.where(odd, 1, 0)
    first_lane = lax.broadcasted_iota(jnp.int32, (EDGE, BLOCK), 1) % (BLOCK // 2) < KEEP

    def turned(value):
        return pltpu.roll(value, BLOCK // 2, 1)

    def edges_of(owner, m):
        mine = far_own[owner // 2, m, 64 : 64 + EDGE]
        other = far_other[owner // 2, m, 64 : 64 + EDGE]
        tile = jnp.where(odd, other, mine) if owner % 2 == 0 else jnp.where(odd, mine, other)
        tile = tile.astype(F32)
        return tile[:8] + tile[8:]

    def whole_tile(ref, i, m):
        rest = ref[i, m, 64 + EDGE :].astype(F32)
        parts = [rest] + [pltpu.roll(rest, BLOCK - g * KEEP, 1) for g in range(1, 4)]
        parts = [jnp.where(first_lane, part, 0.0) for part in parts]
        return ref[i, m, :64].astype(F32) + jnp.concatenate(parts, 0)

    first_rows = []
    for kind in range(2):
        heads, tails = [], []
        for owner in range(16):
            left, right = edges_of(owner, 2 * kind), edges_of(owner, 2 * kind + 1)
            heads.append(jnp.where(edge_lane, left, right))
            tails.append(turned(jnp.where(edge_lane, right, left)))
        for owner in range(16):
            below = tails[owner - 1] if owner else jnp.zeros((8, BLOCK), F32)
            above = tails[owner + 1] if owner < 15 else pltpu.roll(tails[15], 3, 0)
            ends[kind, owner] = heads[owner] + jnp.where(edge_row < 3, below, above)
        both = jnp.transpose(ends[kind].reshape(128, HEAD_CHANNELS)).astype(BF16)
        fix = jnp.dot(both, table[...], preferred_element_type=F32)
        for i in range(8):
            for m in range(2):
                rows = slice(64 * m, 64 * (m + 1))
                mine = whole_tile(far_own, i, 2 * kind + m)
                other = whole_tile(far_other, i, 2 * kind + m)
                low = jnp.where(own_lane, mine, other) + fix[rows, i * BLOCK : (i + 1) * BLOCK]
                high = jnp.where(own_lane, other, mine)
                high = high + fix[rows, (8 + i) * BLOCK : (9 + i) * BLOCK]
                packed[kind, 0, i, rows] = low.astype(BF16)
                packed[kind, 1, i, rows] = high.astype(BF16)
        pick = (
            (edge_row < 3)
            & (lax.broadcasted_iota(jnp.int32, (8, BLOCK), 1) == edge_row)
        ) | (
            (edge_row >= 3)
            & (edge_row < 6)
            & (lax.broadcasted_iota(jnp.int32, (8, BLOCK), 1) == edge_row - 3 + BLOCK // 2)
        )
        first_rows.append(
            lax.dot_general(
                ends[kind, place].astype(BF16),
                jnp.where(pick, 1.0, 0.0).astype(BF16),
                TN,
                preferred_element_type=F32,
            )
        )

    def near_tile(kind, start):
        tile = jnp.concatenate(
            [pairs[2 * kind, :, start : start + BLOCK], pairs[2 * kind + 1, :, start : start + BLOCK]], 0
        )
        if start % SPAN == 0:
            first = first_rows[kind] if start == 0 else turned(first_rows[kind])
            tile = jnp.where(lane < TAPS - 1, first, tile.astype(F32)).astype(BF16)
        return tile

    key_block = (lax.broadcasted_iota(jnp.int32, (1, BLOCK), 1) % (BLOCK // 2)) // KEEP
    left_lanes = lax.broadcasted_iota(jnp.int32, (1, BLOCK), 1) < BLOCK // 2
    per_chunk = CHUNK // BLOCK
    for r in range(SPAN // CHUNK):
        tops = [jnp.full((CHUNK, BLOCK), NEGATIVE, F32) for _ in range(2)]
        for half in range(2):
            tiles = []
            for c in range(per_chunk):
                start = half * SPAN + r * CHUNK + c * BLOCK
                near = jnp.dot(
                    q[start : start + BLOCK], near_tile(0, start), preferred_element_type=F32
                )
                tiles.append(jnp.where(row >= lane, near, NEGATIVE))
            tops[half] = jnp.concatenate(tiles, 0)
            scores[17 + half] = tops[half]
        upper = q[SPAN + r * CHUNK : SPAN + (r + 1) * CHUNK]
        for i in range(4):
            far = jnp.dot(
                upper,
                jnp.concatenate([packed[0, 0, 2 * i], packed[0, 0, 2 * i + 1]], 1),
                preferred_element_type=F32,
            )
            scores[9 + 2 * i] = far[:, :BLOCK]
            scores[10 + 2 * i] = far[:, BLOCK:]
            tops[1] = jnp.maximum(tops[1], jnp.maximum(far[:, :BLOCK], far[:, BLOCK:]))
        for j in range(9):
            high = j > middle
            side = high.astype(jnp.int32)
            partial = (j == middle) | (j == middle + 1)
            start = pl.multiple_of(side * SPAN + r * CHUNK, CHUNK)
            far = jnp.dot(
                q[pl.ds(start, CHUNK)], packed[0, side, j - side], preferred_element_type=F32
            )
            biases = []
            for c in range(per_chunk):
                block = r * per_chunk + c
                left = jnp.where(high, jnp.where(odd, block, 4), jnp.where(odd, 4, block))
                right = jnp.where(high, jnp.where(odd, 0, block), jnp.where(odd, block, 0))
                left, right = jnp.where(partial, left, 4), jnp.where(partial, right, 4)
                seen = key_block < jnp.where(left_lanes, left, right)
                biases.append(
                    jnp.broadcast_to(jnp.where(seen, 0.0, NEGATIVE), (BLOCK, BLOCK))
                )
            far = far + jnp.concatenate(biases, 0)
            scores[j] = far
            tops[0] = jnp.maximum(tops[0], jnp.where(high, NEGATIVE, far))
            tops[1] = jnp.maximum(tops[1], jnp.where(high, far, NEGATIVE))
        tops = [
            jnp.broadcast_to(jnp.max(t, 1, keepdims=True) * factor, (CHUNK, BLOCK)) for t in tops
        ]
        totals, sums = [], []
        for half in range(2):
            weights = jnp.exp2(scores[17 + half] * factor - tops[half])
            totals.append(weights)
            weights = weights.astype(BF16)
            sums.append(
                jnp.concatenate(
                    [
                        lax.dot_general(
                            weights[c * BLOCK : (c + 1) * BLOCK],
                            near_tile(1, half * SPAN + r * CHUNK + c * BLOCK),
                            NT,
                            preferred_element_type=F32,
                        )
                        for c in range(per_chunk)
                    ],
                    0,
                )
            )
        for i in range(4):
            first = jnp.exp2(scores[9 + 2 * i] * factor - tops[1])
            second = jnp.exp2(scores[10 + 2 * i] * factor - tops[1])
            totals[1] = totals[1] + first + second
            sums[1] = sums[1] + lax.dot_general(
                jnp.concatenate([first, second], 1).astype(BF16),
                jnp.concatenate([packed[1, 0, 2 * i], packed[1, 0, 2 * i + 1]], 1),
                NT,
                preferred_element_type=F32,
            )
        for j in range(9):
            high = j > middle
            side = high.astype(jnp.int32)
            weights = jnp.exp2(scores[j] * factor - jnp.where(high, tops[1], tops[0]))
            totals[0] = totals[0] + jnp.where(high, 0.0, weights)
            totals[1] = totals[1] + jnp.where(high, weights, 0.0)
            part = lax.dot_general(
                weights.astype(BF16), packed[1, side, j - side], NT, preferred_element_type=F32
            )
            sums[0] = sums[0] + jnp.where(high, 0.0, part)
            sums[1] = sums[1] + jnp.where(high, part, 0.0)
        for half in range(2):
            attended = sums[half] / jnp.sum(totals[half], 1, keepdims=True)
            mean = jnp.mean(attended * attended, 1, keepdims=True)
            normed = attended * lax.rsqrt(mean + EPSILON)
            start = half * SPAN + r * CHUNK
            out[start : start + CHUNK] = (normed * gain[...]).astype(BF16)


def cost(flops, moved):
    return pl.CostEstimate(flops=flops, bytes_accessed=moved, transcendentals=0)


def swapped(value, axis):
    return lax.ppermute(value, axis, [(0, 1), (1, 0)])


def per_device(queries, keys_values, query_taps, pair_taps, out_gain):
    def call(kernel, name, out_shape, operands, spaces=None, scratch=(), flops=1 << 24):
        many = isinstance(out_shape, tuple)
        return pl.pallas_call(
            kernel,
            out_shape=out_shape,
            in_specs=[spec(s) for s in spaces] if spaces else [spec()] * len(operands),
            out_specs=(spec(),) * len(out_shape) if many else spec(),
            scratch_shapes=scratch,
            compiler_params=pltpu.CompilerParams(vmem_limit_bytes=24 << 20),
            cost_estimate=cost(flops, 1 << 20),
            name=name,
        )(*operands)

    def shape(*dims):
        return jax.ShapeDtypeStruct(dims, BF16)

    conv, blocks = pl.pallas_call(
        conv_kernel,
        out_shape=(shape(64, ROWS), shape(32, SENT, BLOCK)),
        in_specs=[spec(pl.ANY)] * 3,
        out_specs=(spec(pl.ANY), spec(pl.ANY)),
        scratch_shapes=[
            VMEM((64, ROWS), BF16),
            VMEM((TAPS, 64), F32),
            VMEM((BLOCK, BLOCK), BF16),
            VMEM((64, ROWS), BF16),
            VMEM((32, SENT, BLOCK), BF16),
            pltpu.SemaphoreType.DMA((5,)),
        ],
        compiler_params=pltpu.CompilerParams(vmem_limit_bytes=56 << 20),
        cost_estimate=cost(1 << 24, 1 << 20),
        name="conv",
    )(keys_values.T, pair_taps, jnp.asarray(dct_tile()))
    gathered = lax.all_to_all(blocks, CHIPS + GROUP, 0, 0, tiled=True)
    near = swapped(conv, "y_hi")
    tails = call(
        tails_kernel,
        "tails",
        shape(2, EDGE, BLOCK),
        (queries, near, conv),
        (VMEM, pl.ANY, VMEM),
        flops=1 << 37,
    )
    swap = swapped(tails, "core")
    hop = lax.ppermute(
        tails, CTX, [(i, i + 1) for i in range(1, 15, 2)] + [(i + 1, i) for i in range(1, 15, 2)]
    )
    query_conv, gain = call(
        query_kernel,
        "queries",
        (shape(ROWS, HEAD_CHANNELS), jax.ShapeDtypeStruct((1, HEAD_CHANNELS), F32)),
        (queries, tails, swap, hop, query_taps, out_gain.reshape(1, -1)),
    )
    joined = call(
        join_kernel, "join", shape(128, ROWS), (conv, near, query_conv), (VMEM, VMEM, pl.ANY)
    )
    far = swapped(joined, "z_lo")
    gathered, query_conv = lax.optimization_barrier((gathered, query_conv))
    far_own = gathered.reshape(8, 4, SENT, BLOCK)
    far_other = swapped(far_own, "core")
    pairs = call(pairs_kernel, "pairs", shape(4, 64, ROWS), (conv, near, far), flops=1 << 37)
    return call(
        attend_kernel,
        "attend",
        shape(ROWS, HEAD_CHANNELS),
        (query_conv, pairs, far_own, far_other, jnp.asarray(head_tables()), gain),
        scratch=[
            VMEM((2, 2, 8, HEAD_CHANNELS, BLOCK), BF16),
            VMEM((19, CHUNK, BLOCK), F32),
            VMEM((2, 16, 8, HEAD_CHANNELS), F32),
        ],
        flops=1 << 30,
    )


def solution(mesh):
    fine = Mesh(mesh.devices.reshape(2, 4, 2, 8, 2, 2), CTX + MP)
    in_specs = (P(CTX, MP), P(CTX, MP), P(None, MP), P(None, MP), P(MP))
    return jax.shard_map(
        per_device, mesh=fine, in_specs=in_specs, out_specs=P(CTX, MP), check_vma=False
    )
```

```python
import functools
import math

import jax
import jax.numpy as jnp
import numpy as np
from jax import lax
from jax.experimental import pallas as pl
from jax.experimental.pallas import tpu as pltpu
from jax.sharding import Mesh, PartitionSpec as P

HEAD_CHANNELS = 128
TAPS = 4
BLOCK = 128
KEEP = 16
SPAN = 512
ROWS = 2 * SPAN
NEGATIVE = -1e30
EPSILON = 1e-06
EDGE = 16
SENT = 64 + 2 * EDGE
CHUNK = 256

CTX = ("y_lo", "x", "core")
MP = ("z_hi", "z_lo", "y_hi")
GROUP = ("z_lo", "y_hi")
CHIPS = ("y_lo", "x")

VMEM = pltpu.VMEM
SMEM = pltpu.SMEM
F32 = jnp.float32
BF16 = jnp.bfloat16
NT = (((1,), (1,)), ((), ()))
TN = (((0,), (0,)), ((), ()))


def spec(space=VMEM):
    return pl.BlockSpec(memory_space=space)


def dct_table():
    j = np.arange(KEEP, dtype=np.float32)[:, None]
    u = np.arange(BLOCK, dtype=np.float32)[None, :]
    table = np.cos(np.float32(math.pi) * (u + np.float32(0.5)) * j / np.float32(BLOCK))
    table = table * np.float32(math.sqrt(2.0 / BLOCK))
    table = np.where(j == 0, table * np.float32(math.sqrt(0.5)), table)
    return table.astype(jnp.bfloat16)


def dct_tile():
    return np.tile(dct_table().T, (1, BLOCK // KEEP))


def head_tables():
    table = dct_table()
    whole = np.zeros((16, 8, 2, 8, BLOCK), table.dtype)
    half = BLOCK // 2
    for owner in range(16):
        for t in range(TAPS - 1):
            low, high = (0, half) if owner % 2 == 0 else (half, 0)
            whole[owner, t, 0, owner // 2, low : low + KEEP] = table[:, t]
            whole[owner, 3 + t, 1, owner // 2, high : high + KEEP] = table[:, t]
    return whole.reshape(128, 16 * BLOCK)


def conv_kernel(
    kv_in, taps_in, table_in, conv_result, block_result, kv, taps, table, conv_out, block_out, sems
):
    moves = [(kv_in, kv), (taps_in, taps), (table_in, table)]
    moves += [(conv_out, conv_result), (block_out, block_result)]
    moves = [pltpu.make_async_copy(*move, sems.at[k]) for k, move in enumerate(moves)]
    for move in moves[:3]:
        move.start()
    for move in moves[:3]:
        move.wait()
    lanes = lax.broadcasted_iota(jnp.int32, (64, BLOCK), 1)
    turned = jnp.transpose(
        jnp.concatenate(
            [
                jnp.concatenate([taps[...], jnp.zeros((4, 64), F32)], 0),
                jnp.zeros((8, 64), F32),
            ],
            1,
        )
    )[:64]
    heads, tails = [], []
    for half in range(2):
        values = kv[:, half * SPAN : (half + 1) * SPAN].astype(F32)
        padded = jnp.concatenate([values, jnp.zeros((64, BLOCK), F32)], 1)
        total = turned[:, 0:1] * padded
        for w in range(1, TAPS):
            total = total + turned[:, w : w + 1] * pltpu.roll(padded, w, 1)
        conv_out[:, half * SPAN : (half + 1) * SPAN] = total[:, :SPAN].astype(BF16)
        if half:
            moves[3].start()
        heads.append(total[:, :BLOCK])
        tails.append(total[:, SPAN:])

    def join(pair):
        upper = pltpu.roll(pair[1], 3, 1)
        return jnp.where(lanes < 3, pair[0], jnp.where(lanes < 6, upper, 0.0))

    heads, tails = join(heads), join(tails)
    uneven = lax.axis_index("y_hi") == 1
    edges = jnp.concatenate([jnp.where(uneven, tails, heads), jnp.where(uneven, heads, tails)], 0)
    edges = jnp.transpose(edges)[:8]
    high = edges.astype(BF16)
    low = edges - high.astype(F32)
    edges = jnp.concatenate([high.astype(F32), low], 0).astype(BF16)
    packed = jnp.zeros((64, BLOCK), F32)
    for b in range(ROWS // BLOCK):
        part = conv_out[:, b * BLOCK : (b + 1) * BLOCK]
        if b * BLOCK % SPAN == 0:
            part = jnp.where(lanes < TAPS - 1, 0.0, part.astype(F32)).astype(BF16)
        part = jnp.dot(part, table[...], preferred_element_type=F32)
        packed = jnp.where(lanes // KEEP == b, part, packed)
    packed = jnp.where(lax.axis_index("core") == 1, pltpu.roll(packed, BLOCK // 2, 1), packed)
    high = packed.astype(BF16)
    low = jnp.where(lanes % (BLOCK // 2) < KEEP, packed - high.astype(F32), 0.0)
    rest = low[:EDGE]
    for g in range(1, 4):
        rest = rest + pltpu.roll(low[g * EDGE : (g + 1) * EDGE], g * KEEP, 1)
    rest = rest.astype(BF16)
    for k in range(block_out.shape[0]):
        block_out[k, :64] = high
        block_out[k, 64 : 64 + EDGE] = edges
        block_out[k, 64 + EDGE :] = rest
    moves[4].start()
    moves[3].wait()
    moves[4].wait()


def tails_kernel(q, near, conv, out):
    for half in range(2):
        out[half] = q[(half + 1) * SPAN - EDGE : (half + 1) * SPAN]


def join_kernel(mine, near, query_conv, out):
    out[:64] = mine[...]
    out[64:] = near[...]


def query_kernel(q, own, swap, hop, taps, gain, out, gain_out):
    gain_out[...] = gain[...]
    place = lax.axis_index(CTX)
    odd = place % 2 == 1
    own, swap, hop = own[...].astype(F32), swap[...].astype(F32), hop[...].astype(F32)
    lower = jnp.where(odd, swap[0], hop[0])
    lower = jnp.where(place == 0, jnp.zeros_like(lower), lower)
    upper = jnp.where(odd, hop[1], swap[1])
    upper = jnp.where(place == 15, own[0], upper)
    for half, halo in enumerate((lower, upper)):
        for b in range(SPAN // BLOCK):
            start = half * SPAN + b * BLOCK
            values = q[start : start + BLOCK].astype(F32)
            if b:
                halo = q[start - EDGE : start].astype(F32)
            padded = jnp.concatenate([halo, values], 0)
            total = taps[0:1] * values
            for w in range(1, TAPS):
                total = total + taps[w : w + 1] * pltpu.roll(padded, w, 0)[EDGE:]
            out[start : start + BLOCK] = total.astype(BF16)


def pairs_kernel(mine, near, far, edges, pairs):
    member = lax.axis_index(GROUP)
    pairs[member] = mine[...]
    pairs[member ^ 1] = near[...]
    pairs[member ^ 2] = far[:64]
    pairs[member ^ 3] = far[64:]


def block_edges(ref, i, m):
    tile = ref[i, m, 64 : 64 + EDGE].astype(F32)
    return tile[:8] + tile[8:]


def block_rows(ref, i, m):
    first_lane = lax.broadcasted_iota(jnp.int32, (EDGE, BLOCK), 1) % (BLOCK // 2) < KEEP
    rest = ref[i, m, 64 + EDGE :].astype(F32)
    parts = [rest] + [pltpu.roll(rest, BLOCK - g * KEEP, 1) for g in range(1, 4)]
    parts = [jnp.where(first_lane, part, 0.0) for part in parts]
    return ref[i, m, :64].astype(F32) + jnp.concatenate(parts, 0)


def own_kernel(far, table, tiles, edges):
    for i in range(8):
        for m in range(4):
            tiles[i, m] = block_rows(far, i, m)
            edges[i, m] = block_edges(far, i, m)


def attend_kernel(
    q, pairs, own_tiles, own_edges, far_other, table, gain, out, packed, scores, ends
):
    place = lax.axis_index(CTX)
    middle = place // 2
    odd = place % 2 == 1
    factor = math.log2(math.e) / math.sqrt(HEAD_CHANNELS)
    lane = lax.broadcasted_iota(jnp.int32, (BLOCK, BLOCK), 1)
    row = lax.broadcasted_iota(jnp.int32, (BLOCK, BLOCK), 0)
    edge_lane = lax.broadcasted_iota(jnp.int32, (8, BLOCK), 1) < BLOCK // 2
    edge_row = lax.broadcasted_iota(jnp.int32, (8, BLOCK), 0)
    tile_lane = lax.broadcasted_iota(jnp.int32, (64, BLOCK), 1)
    own_lane = jnp.where(tile_lane < BLOCK // 2, 1, 0) != jnp.where(odd, 1, 0)

    def turned(value):
        return pltpu.roll(value, BLOCK // 2, 1)

    def edges_of(owner, m):
        mine, other = own_edges[owner // 2, m], block_edges(far_other, owner // 2, m)
        return jnp.where(odd, other, mine) if owner % 2 == 0 else jnp.where(odd, mine, other)

    first_rows = []
    for kind in range(2):
        heads, tails = [], []
        for owner in range(16):
            left, right = edges_of(owner, 2 * kind), edges_of(owner, 2 * kind + 1)
            heads.append(jnp.where(edge_lane, left, right))
            tails.append(turned(jnp.where(edge_lane, right, left)))
        for owner in range(16):
            below = tails[owner - 1] if owner else jnp.zeros((8, BLOCK), F32)
            above = tails[owner + 1] if owner < 15 else pltpu.roll(tails[15], 3, 0)
            ends[kind, owner] = heads[owner] + jnp.where(edge_row < 3, below, above)
        both = jnp.transpose(ends[kind].reshape(128, HEAD_CHANNELS)).astype(BF16)
        fix = jnp.dot(both, table[...], preferred_element_type=F32)
        for i in range(8):
            for m in range(2):
                rows = slice(64 * m, 64 * (m + 1))
                mine = own_tiles[i, 2 * kind + m]
                other = block_rows(far_other, i, 2 * kind + m)
                low = jnp.where(own_lane, mine, other) + fix[rows, i * BLOCK : (i + 1) * BLOCK]
                high = jnp.where(own_lane, other, mine)
                high = high + fix[rows, (8 + i) * BLOCK : (9 + i) * BLOCK]
                packed[kind, 0, i, rows] = low.astype(BF16)
                packed[kind, 1, i, rows] = high.astype(BF16)
        pick = (
            (edge_row < 3)
            & (lax.broadcasted_iota(jnp.int32, (8, BLOCK), 1) == edge_row)
        ) | (
            (edge_row >= 3)
            & (edge_row < 6)
            & (lax.broadcasted_iota(jnp.int32, (8, BLOCK), 1) == edge_row - 3 + BLOCK // 2)
        )
        first_rows.append(
            lax.dot_general(
                ends[kind, place].astype(BF16),
                jnp.where(pick, 1.0, 0.0).astype(BF16),
                TN,
                preferred_element_type=F32,
            )
        )

    def near_tile(kind, start):
        tile = jnp.concatenate(
            [pairs[2 * kind, :, start : start + BLOCK], pairs[2 * kind + 1, :, start : start + BLOCK]], 0
        )
        if start % SPAN == 0:
            first = first_rows[kind] if start == 0 else turned(first_rows[kind])
            tile = jnp.where(lane < TAPS - 1, first, tile.astype(F32)).astype(BF16)
        return tile

    key_block = (lax.broadcasted_iota(jnp.int32, (1, BLOCK), 1) % (BLOCK // 2)) // KEEP
    left_lanes = lax.broadcasted_iota(jnp.int32, (1, BLOCK), 1) < BLOCK // 2
    per_chunk = CHUNK // BLOCK
    for r in range(SPAN // CHUNK):
        tops = [jnp.full((CHUNK, BLOCK), NEGATIVE, F32) for _ in range(2)]
        for half in range(2):
            tiles = []
            for c in range(per_chunk):
                start = half * SPAN + r * CHUNK + c * BLOCK
                near = jnp.dot(
                    q[start : start + BLOCK], near_tile(0, start), preferred_element_type=F32
                )
                tiles.append(jnp.where(row >= lane, near, NEGATIVE))
            tops[half] = jnp.concatenate(tiles, 0)
            scores[17 + half] = tops[half]
        upper = q[SPAN + r * CHUNK : SPAN + (r + 1) * CHUNK]
        for i in range(4):
            far = jnp.dot(
                upper,
                jnp.concatenate([packed[0, 0, 2 * i], packed[0, 0, 2 * i + 1]], 1),
                preferred_element_type=F32,
            )
            scores[9 + 2 * i] = far[:, :BLOCK]
            scores[10 + 2 * i] = far[:, BLOCK:]
            tops[1] = jnp.maximum(tops[1], jnp.maximum(far[:, :BLOCK], far[:, BLOCK:]))
        for j in range(9):
            high = j > middle
            side = high.astype(jnp.int32)
            partial = (j == middle) | (j == middle + 1)
            start = pl.multiple_of(side * SPAN + r * CHUNK, CHUNK)
            far = jnp.dot(
                q[pl.ds(start, CHUNK)], packed[0, side, j - side], preferred_element_type=F32
            )
            biases = []
            for c in range(per_chunk):
                block = r * per_chunk + c
                left = jnp.where(high, jnp.where(odd, block, 4), jnp.where(odd, 4, block))
                right = jnp.where(high, jnp.where(odd, 0, block), jnp.where(odd, block, 0))
                left, right = jnp.where(partial, left, 4), jnp.where(partial, right, 4)
                seen = key_block < jnp.where(left_lanes, left, right)
                biases.append(
                    jnp.broadcast_to(jnp.where(seen, 0.0, NEGATIVE), (BLOCK, BLOCK))
                )
            far = far + jnp.concatenate(biases, 0)
            scores[j] = far
            tops[0] = jnp.maximum(tops[0], jnp.where(high, NEGATIVE, far))
            tops[1] = jnp.maximum(tops[1], jnp.where(high, far, NEGATIVE))
        tops = [
            jnp.broadcast_to(jnp.max(t, 1, keepdims=True) * factor, (CHUNK, BLOCK)) for t in tops
        ]
        totals, sums = [], []
        for half in range(2):
            weights = jnp.exp2(scores[17 + half] * factor - tops[half])
            totals.append(weights)
            weights = weights.astype(BF16)
            sums.append(
                jnp.concatenate(
                    [
                        lax.dot_general(
                            weights[c * BLOCK : (c + 1) * BLOCK],
                            near_tile(1, half * SPAN + r * CHUNK + c * BLOCK),
                            NT,
                            preferred_element_type=F32,
                        )
                        for c in range(per_chunk)
                    ],
                    0,
                )
            )
        for i in range(4):
            first = jnp.exp2(scores[9 + 2 * i] * factor - tops[1])
            second = jnp.exp2(scores[10 + 2 * i] * factor - tops[1])
            totals[1] = totals[1] + first + second
            sums[1] = sums[1] + lax.dot_general(
                jnp.concatenate([first, second], 1).astype(BF16),
                jnp.concatenate([packed[1, 0, 2 * i], packed[1, 0, 2 * i + 1]], 1),
                NT,
                preferred_element_type=F32,
            )
        for j in range(9):
            high = j > middle
            side = high.astype(jnp.int32)
            weights = jnp.exp2(scores[j] * factor - jnp.where(high, tops[1], tops[0]))
            totals[0] = totals[0] + jnp.where(high, 0.0, weights)
            totals[1] = totals[1] + jnp.where(high, weights, 0.0)
            part = lax.dot_general(
                weights.astype(BF16), packed[1, side, j - side], NT, preferred_element_type=F32
            )
            sums[0] = sums[0] + jnp.where(high, 0.0, part)
            sums[1] = sums[1] + jnp.where(high, part, 0.0)
        for half in range(2):
            attended = sums[half] / jnp.sum(totals[half], 1, keepdims=True)
            mean = jnp.mean(attended * attended, 1, keepdims=True)
            normed = attended * lax.rsqrt(mean + EPSILON)
            start = half * SPAN + r * CHUNK
            out[start : start + CHUNK] = (normed * gain[...]).astype(BF16)


def cost(flops, moved):
    return pl.CostEstimate(flops=flops, bytes_accessed=moved, transcendentals=0)


def swapped(value, axis):
    return lax.ppermute(value, axis, [(0, 1), (1, 0)])


def per_device(queries, keys_values, query_taps, pair_taps, out_gain):
    def call(kernel, name, out_shape, operands, spaces=None, scratch=(), flops=1 << 24):
        many = isinstance(out_shape, tuple)
        return pl.pallas_call(
            kernel,
            out_shape=out_shape,
            in_specs=[spec(s) for s in spaces] if spaces else [spec()] * len(operands),
            out_specs=(spec(),) * len(out_shape) if many else spec(),
            scratch_shapes=scratch,
            compiler_params=pltpu.CompilerParams(vmem_limit_bytes=24 << 20),
            cost_estimate=cost(flops, 1 << 20),
            name=name,
        )(*operands)

    def shape(*dims):
        return jax.ShapeDtypeStruct(dims, BF16)

    conv, blocks = pl.pallas_call(
        conv_kernel,
        out_shape=(shape(64, ROWS), shape(32, SENT, BLOCK)),
        in_specs=[spec(pl.ANY)] * 3,
        out_specs=(spec(pl.ANY), spec(pl.ANY)),
        scratch_shapes=[
            VMEM((64, ROWS), BF16),
            VMEM((TAPS, 64), F32),
            VMEM((BLOCK, BLOCK), BF16),
            VMEM((64, ROWS), BF16),
            VMEM((32, SENT, BLOCK), BF16),
            pltpu.SemaphoreType.DMA((5,)),
        ],
        compiler_params=pltpu.CompilerParams(vmem_limit_bytes=56 << 20),
        cost_estimate=cost(1 << 24, 1 << 20),
        name="conv",
    )(keys_values.T, pair_taps, jnp.asarray(dct_tile()))
    gathered = lax.all_to_all(blocks, CHIPS + GROUP, 0, 0, tiled=True)
    near = swapped(conv, "y_hi")
    tails = call(
        tails_kernel,
        "tails",
        shape(2, EDGE, BLOCK),
        (queries, near, conv),
        (VMEM, pl.ANY, VMEM),
        flops=1 << 37,
    )
    swap = swapped(tails, "core")
    hop = lax.ppermute(
        tails, CTX, [(i, i + 1) for i in range(1, 15, 2)] + [(i + 1, i) for i in range(1, 15, 2)]
    )
    query_conv, gain = call(
        query_kernel,
        "queries",
        (shape(ROWS, HEAD_CHANNELS), jax.ShapeDtypeStruct((1, HEAD_CHANNELS), F32)),
        (queries, tails, swap, hop, query_taps, out_gain.reshape(1, -1)),
    )
    joined = call(
        join_kernel, "join", shape(128, ROWS), (conv, near, query_conv), (VMEM, VMEM, pl.ANY)
    )
    far = swapped(joined, "z_lo")
    gathered, query_conv = lax.optimization_barrier((gathered, query_conv))
    far_own = gathered.reshape(8, 4, SENT, BLOCK)
    far_other = swapped(far_own, "core")
    table = jnp.asarray(head_tables())
    tiles, edges = call(
        own_kernel,
        "own",
        (
            jax.ShapeDtypeStruct((8, 4, 64, BLOCK), F32),
            jax.ShapeDtypeStruct((8, 4, 8, BLOCK), F32),
        ),
        (far_own, table),
    )
    pairs = call(
        pairs_kernel,
        "pairs",
        shape(4, 64, ROWS),
        (conv, near, far, edges),
        (VMEM, VMEM, VMEM, pl.ANY),
        flops=1 << 37,
    )
    return call(
        attend_kernel,
        "attend",
        shape(ROWS, HEAD_CHANNELS),
        (query_conv, pairs, tiles, edges, far_other, table, gain),
        scratch=[
            VMEM((2, 2, 8, HEAD_CHANNELS, BLOCK), BF16),
            VMEM((19, CHUNK, BLOCK), F32),
            VMEM((2, 16, 8, HEAD_CHANNELS), F32),
        ],
        flops=1 << 30,
    )


def solution(mesh):
    fine = Mesh(mesh.devices.reshape(2, 4, 2, 8, 2, 2), CTX + MP)
    in_specs = (P(CTX, MP), P(CTX, MP), P(None, MP), P(None, MP), P(MP))
    return jax.shard_map(
        per_device, mesh=fine, in_specs=in_specs, out_specs=P(CTX, MP), check_vma=False
    )
```

```python
import functools
import math

import jax
import jax.numpy as jnp
import numpy as np
from jax import lax
from jax.experimental import pallas as pl
from jax.experimental.pallas import tpu as pltpu
from jax.sharding import Mesh, PartitionSpec as P

HEAD_CHANNELS = 128
TAPS = 4
BLOCK = 128
KEEP = 16
SPAN = 512
ROWS = 2 * SPAN
NEGATIVE = -1e30
EPSILON = 1e-06
EDGE = 16
SENT = 64 + 2 * EDGE
CHUNK = 256

CTX = ("y_lo", "x", "core")
MP = ("z_hi", "z_lo", "y_hi")
GROUP = ("z_lo", "y_hi")
CHIPS = ("y_lo", "x")

VMEM = pltpu.VMEM
SMEM = pltpu.SMEM
F32 = jnp.float32
BF16 = jnp.bfloat16
NT = (((1,), (1,)), ((), ()))
TN = (((0,), (0,)), ((), ()))


def spec(space=VMEM):
    return pl.BlockSpec(memory_space=space)


def dct_table():
    j = np.arange(KEEP, dtype=np.float32)[:, None]
    u = np.arange(BLOCK, dtype=np.float32)[None, :]
    table = np.cos(np.float32(math.pi) * (u + np.float32(0.5)) * j / np.float32(BLOCK))
    table = table * np.float32(math.sqrt(2.0 / BLOCK))
    table = np.where(j == 0, table * np.float32(math.sqrt(0.5)), table)
    return table.astype(jnp.bfloat16)


def dct_tile():
    return np.tile(dct_table().T, (1, BLOCK // KEEP))


def head_tables():
    table = dct_table()
    whole = np.zeros((16, 8, 2, 8, BLOCK), table.dtype)
    half = BLOCK // 2
    for owner in range(16):
        for t in range(TAPS - 1):
            low, high = (0, half) if owner % 2 == 0 else (half, 0)
            whole[owner, t, 0, owner // 2, low : low + KEEP] = table[:, t]
            whole[owner, 3 + t, 1, owner // 2, high : high + KEEP] = table[:, t]
    return whole.reshape(128, 16 * BLOCK)


def conv_kernel(
    kv_in, taps_in, table_in, conv_result, block_result, kv, taps, table, conv_out, block_out, sems
):
    moves = [(kv_in, kv), (taps_in, taps), (table_in, table)]
    moves += [(conv_out, conv_result), (block_out, block_result)]
    moves = [pltpu.make_async_copy(*move, sems.at[k]) for k, move in enumerate(moves)]
    for move in moves[:3]:
        move.start()
    for move in moves[:3]:
        move.wait()
    lanes = lax.broadcasted_iota(jnp.int32, (64, BLOCK), 1)
    turned = jnp.transpose(
        jnp.concatenate(
            [
                jnp.concatenate([taps[...], jnp.zeros((4, 64), F32)], 0),
                jnp.zeros((8, 64), F32),
            ],
            1,
        )
    )[:64]
    heads, tails = [], []
    for half in range(2):
        values = kv[:, half * SPAN : (half + 1) * SPAN].astype(F32)
        padded = jnp.concatenate([values, jnp.zeros((64, BLOCK), F32)], 1)
        total = turned[:, 0:1] * padded
        for w in range(1, TAPS):
            total = total + turned[:, w : w + 1] * pltpu.roll(padded, w, 1)
        conv_out[:, half * SPAN : (half + 1) * SPAN] = total[:, :SPAN].astype(BF16)
        if half:
            moves[3].start()
        heads.append(total[:, :BLOCK])
        tails.append(total[:, SPAN:])

    def join(pair):
        upper = pltpu.roll(pair[1], 3, 1)
        return jnp.where(lanes < 3, pair[0], jnp.where(lanes < 6, upper, 0.0))

    heads, tails = join(heads), join(tails)
    uneven = lax.axis_index("y_hi") == 1
    edges = jnp.concatenate([jnp.where(uneven, tails, heads), jnp.where(uneven, heads, tails)], 0)
    edges = jnp.transpose(edges)[:8]
    high = edges.astype(BF16)
    low = edges - high.astype(F32)
    edges = jnp.concatenate([high.astype(F32), low], 0).astype(BF16)
    packed = jnp.zeros((64, BLOCK), F32)
    for b in range(ROWS // BLOCK):
        part = conv_out[:, b * BLOCK : (b + 1) * BLOCK]
        if b * BLOCK % SPAN == 0:
            part = jnp.where(lanes < TAPS - 1, 0.0, part.astype(F32)).astype(BF16)
        part = jnp.dot(part, table[...], preferred_element_type=F32)
        packed = jnp.where(lanes // KEEP == b, part, packed)
    packed = jnp.where(lax.axis_index("core") == 1, pltpu.roll(packed, BLOCK // 2, 1), packed)
    high = packed.astype(BF16)
    low = jnp.where(lanes % (BLOCK // 2) < KEEP, packed - high.astype(F32), 0.0)
    rest = low[:EDGE]
    for g in range(1, 4):
        rest = rest + pltpu.roll(low[g * EDGE : (g + 1) * EDGE], g * KEEP, 1)
    rest = rest.astype(BF16)
    for k in range(block_out.shape[0]):
        block_out[k, :64] = high
        block_out[k, 64 : 64 + EDGE] = edges
        block_out[k, 64 + EDGE :] = rest
    moves[4].start()
    moves[3].wait()
    moves[4].wait()


def tails_kernel(q, near, conv, out):
    for half in range(2):
        out[half] = q[(half + 1) * SPAN - EDGE : (half + 1) * SPAN]


def join_kernel(mine, near, hop, out):
    out[:64] = mine[...]
    out[64:] = near[...]


def query_kernel(q, own, swap, hop, taps, gain, out, gain_out):
    gain_out[...] = gain[...]
    place = lax.axis_index(CTX)
    odd = place % 2 == 1
    own, swap, hop = own[...].astype(F32), swap[...].astype(F32), hop[...].astype(F32)
    lower = jnp.where(odd, swap[0], hop[0])
    lower = jnp.where(place == 0, jnp.zeros_like(lower), lower)
    upper = jnp.where(odd, hop[1], swap[1])
    upper = jnp.where(place == 15, own[0], upper)
    for half, halo in enumerate((lower, upper)):
        for b in range(SPAN // BLOCK):
            start = half * SPAN + b * BLOCK
            values = q[start : start + BLOCK].astype(F32)
            if b:
                halo = q[start - EDGE : start].astype(F32)
            padded = jnp.concatenate([halo, values], 0)
            total = taps[0:1] * values
            for w in range(1, TAPS):
                total = total + taps[w : w + 1] * pltpu.roll(padded, w, 0)[EDGE:]
            out[start : start + BLOCK] = total.astype(BF16)


def pairs_kernel(mine, near, far, edges, pairs):
    member = lax.axis_index(GROUP)
    pairs[member] = mine[...]
    pairs[member ^ 1] = near[...]
    pairs[member ^ 2] = far[:64]
    pairs[member ^ 3] = far[64:]


def block_edges(ref, i, m):
    tile = ref[i, m, 64 : 64 + EDGE].astype(F32)
    return tile[:8] + tile[8:]


def block_rows(ref, i, m):
    first_lane = lax.broadcasted_iota(jnp.int32, (EDGE, BLOCK), 1) % (BLOCK // 2) < KEEP
    rest = ref[i, m, 64 + EDGE :].astype(F32)
    parts = [rest] + [pltpu.roll(rest, BLOCK - g * KEEP, 1) for g in range(1, 4)]
    parts = [jnp.where(first_lane, part, 0.0) for part in parts]
    return ref[i, m, :64].astype(F32) + jnp.concatenate(parts, 0)


def own_kernel(far, table, tiles, edges):
    for i in range(8):
        for m in range(4):
            tiles[i, m] = block_rows(far, i, m)
            edges[i, m] = block_edges(far, i, m)


def attend_kernel(
    q, pairs, own_tiles, own_edges, far_other, table, gain, out, packed, scores, ends
):
    place = lax.axis_index(CTX)
    middle = place // 2
    odd = place % 2 == 1
    factor = math.log2(math.e) / math.sqrt(HEAD_CHANNELS)
    lane = lax.broadcasted_iota(jnp.int32, (BLOCK, BLOCK), 1)
    row = lax.broadcasted_iota(jnp.int32, (BLOCK, BLOCK), 0)
    edge_lane = lax.broadcasted_iota(jnp.int32, (8, BLOCK), 1) < BLOCK // 2
    edge_row = lax.broadcasted_iota(jnp.int32, (8, BLOCK), 0)
    tile_lane = lax.broadcasted_iota(jnp.int32, (64, BLOCK), 1)
    own_lane = jnp.where(tile_lane < BLOCK // 2, 1, 0) != jnp.where(odd, 1, 0)

    def turned(value):
        return pltpu.roll(value, BLOCK // 2, 1)

    def edges_of(owner, m):
        mine, other = own_edges[owner // 2, m], block_edges(far_other, owner // 2, m)
        return jnp.where(odd, other, mine) if owner % 2 == 0 else jnp.where(odd, mine, other)

    first_rows = []
    for kind in range(2):
        heads, tails = [], []
        for owner in range(16):
            left, right = edges_of(owner, 2 * kind), edges_of(owner, 2 * kind + 1)
            heads.append(jnp.where(edge_lane, left, right))
            tails.append(turned(jnp.where(edge_lane, right, left)))
        for owner in range(16):
            below = tails[owner - 1] if owner else jnp.zeros((8, BLOCK), F32)
            above = tails[owner + 1] if owner < 15 else pltpu.roll(tails[15], 3, 0)
            ends[kind, owner] = heads[owner] + jnp.where(edge_row < 3, below, above)
        both = jnp.transpose(ends[kind].reshape(128, HEAD_CHANNELS)).astype(BF16)
        fix = jnp.dot(both, table[...], preferred_element_type=F32)
        for i in range(8):
            for m in range(2):
                rows = slice(64 * m, 64 * (m + 1))
                mine = own_tiles[i, 2 * kind + m]
                other = block_rows(far_other, i, 2 * kind + m)
                low = jnp.where(own_lane, mine, other) + fix[rows, i * BLOCK : (i + 1) * BLOCK]
                high = jnp.where(own_lane, other, mine)
                high = high + fix[rows, (8 + i) * BLOCK : (9 + i) * BLOCK]
                packed[kind, 0, i, rows] = low.astype(BF16)
                packed[kind, 1, i, rows] = high.astype(BF16)
        pick = (
            (edge_row < 3)
            & (lax.broadcasted_iota(jnp.int32, (8, BLOCK), 1) == edge_row)
        ) | (
            (edge_row >= 3)
            & (edge_row < 6)
            & (lax.broadcasted_iota(jnp.int32, (8, BLOCK), 1) == edge_row - 3 + BLOCK // 2)
        )
        first_rows.append(
            lax.dot_general(
                ends[kind, place].astype(BF16),
                jnp.where(pick, 1.0, 0.0).astype(BF16),
                TN,
                preferred_element_type=F32,
            )
        )

    def near_tile(kind, start):
        tile = jnp.concatenate(
            [pairs[2 * kind, :, start : start + BLOCK], pairs[2 * kind + 1, :, start : start + BLOCK]], 0
        )
        if start % SPAN == 0:
            first = first_rows[kind] if start == 0 else turned(first_rows[kind])
            tile = jnp.where(lane < TAPS - 1, first, tile.astype(F32)).astype(BF16)
        return tile

    key_block = (lax.broadcasted_iota(jnp.int32, (1, BLOCK), 1) % (BLOCK // 2)) // KEEP
    left_lanes = lax.broadcasted_iota(jnp.int32, (1, BLOCK), 1) < BLOCK // 2
    per_chunk = CHUNK // BLOCK
    for r in range(SPAN // CHUNK):
        tops = [jnp.full((CHUNK, BLOCK), NEGATIVE, F32) for _ in range(2)]
        for half in range(2):
            tiles = []
            for c in range(per_chunk):
                start = half * SPAN + r * CHUNK + c * BLOCK
                near = jnp.dot(
                    q[start : start + BLOCK], near_tile(0, start), preferred_element_type=F32
                )
                tiles.append(jnp.where(row >= lane, near, NEGATIVE))
            tops[half] = jnp.concatenate(tiles, 0)
            scores[17 + half] = tops[half]
        upper = q[SPAN + r * CHUNK : SPAN + (r + 1) * CHUNK]
        for i in range(4):
            far = jnp.dot(
                upper,
                jnp.concatenate([packed[0, 0, 2 * i], packed[0, 0, 2 * i + 1]], 1),
                preferred_element_type=F32,
            )
            scores[9 + 2 * i] = far[:, :BLOCK]
            scores[10 + 2 * i] = far[:, BLOCK:]
            tops[1] = jnp.maximum(tops[1], jnp.maximum(far[:, :BLOCK], far[:, BLOCK:]))
        for j in range(9):
            high = j > middle
            side = high.astype(jnp.int32)
            partial = (j == middle) | (j == middle + 1)
            start = pl.multiple_of(side * SPAN + r * CHUNK, CHUNK)
            far = jnp.dot(
                q[pl.ds(start, CHUNK)], packed[0, side, j - side], preferred_element_type=F32
            )
            biases = []
            for c in range(per_chunk):
                block = r * per_chunk + c
                left = jnp.where(high, jnp.where(odd, block, 4), jnp.where(odd, 4, block))
                right = jnp.where(high, jnp.where(odd, 0, block), jnp.where(odd, block, 0))
                left, right = jnp.where(partial, left, 4), jnp.where(partial, right, 4)
                seen = key_block < jnp.where(left_lanes, left, right)
                biases.append(
                    jnp.broadcast_to(jnp.where(seen, 0.0, NEGATIVE), (BLOCK, BLOCK))
                )
            far = far + jnp.concatenate(biases, 0)
            scores[j] = far
            tops[0] = jnp.maximum(tops[0], jnp.where(high, NEGATIVE, far))
            tops[1] = jnp.maximum(tops[1], jnp.where(high, far, NEGATIVE))
        tops = [
            jnp.broadcast_to(jnp.max(t, 1, keepdims=True) * factor, (CHUNK, BLOCK)) for t in tops
        ]
        totals, sums = [], []
        for half in range(2):
            weights = jnp.exp2(scores[17 + half] * factor - tops[half])
            totals.append(weights)
            weights = weights.astype(BF16)
            sums.append(
                jnp.concatenate(
                    [
                        lax.dot_general(
                            weights[c * BLOCK : (c + 1) * BLOCK],
                            near_tile(1, half * SPAN + r * CHUNK + c * BLOCK),
                            NT,
                            preferred_element_type=F32,
                        )
                        for c in range(per_chunk)
                    ],
                    0,
                )
            )
        for i in range(4):
            first = jnp.exp2(scores[9 + 2 * i] * factor - tops[1])
            second = jnp.exp2(scores[10 + 2 * i] * factor - tops[1])
            totals[1] = totals[1] + first + second
            sums[1] = sums[1] + lax.dot_general(
                jnp.concatenate([first, second], 1).astype(BF16),
                jnp.concatenate([packed[1, 0, 2 * i], packed[1, 0, 2 * i + 1]], 1),
                NT,
                preferred_element_type=F32,
            )
        for j in range(9):
            high = j > middle
            side = high.astype(jnp.int32)
            weights = jnp.exp2(scores[j] * factor - jnp.where(high, tops[1], tops[0]))
            totals[0] = totals[0] + jnp.where(high, 0.0, weights)
            totals[1] = totals[1] + jnp.where(high, weights, 0.0)
            part = lax.dot_general(
                weights.astype(BF16), packed[1, side, j - side], NT, preferred_element_type=F32
            )
            sums[0] = sums[0] + jnp.where(high, 0.0, part)
            sums[1] = sums[1] + jnp.where(high, part, 0.0)
        for half in range(2):
            attended = sums[half] / jnp.sum(totals[half], 1, keepdims=True)
            mean = jnp.mean(attended * attended, 1, keepdims=True)
            normed = attended * lax.rsqrt(mean + EPSILON)
            start = half * SPAN + r * CHUNK
            out[start : start + CHUNK] = (normed * gain[...]).astype(BF16)


def cost(flops, moved):
    return pl.CostEstimate(flops=flops, bytes_accessed=moved, transcendentals=0)


def swapped(value, axis):
    return lax.ppermute(value, axis, [(0, 1), (1, 0)])


def per_device(queries, keys_values, query_taps, pair_taps, out_gain):
    def call(kernel, name, out_shape, operands, spaces=None, scratch=(), flops=1 << 24):
        many = isinstance(out_shape, tuple)
        return pl.pallas_call(
            kernel,
            out_shape=out_shape,
            in_specs=[spec(s) for s in spaces] if spaces else [spec()] * len(operands),
            out_specs=(spec(),) * len(out_shape) if many else spec(),
            scratch_shapes=scratch,
            compiler_params=pltpu.CompilerParams(vmem_limit_bytes=24 << 20),
            cost_estimate=cost(flops, 1 << 20),
            name=name,
        )(*operands)

    def shape(*dims):
        return jax.ShapeDtypeStruct(dims, BF16)

    conv, blocks = pl.pallas_call(
        conv_kernel,
        out_shape=(shape(64, ROWS), shape(32, SENT, BLOCK)),
        in_specs=[spec(pl.ANY)] * 3,
        out_specs=(spec(pl.ANY), spec(pl.ANY)),
        scratch_shapes=[
            VMEM((64, ROWS), BF16),
            VMEM((TAPS, 64), F32),
            VMEM((BLOCK, BLOCK), BF16),
            VMEM((64, ROWS), BF16),
            VMEM((32, SENT, BLOCK), BF16),
            pltpu.SemaphoreType.DMA((5,)),
        ],
        compiler_params=pltpu.CompilerParams(vmem_limit_bytes=56 << 20),
        cost_estimate=cost(1 << 24, 1 << 20),
        name="conv",
    )(keys_values.T, pair_taps, jnp.asarray(dct_tile()))
    gathered = lax.all_to_all(blocks, CHIPS + GROUP, 0, 0, tiled=True)
    near = swapped(conv, "y_hi")
    tails = call(
        tails_kernel,
        "tails",
        shape(2, EDGE, BLOCK),
        (queries, near, conv),
        (VMEM, pl.ANY, VMEM),
        flops=1 << 37,
    )
    swap = swapped(tails, "core")
    hop = lax.ppermute(
        tails, CTX, [(i, i + 1) for i in range(1, 15, 2)] + [(i + 1, i) for i in range(1, 15, 2)]
    )
    query_conv, gain = call(
        query_kernel,
        "queries",
        (shape(ROWS, HEAD_CHANNELS), jax.ShapeDtypeStruct((1, HEAD_CHANNELS), F32)),
        (queries, tails, swap, hop, query_taps, out_gain.reshape(1, -1)),
    )
    joined = call(
        join_kernel, "join", shape(128, ROWS), (conv, near, hop), (VMEM, VMEM, pl.ANY)
    )
    far = swapped(joined, "z_lo")
    gathered, query_conv = lax.optimization_barrier((gathered, query_conv))
    far_own = gathered.reshape(8, 4, SENT, BLOCK)
    far_other = swapped(far_own, "core")
    table = jnp.asarray(head_tables())
    tiles, edges = call(
        own_kernel,
        "own",
        (
            jax.ShapeDtypeStruct((8, 4, 64, BLOCK), F32),
            jax.ShapeDtypeStruct((8, 4, 8, BLOCK), F32),
        ),
        (far_own, table),
    )
    pairs = call(
        pairs_kernel,
        "pairs",
        shape(4, 64, ROWS),
        (conv, near, far, edges),
        (VMEM, VMEM, VMEM, pl.ANY),
        flops=1 << 37,
    )
    return call(
        attend_kernel,
        "attend",
        shape(ROWS, HEAD_CHANNELS),
        (query_conv, pairs, tiles, edges, far_other, table, gain),
        scratch=[
            VMEM((2, 2, 8, HEAD_CHANNELS, BLOCK), BF16),
            VMEM((19, CHUNK, BLOCK), F32),
            VMEM((2, 16, 8, HEAD_CHANNELS), F32),
        ],
        flops=1 << 30,
    )


def solution(mesh):
    fine = Mesh(mesh.devices.reshape(2, 4, 2, 8, 2, 2), CTX + MP)
    in_specs = (P(CTX, MP), P(CTX, MP), P(None, MP), P(None, MP), P(MP))
    return jax.shard_map(
        per_device, mesh=fine, in_specs=in_specs, out_specs=P(CTX, MP), check_vma=False
    )
```
